32 devices in a mesh: rep: 8 (over y, x, core), fsdp: 4 (over z).
Axes of the slice: x: 2, y: 2, z: 4, core: 2. Of those that a mesh axis runs over, the one named last changes fastest.
Arguments:
- inputs: bfloat16 [4096, 2048], P(('rep', 'fsdp')), may hold values from -6 to 6
- doc_lengths: int32 [8, 8], P('rep'), may hold values from 1 to 385, as said below
- attn_gain: bfloat16 [2048], P('fsdp'), may hold values from 0.25 to 1.75
- query_weight: bfloat16 [2048, 2048], P('fsdp'), may hold values from -0.125 to 0.125
- key_projection: bfloat16 [2048, 512], P('fsdp'), may hold values from -0.125 to 0.125
- value_projection: bfloat16 [2048, 512], P('fsdp'), may hold values from -0.125 to 0.125
- query_gain: bfloat16 [64], P('fsdp'), may hold values from 0.099609375 to 1.8984375
- key_norm_gain: bfloat16 [64], P('fsdp'), may hold values from 0.099609375 to 1.8984375
- out_weight: bfloat16 [2048, 2048], P('fsdp'), may hold values from -0.5 to 0.5
- ffn_gain: bfloat16 [2048], P('fsdp'), may hold values from 0.25 to 1.75
- gate_weight: bfloat16 [2048, 8192], P('fsdp'), may hold values from -0.125 to 0.125
- up_weight: bfloat16 [2048, 8192], P('fsdp'), may hold values from -0.125 to 0.125
- down_weight: bfloat16 [8192, 2048], P('fsdp'), may hold values from -0.0625 to 0.0625
- cotangent: bfloat16 [4096, 2048], P(('rep', 'fsdp')), may hold values from -6 to 6
Outputs:
- output: bfloat16 [4096, 2048], P(('rep', 'fsdp'))
- input_grad: bfloat16 [4096, 2048], P(('rep', 'fsdp'))
- attn_gain_grad: float32 [2048], P('fsdp')
- query_weight_grad: float32 [2048, 2048], P('fsdp')
- key_weight_grad: float32 [2048, 512], P('fsdp')
- value_weight_grad: float32 [2048, 512], P('fsdp')
- query_gain_grad: float32 [64], P('fsdp')
- key_gain_grad: float32 [64], P('fsdp')
- out_weight_grad: float32 [2048, 2048], P('fsdp')
- ffn_gain_grad: float32 [2048], P('fsdp')
- gate_weight_grad: float32 [2048, 8192], P('fsdp')
- up_weight_grad: float32 [2048, 8192], P('fsdp')
- down_weight_grad: float32 [8192, 2048], P('fsdp')
The draws below stay inside these ranges and needn't reach their ends.
Inputs may be any that keep to these rules, and one draw needn't show every extreme that they name: `doc_lengths`: each row lists the lengths of 8 documents packed in order into the 512 tokens of one sequence and sums to 512; in each row one document, at a place drawn from the seed, has exactly 385 tokens, starts before position 128 and ends at or after position 384.
All inputs are finite; a program needn't handle non-finite values.
Results may differ from the reference program's by a relative error of at most 0.019.
Values may be sent and summed in bfloat16 or wider, within the bound.
No kernel may reach another device: no remote copies, remote signals or barrier semaphores. Data moves between devices by JAX's collectives and lax.ppermute only.
A program may use at most 448 MiB of HBM per device.

```python
import jax
import jax.numpy as jnp
from jax import lax

MODEL_DIMENSION = 2048
QUERY_HEAD_COUNT = 32
KEY_VALUE_HEADS = 8
HEAD_SIZE = 64
FF = 8192
TOK_DEV = 128
NDOCS = 8
SEQ = 512
SEQS = 8
TOKENS = 4096


def draw_doc_lengths(key, part):

    def one_row(row_key):
        weight_key = jax.random.fold_in(row_key, 1)
        place_key = jax.random.fold_in(row_key, 2)
        small_total = TOK_DEV - 1
        spread = 2 ** jax.random.randint(weight_key, (NDOCS - 1,), 0, 5)
        extra_total = small_total - (NDOCS - 1)
        extras = extra_total * spread // jnp.sum(spread)
        extras = extras.at[0].add(extra_total - jnp.sum(extras))
        smalls = 1 + extras
        big_place = jax.random.randint(place_key, (), 0, NDOCS)
        slot_ids = jnp.arange(NDOCS)
        shifted_up = jnp.concatenate([smalls, smalls[-1:]])
        shifted_down = jnp.concatenate([smalls[:1], smalls])
        return jnp.where(slot_ids < big_place, shifted_up, jnp.where(slot_ids > big_place, shifted_down, SEQ - small_total)).astype(jnp.int32)
    return jax.vmap(one_row)(jax.random.split(key, SEQS))


def levels(rng, extent, cuts, least, top_value):
    gain, own = 1.0, jax.random.fold_in(rng, 6)
    for position, parts in cuts:
        steps = jnp.exp(jax.random.uniform(jax.random.fold_in(own, position), (parts,), jnp.float32, least / len(cuts), top_value / len(cuts)))
        gain = gain * jnp.repeat(steps, extent[position] // parts).reshape([-1 if axis == position else 1 for axis in range(len(extent))])
    return gain


def noise(stream_key, dims, scale, reach, cuts=(), kind=jnp.bfloat16):
    drawn = jax.random.normal(stream_key, dims, jnp.float32) * scale
    if len(cuts) > 0:
        drawn = levels(stream_key, dims, cuts, -0.22, 0.18) * drawn
    return jnp.clip(drawn, min=-reach, max=reach).astype(kind)


def setup_inputs(seed: int = 0) -> dict:
    keys = jax.random.split(jax.random.key(seed), 15)
    inputs = noise(keys[0], (TOKENS, MODEL_DIMENSION), 1.0, 6.0, ((0, 32),))
    doc_lengths = draw_doc_lengths(jax.random.fold_in(keys[14], 71), 0)
    attn_gain = jnp.clip(1.0 + 0.15 * jax.random.normal(keys[2], (MODEL_DIMENSION,), jnp.float32), 0.25, 1.75).astype(jnp.bfloat16)
    query_weight = noise(keys[3], (MODEL_DIMENSION, QUERY_HEAD_COUNT * HEAD_SIZE), MODEL_DIMENSION ** -0.5, 0.125, ((0, 4),))
    key_projection = noise(keys[4], (MODEL_DIMENSION, KEY_VALUE_HEADS * HEAD_SIZE), MODEL_DIMENSION ** -0.5, 0.125, ((0, 4),))
    value_projection = noise(keys[5], (MODEL_DIMENSION, KEY_VALUE_HEADS * HEAD_SIZE), MODEL_DIMENSION ** -0.5, 0.125, ((0, 4),))
    query_gain = jnp.clip(1.0 + 0.18 * jax.random.normal(keys[6], (HEAD_SIZE,), jnp.float32), 0.099609375, 1.8984375).astype(jnp.bfloat16)
    key_norm_gain = jnp.clip(1.0 + 0.18 * jax.random.normal(keys[7], (HEAD_SIZE,), jnp.float32), 0.099609375, 1.8984375).astype(jnp.bfloat16)
    out_weight = noise(keys[8], (QUERY_HEAD_COUNT * HEAD_SIZE, MODEL_DIMENSION), (QUERY_HEAD_COUNT * HEAD_SIZE // 16) ** -0.5, 0.5, ((0, 4),))
    ffn_gain = jnp.clip(1.0 + 0.15 * jax.random.normal(keys[9], (MODEL_DIMENSION,), jnp.float32), 0.25, 1.75).astype(jnp.bfloat16)
    gate_weight = noise(keys[10], (MODEL_DIMENSION, FF), MODEL_DIMENSION ** -0.5, 0.125, ((0, 4),))
    up_weight = noise(keys[11], (MODEL_DIMENSION, FF), MODEL_DIMENSION ** -0.5, 0.125, ((0, 4),))
    down_weight = noise(keys[12], (FF, MODEL_DIMENSION), FF ** -0.5, 0.0625, ((0, 4),))
    cotangent = noise(keys[13], (TOKENS, MODEL_DIMENSION), 1.0, 6.0, ((0, 32),))
    return dict(inputs=inputs, doc_lengths=doc_lengths, attn_gain=attn_gain, query_weight=query_weight, key_projection=key_projection, value_projection=value_projection, query_gain=query_gain, key_norm_gain=key_norm_gain, out_weight=out_weight, ffn_gain=ffn_gain, gate_weight=gate_weight, up_weight=up_weight, down_weight=down_weight, cotangent=cotangent)


EPSILON = 1e-05
THETA_BASE = 1000000.0
NEG_FILL = -1e+30
PRECISE = lax.Precision.HIGHEST

@jax.custom_vjp
def lowered_values(v):
    return lax.optimization_barrier(v.astype(jnp.bfloat16)).astype(jnp.float32)

@jax.custom_vjp
def low_back(v):
    return v

def low_keep(v):
    return (lowered_values(v), None)

def low_pass(kept, grad):
    return (grad,)

def back_keep(v):
    return (v, None)

def back_low(kept, grad):
    return (lowered_values(grad),)
lowered_values.defvjp(low_keep, low_pass)
low_back.defvjp(back_keep, back_low)

def rotary_tables(positions):
    half_dim = HEAD_SIZE // 2
    inverse = THETA_BASE ** (-(jnp.arange(half_dim, dtype=jnp.float32) * 2.0) / HEAD_SIZE)
    angles = positions.astype(jnp.float32)[:, None] * inverse[None, :]
    return (jnp.cos(angles)[:, None, :], jnp.sin(angles)[:, None, :])

def apply_rotary(values, cosine_table, sine_values):
    half_dim = values.shape[-1] // 2
    first_part = values[..., :half_dim]
    second_part = values[..., half_dim:]
    return jnp.concatenate([first_part * cosine_table - second_part * sine_values, second_part * cosine_table + first_part * sine_values], axis=-1)

def per_head_norm(values, gain_vec):
    return values * lax.rsqrt(lax.optimization_barrier(jnp.mean(values * values, axis=-1, keepdims=True)) + EPSILON) * gain_vec

def layer_forward(inputs, params, segment, cosine_table, sine_values):
    attn_gain, query_weight, key_projection, value_projection, query_gain, key_norm_gain, out_weight, ffn_gain, gate_weight, up_weight, down_weight = params
    span_length = inputs.shape[0]
    inv_one = lax.rsqrt(lax.optimization_barrier(jnp.mean(inputs * inputs, axis=-1, keepdims=True)) + EPSILON)
    normed_one = lowered_values(inputs * inv_one * attn_gain)
    query_pre = low_back(jnp.dot(normed_one, query_weight, precision=PRECISE))
    key_before_norm = low_back(jnp.dot(normed_one, key_projection, precision=PRECISE))
    value_matrix = low_back(lowered_values(jnp.dot(normed_one, value_projection, precision=PRECISE)))
    query_rows = lowered_values(apply_rotary(per_head_norm(query_pre.reshape(span_length, QUERY_HEAD_COUNT, HEAD_SIZE), query_gain), cosine_table, sine_values))
    rotated_keys = lowered_values(apply_rotary(per_head_norm(key_before_norm.reshape(span_length, KEY_VALUE_HEADS, HEAD_SIZE), key_norm_gain), cosine_table, sine_values))
    places = jnp.arange(span_length)
    allowed = (segment[:, None] == segment[None, :]) & (places[None, :] <= places[:, None])
    grouped_heads = query_rows.reshape(span_length, KEY_VALUE_HEADS, QUERY_HEAD_COUNT // KEY_VALUE_HEADS, HEAD_SIZE).transpose(1, 0, 2, 3)

    def group_of_head(operands):
        query_block, key_block, value_block = operands
        scores = jnp.einsum('qgd,kd->gqk', query_block, key_block, precision=PRECISE) * HEAD_SIZE ** (-0.5)
        scores = jnp.where(allowed[None], low_back(scores), NEG_FILL)
        weights = lowered_values(jax.nn.softmax(scores, axis=-1))
        return jnp.einsum('gqk,kd->qgd', weights, value_block, precision=PRECISE)
    output_per_head = lax.map(jax.checkpoint(group_of_head), (grouped_heads, rotated_keys.transpose(1, 0, 2), value_matrix.reshape(span_length, KEY_VALUE_HEADS, HEAD_SIZE).transpose(1, 0, 2)))
    attended = low_back(lowered_values(output_per_head.transpose(1, 0, 2, 3).reshape(span_length, QUERY_HEAD_COUNT * HEAD_SIZE)))
    hidden_one = inputs + low_back(jnp.dot(attended, out_weight, precision=PRECISE))
    inv_two = lax.rsqrt(lax.optimization_barrier(jnp.mean(hidden_one * hidden_one, axis=-1, keepdims=True)) + EPSILON)
    normed_two = lowered_values(hidden_one * inv_two * ffn_gain)
    gate_pre = low_back(jnp.dot(normed_two, gate_weight, precision=PRECISE))
    upward = low_back(jnp.dot(normed_two, up_weight, precision=PRECISE))
    hidden = lowered_values(jax.nn.silu(gate_pre) * upward)
    return hidden_one + low_back(jnp.dot(hidden, down_weight, precision=PRECISE))

def reference(inputs, doc_lengths, attn_gain, query_weight, key_projection, value_projection, query_gain, key_norm_gain, out_weight, ffn_gain, gate_weight, up_weight, down_weight, cotangent):
    params = tuple((weight_in.astype(jnp.float32) for weight_in in (attn_gain, query_weight, key_projection, value_projection, query_gain, key_norm_gain, out_weight, ffn_gain, gate_weight, up_weight, down_weight)))
    positions = jnp.arange(SEQ)
    doc_ends = jnp.cumsum(doc_lengths, axis=1)
    segments = lax.optimization_barrier(jnp.sum((positions[None, :, None] >= doc_ends[:, None, :]).astype(jnp.int32), axis=-1))
    cosine_table, sine_values = rotary_tables(positions)
    seq_inputs = inputs.astype(jnp.float32).reshape(SEQS, SEQ, MODEL_DIMENSION)
    seq_cot = cotangent.astype(jnp.float32).reshape(SEQS, SEQ, MODEL_DIMENSION)

    def per_sequence(totals, operands):
        seq_in, seq_grad, segment = operands
        result, pullback = jax.vjp(lambda first_arg, second_arg: layer_forward(first_arg, second_arg, segment, cosine_table, sine_values), seq_in, params)
        grad_in, param_grads = pullback(seq_grad)
        totals = tuple((running + grad_term for running, grad_term in zip(totals, param_grads)))
        return (totals, (result.astype(jnp.bfloat16), grad_in.astype(jnp.bfloat16)))
    totals, (results, input_grads) = lax.scan(per_sequence, tuple((jnp.zeros_like(weight_in) for weight_in in params)), (seq_inputs, seq_cot, segments))
    return (results.reshape(TOKENS, MODEL_DIMENSION), input_grads.reshape(TOKENS, MODEL_DIMENSION), totals[0], totals[1], totals[2], totals[3], totals[4], totals[5], totals[6], totals[7], totals[8], totals[9], totals[10])
```

```python
import jax
import jax.numpy as jnp
from jax import lax
from jax.sharding import Mesh, PartitionSpec as P

HEAD_SIZE = 64
EPSILON = 1e-05
THETA_BASE = 1000000.0
NEG_FILL = -1e30
BF = jnp.bfloat16
F32 = jnp.float32
PLANE = ("chip", "core")


def rotary_tables(positions, head_dim):
    half_dim = head_dim // 2
    inverse = THETA_BASE ** (-(jnp.arange(half_dim, dtype=F32) * 2.0) / head_dim)
    angles = positions.astype(F32)[:, None] * inverse[None, :]
    return (jnp.cos(angles)[:, None, :], jnp.sin(angles)[:, None, :])


def apply_rotary(values, cosine_table, sine_values):
    half_dim = values.shape[-1] // 2
    first_part = values[..., :half_dim]
    second_part = values[..., half_dim:]
    return jnp.concatenate(
        [
            first_part * cosine_table - second_part * sine_values,
            second_part * cosine_table + first_part * sine_values,
        ],
        axis=-1,
    )


def unit_rows(values):
    inverse = lax.rsqrt(jnp.mean(values * values, axis=-1, keepdims=True) + EPSILON)
    return (values * inverse, inverse)


def unit_back(grad_unit, unit_vals, inverse):
    return inverse * (
        grad_unit - unit_vals * jnp.mean(grad_unit * unit_vals, axis=-1, keepdims=True)
    )


def mm(a, b):
    return jnp.dot(a, b, preferred_element_type=F32)


def mm_last(a, b):
    return lax.dot_general(a, b, (((1,), (1,)), ((), ())), preferred_element_type=F32)


def mm_first(a, b):
    return lax.dot_general(a, b, (((0,), (0,)), ((), ())), preferred_element_type=F32)


def swap_cores(a):
    return lax.ppermute(a, "core", [(0, 1), (1, 0)])


def line_gather(own):
    count = lax.axis_size("fsdp")
    ahead = [(i, i + 1) for i in range(count - 1)]
    back = [(i + 1, i) for i in range(count - 1)]
    right, left, rights, lefts = own, own, [], []
    for _ in range(count - 1):
        right = lax.ppermute(right, "fsdp", ahead)
        left = lax.ppermute(left, "fsdp", back)
        rights.append(right)
        lefts.append(left)
    mine = lax.axis_index("fsdp")
    return [own] + [
        jnp.where(mine >= d, rights[d - 1], lefts[count - d - 1]) for d in range(1, count)
    ]


def line_scatter(parts):
    count = lax.axis_size("fsdp")
    right = left = None
    for t in range(count - 1):
        low = parts[t + 1].astype(F32)
        high = parts[count - 1 - t].astype(F32)
        if t:
            low, high = low + right.astype(F32), high + left.astype(F32)
        right = lax.ppermute(low.astype(BF), "fsdp", [(i, i + 1) for i in range(t + 1)])
        left = lax.ppermute(
            high.astype(BF), "fsdp", [(count - 1 - i, count - 2 - i) for i in range(t + 1)]
        )
    return parts[0].astype(F32) + right.astype(F32) + left.astype(F32)


def transpose_line(pieces):
    return lax.all_to_all(pieces, "fsdp", split_axis=0, concat_axis=0, tiled=True)


def gather_small(own):
    count = lax.axis_size("fsdp")
    mine = lax.axis_index("fsdp")
    ring = [own] + [
        lax.ppermute(own, "fsdp", [((i + d) % count, i) for i in range(count)])
        for d in range(1, count)
    ]
    twice = jnp.stack(ring + ring)
    return lax.dynamic_slice_in_dim(twice, count - mine, count)


def sum_small(rows):
    count = lax.axis_size("fsdp")
    chips = lax.axis_size("chip")
    mine = lax.axis_index("fsdp")
    total = lax.dynamic_index_in_dim(rows, mine, keepdims=False)
    for d in range(1, count):
        term = lax.dynamic_index_in_dim(rows, (mine + d) % count, keepdims=False)
        total = total + lax.ppermute(
            term, "fsdp", [(i, (i + d) % count) for i in range(count)]
        )
    total = total + swap_cores(total)
    bit = 1
    while bit < chips:
        total = total + lax.ppermute(total, "chip", [(i, i ^ bit) for i in range(chips)])
        bit *= 2
    return total


def shards(
    inputs,
    doc_lengths,
    attn_gain,
    query_weight,
    key_projection,
    value_projection,
    query_gain,
    key_norm_gain,
    out_weight,
    ffn_gain,
    gate_weight,
    up_weight,
    down_weight,
    cotangent,
):
    tok, width = inputs.shape
    count = lax.axis_size("fsdp")
    chips = lax.axis_size("chip")
    rep = chips * 2
    mine = lax.axis_index("fsdp")
    chip = lax.axis_index("chip")
    core = lax.axis_index("core")
    seq = tok * count
    hd = HEAD_SIZE
    rows = query_weight.shape[0]
    q_cols = query_weight.shape[1] // count
    kv_cols = key_projection.shape[1] // count
    ff = gate_weight.shape[1]
    ff_own = ff // count // 2
    q_heads, kv_heads = q_cols // hd, kv_cols // hd
    groups = q_heads // kv_heads
    scale = hd ** (-0.5)

    share = rows // rep
    at = (chip * 2 + core) * share
    piece = jnp.concatenate(
        [
            lax.dynamic_slice_in_dim(w, at, share).reshape(share, count, -1)
            for w in (query_weight, key_projection, value_projection)
        ],
        axis=2,
    )
    piece = transpose_line(piece.transpose(1, 0, 2))
    proj = lax.all_gather(piece, PLANE, axis=0)
    proj = proj.transpose(1, 0, 2, 3).reshape(width, q_cols + 2 * kv_cols)

    x_all = jnp.concatenate(line_gather(inputs), axis=0)

    gains = gather_small(jnp.concatenate([attn_gain, ffn_gain, query_gain, key_norm_gain]))
    gains = gains.astype(F32)
    gain_one = gains[:, :rows].reshape(-1)
    gain_two = gains[:, rows : 2 * rows].reshape(-1)
    small = hd // count
    gain_query = gains[:, 2 * rows : 2 * rows + small].reshape(-1)
    gain_key = gains[:, 2 * rows + small :].reshape(-1)

    part = rows // chips
    slabs = [
        lax.dynamic_slice_in_dim(w, chip * part, part).reshape(part, count, 2, ff_own)
        for w in (gate_weight, up_weight)
    ]
    slab = jnp.concatenate(
        [lax.dynamic_index_in_dim(s, core, axis=2, keepdims=False) for s in slabs], axis=2
    )
    slab = transpose_line(slab.transpose(1, 0, 2))
    pair = lax.all_gather(slab, "chip", axis=0)
    pair = pair.transpose(1, 0, 2, 3).reshape(width, 2 * ff_own)

    order = (mine - jnp.arange(count, dtype=jnp.int32)) % count
    positions = (order[:, None] * tok + jnp.arange(tok, dtype=jnp.int32)[None, :]).reshape(-1)
    lengths = doc_lengths[0]
    docs = lengths.shape[0]
    upto = jnp.arange(docs)[None, :] <= jnp.arange(docs)[:, None]
    ends = jnp.sum(jnp.where(upto, lengths[None, :], 0), axis=1)
    segment = jnp.sum((positions[:, None] >= ends[None, :]).astype(jnp.int32), axis=1)
    allowed = (segment[:, None] == segment[None, :]) & (positions[None, :] <= positions[:, None])
    cosine, sine = rotary_tables(positions, hd)

    unit_one, inverse_one = unit_rows(x_all.astype(F32))
    normed_one = (unit_one * gain_one).astype(BF)
    qkv = mm(normed_one, proj)
    q_unit, q_inv = unit_rows(qkv[:, :q_cols].reshape(seq, q_heads, hd))
    k_unit, k_inv = unit_rows(qkv[:, q_cols : q_cols + kv_cols].reshape(seq, kv_heads, hd))
    values = qkv[:, q_cols + kv_cols :].astype(BF).reshape(seq, kv_heads, hd)
    queries = apply_rotary(q_unit * gain_query, cosine, sine).astype(BF)
    keys = apply_rotary(k_unit * gain_key, cosine, sine).astype(BF)
    grouped = queries.reshape(seq, kv_heads, groups, hd)
    scores = jnp.einsum("tngd,snd->ngts", grouped, keys, preferred_element_type=F32) * scale
    scores = jnp.where(allowed, scores, NEG_FILL)
    expo = jnp.exp(scores - jnp.max(scores, axis=-1, keepdims=True))
    probs = expo / jnp.sum(expo, axis=-1, keepdims=True)
    probs_low = probs.astype(BF)
    attended = jnp.einsum("ngts,snd->tngd", probs_low, values, preferred_element_type=F32)
    attended = attended.astype(BF).reshape(seq, q_cols)
    out_part = mm(attended, out_weight).reshape(count, tok, width)
    inputs_wide = inputs.astype(F32)
    hidden_one = inputs_wide + line_scatter([out_part[d] for d in range(count)])

    unit_two, inverse_two = unit_rows(hidden_one)
    normed_two = jnp.concatenate(
        line_gather((unit_two * gain_two).astype(BF)), axis=0
    )
    normed_two = jnp.concatenate([normed_two, swap_cores(normed_two)], axis=0)
    cot_own = jnp.concatenate(line_gather(cotangent), axis=0)
    cot_all = jnp.concatenate([cot_own, swap_cores(cot_own)], axis=0)
    down_own = lax.dynamic_slice_in_dim(down_weight, core * ff_own, ff_own)
    grad_hidden = mm_last(cot_all, down_own)
    both = mm(normed_two, pair)
    gate_pre, upward = both[:, :ff_own], both[:, ff_own:]
    sigmoid = jax.nn.sigmoid(gate_pre)
    silu = gate_pre * sigmoid
    hidden = (silu * upward).astype(BF)
    grad_both = jnp.concatenate(
        [
            (grad_hidden * upward * sigmoid * (1.0 + gate_pre * (1.0 - sigmoid))).astype(BF),
            (grad_hidden * silu).astype(BF),
        ],
        axis=1,
    )

    def sum_tokens(left, weight, product):
        other = swap_cores(product(left[seq:], weight).astype(BF))
        own = product(left[:seq], weight) + other.astype(F32)
        own = own.reshape(count, tok, width)
        return line_scatter([own[d] for d in range(count)])

    grad_normed_two = sum_tokens(grad_both, pair, mm_last)
    output = (hidden_one + sum_tokens(hidden, down_own, mm)).astype(BF)

    down_sum = lax.psum_scatter(
        mm_first(hidden, cot_all).astype(BF), "chip", scatter_dimension=0, tiled=True
    )
    down_grad = lax.all_gather(down_sum, PLANE, axis=0)
    down_grad = down_grad.reshape(chips, 2, ff_own // chips, width).transpose(1, 0, 2, 3)
    down_grad = down_grad.reshape(2 * ff_own, width).astype(F32)
    pair_part = mm_first(normed_two, grad_both).astype(BF)
    pair_part = pair_part.reshape(count, chips, part, 2 * ff_own).transpose(1, 0, 2, 3)
    pair_part = pair_part.reshape(width, 2 * ff_own)
    pair_sum = lax.psum_scatter(pair_part, "chip", scatter_dimension=0, tiled=True)
    pair_sum = transpose_line(pair_sum.reshape(count, part, 2 * ff_own))
    pair_grad = lax.all_gather(pair_sum, PLANE, axis=0)
    pair_grad = pair_grad.reshape(chips, 2, count, part, 2, ff_own).transpose(4, 0, 3, 2, 1, 5)
    pair_grad = pair_grad.reshape(2, rows, ff).astype(F32)

    gain_two_sum = jnp.sum(grad_normed_two * unit_two, axis=0)
    grad_hidden_one = cotangent.astype(F32) + unit_back(
        grad_normed_two * gain_two, unit_two, inverse_two
    )
    grad_attn = jnp.concatenate(line_gather(grad_hidden_one.astype(BF)), axis=0)
    grad_att = mm_last(grad_attn, out_weight).astype(BF).reshape(seq, kv_heads, groups, hd)
    grad_probs = jnp.einsum("tngd,snd->ngts", grad_att, values, preferred_element_type=F32)
    delta = jnp.sum(probs * grad_probs, axis=-1, keepdims=True)
    grad_scores = (probs * (grad_probs - delta)).astype(BF)
    grad_q = jnp.einsum("ngts,snd->tngd", grad_scores, keys, preferred_element_type=F32) * scale
    grad_k = jnp.einsum("ngts,tngd->snd", grad_scores, grouped, preferred_element_type=F32) * scale
    grad_v = jnp.einsum("ngts,tngd->snd", probs_low, grad_att, preferred_element_type=F32)
    grad_q_unit = apply_rotary(grad_q.reshape(seq, q_heads, hd), cosine, -sine)
    grad_k_unit = apply_rotary(grad_k, cosine, -sine)
    query_gain_sum = jnp.sum(grad_q_unit * q_unit, axis=(0, 1))
    key_gain_sum = jnp.sum(grad_k_unit * k_unit, axis=(0, 1))
    grad_proj = jnp.concatenate(
        [
            unit_back(grad_q_unit * gain_query, q_unit, q_inv).astype(BF).reshape(seq, q_cols),
            unit_back(grad_k_unit * gain_key, k_unit, k_inv).astype(BF).reshape(seq, kv_cols),
            grad_v.astype(BF).reshape(seq, kv_cols),
        ],
        axis=1,
    )
    one_part = mm_last(grad_proj, proj).reshape(count, tok, width)
    grad_normed_one = line_scatter([one_part[d] for d in range(count)])
    unit_own = unit_one[:tok]
    gain_one_sum = jnp.sum(grad_normed_one * unit_own, axis=0)
    input_grad = (
        grad_hidden_one + unit_back(grad_normed_one * gain_one, unit_own, inverse_one[:tok])
    ).astype(BF)

    proj_part = mm_first(normed_one, grad_proj).astype(BF)
    proj_part = proj_part.reshape(count, rep, share, -1).transpose(1, 0, 2, 3)
    proj_part = proj_part.reshape(width, -1)
    proj_sum = lax.psum_scatter(proj_part, PLANE, scatter_dimension=0, tiled=True)
    proj_sum = transpose_line(proj_sum.reshape(count, share, -1))
    proj_grad = lax.all_gather(proj_sum, PLANE, axis=0)

    def rows_of(start, stop):
        columns = proj_grad[..., start:stop].transpose(0, 2, 1, 3)
        return columns.reshape(rows, -1).astype(F32)

    out_sum = lax.psum_scatter(
        mm_first(attended, grad_attn).astype(BF), PLANE, scatter_dimension=0, tiled=True
    )
    out_grad = lax.all_gather(out_sum, PLANE, axis=0, tiled=True).astype(F32)

    sums = sum_small(
        jnp.concatenate(
            [
                v.reshape(count, -1)
                for v in (gain_one_sum, gain_two_sum, query_gain_sum, key_gain_sum)
            ],
            axis=1,
        )
    )
    return (
        output,
        input_grad,
        sums[:rows],
        rows_of(0, q_cols),
        rows_of(q_cols, q_cols + kv_cols),
        rows_of(q_cols + kv_cols, q_cols + 2 * kv_cols),
        sums[2 * rows : 2 * rows + small],
        sums[2 * rows + small :],
        out_grad,
        sums[rows : 2 * rows],
        pair_grad[0],
        pair_grad[1],
        down_grad,
    )


def solution(mesh):
    chips, count = mesh.shape["rep"] // 2, mesh.shape["fsdp"]
    split = Mesh(mesh.devices.reshape(chips, 2, count), ("chip", "core", "fsdp"))
    tokens, reps, fsdp = (*PLANE, "fsdp"), PLANE, "fsdp"
    in_specs = (
        P(tokens, None),
        P(reps, None),
        P(fsdp),
        P(fsdp, None),
        P(fsdp, None),
        P(fsdp, None),
        P(fsdp),
        P(fsdp),
        P(fsdp, None),
        P(fsdp),
        P(fsdp, None),
        P(fsdp, None),
        P(fsdp, None),
        P(tokens, None),
    )
    out_specs = (
        P(tokens, None),
        P(tokens, None),
        P(fsdp),
        P(fsdp, None),
        P(fsdp, None),
        P(fsdp, None),
        P(fsdp),
        P(fsdp),
        P(fsdp, None),
        P(fsdp),
        P(fsdp, None),
        P(fsdp, None),
        P(fsdp, None),
    )
    return jax.shard_map(
        shards, mesh=split, in_specs=in_specs, out_specs=out_specs, check_vma=False
    )
```

```python
import jax
import jax.numpy as jnp
from jax import lax
from jax.experimental import pallas as pl
from jax.sharding import Mesh, PartitionSpec as P

HEAD_SIZE = 64
EPSILON = 1e-05
THETA_BASE = 1000000.0
NEG_FILL = -1e30
BF = jnp.bfloat16
F32 = jnp.float32
PLANE = ("chip", "core")


def rotary_tables(positions, head_dim):
    half_dim = head_dim // 2
    inverse = THETA_BASE ** (-(jnp.arange(half_dim, dtype=F32) * 2.0) / head_dim)
    angles = positions.astype(F32)[:, None] * inverse[None, :]
    return (jnp.cos(angles)[:, None, :], jnp.sin(angles)[:, None, :])


def apply_rotary(values, cosine_table, sine_values):
    half_dim = values.shape[-1] // 2
    first_part = values[..., :half_dim]
    second_part = values[..., half_dim:]
    return jnp.concatenate(
        [
            first_part * cosine_table - second_part * sine_values,
            second_part * cosine_table + first_part * sine_values,
        ],
        axis=-1,
    )


def unit_rows(values):
    inverse = lax.rsqrt(jnp.mean(values * values, axis=-1, keepdims=True) + EPSILON)
    return (values * inverse, inverse)


def unit_back(grad_unit, unit_vals, inverse):
    return inverse * (
        grad_unit - unit_vals * jnp.mean(grad_unit * unit_vals, axis=-1, keepdims=True)
    )


def mm(a, b):
    return jnp.dot(a, b, preferred_element_type=F32)


def mm_last(a, b):
    return lax.dot_general(a, b, (((1,), (1,)), ((), ())), preferred_element_type=F32)


def mm_first(a, b):
    return lax.dot_general(a, b, (((0,), (0,)), ((), ())), preferred_element_type=F32)


def swap_cores(a):
    return lax.ppermute(a, "core", [(0, 1), (1, 0)])


def line_gather(own):
    count = lax.axis_size("fsdp")
    ahead = [(i, i + 1) for i in range(count - 1)]
    back = [(i + 1, i) for i in range(count - 1)]
    right, left, rights, lefts = own, own, [], []
    for _ in range(count - 1):
        right = lax.ppermute(right, "fsdp", ahead)
        left = lax.ppermute(left, "fsdp", back)
        rights.append(right)
        lefts.append(left)
    mine = lax.axis_index("fsdp")
    return [own] + [
        jnp.where(mine >= d, rights[d - 1], lefts[count - d - 1]) for d in range(1, count)
    ]


def line_scatter(parts, ahead_of=()):
    count = lax.axis_size("fsdp")
    right = left = None
    for t in range(count - 1):
        low = parts[t + 1].astype(F32)
        high = parts[count - 1 - t].astype(F32)
        if t:
            if t <= len(ahead_of):
                right, left, _ = lax.optimization_barrier((right, left, ahead_of[t - 1]))
            low, high = low + right.astype(F32), high + left.astype(F32)
        right = lax.ppermute(low.astype(BF), "fsdp", [(i, i + 1) for i in range(t + 1)])
        left = lax.ppermute(
            high.astype(BF), "fsdp", [(count - 1 - i, count - 2 - i) for i in range(t + 1)]
        )
    return parts[0].astype(F32) + right.astype(F32) + left.astype(F32)


def absolute(ring):
    count = len(ring)
    twice = jnp.stack(ring + ring)
    return lax.dynamic_slice_in_dim(twice, count - lax.axis_index("fsdp"), count)


def exchange_line(piece_for):
    count = lax.axis_size("fsdp")
    mine = lax.axis_index("fsdp")
    return absolute(
        [piece_for(mine)]
        + [
            lax.ppermute(
                piece_for((mine - e) % count),
                "fsdp",
                [(i, (i - e) % count) for i in range(count)],
            )
            for e in range(1, count)
        ]
    )


def after(value, *others):
    return lax.optimization_barrier((value, *others))[0]


def gather_small(own):
    return exchange_line(lambda j: own)


def sum_small(rows):
    count = lax.axis_size("fsdp")
    chips = lax.axis_size("chip")
    mine = lax.axis_index("fsdp")
    total = lax.dynamic_index_in_dim(rows, mine, keepdims=False)
    for d in range(1, count):
        term = lax.dynamic_index_in_dim(rows, (mine + d) % count, keepdims=False)
        total = total + lax.ppermute(
            term, "fsdp", [(i, (i + d) % count) for i in range(count)]
        )
    total = total + swap_cores(total)
    bit = 1
    while bit < chips:
        total = total + lax.ppermute(total, "chip", [(i, i ^ bit) for i in range(chips)])
        bit *= 2
    return total


def cast_pair(own, gate, up):
    half = gate.shape[1]
    gate[...] = own[0, :, :half].astype(F32)
    up[...] = own[0, :, half:].astype(F32)


def place_pair(own, chips, count, part, half):
    block = pl.BlockSpec((part, half), lambda c, j, k: (c, j * 2 + k))
    shape = jax.ShapeDtypeStruct((chips * part, count * 2 * half), F32)
    return pl.pallas_call(
        cast_pair,
        grid=(chips, count, 2),
        in_specs=[pl.BlockSpec((1, part, 2 * half), lambda c, j, k: (c * 2 + k, j, 0))],
        out_specs=[block, block],
        out_shape=[shape, shape],
    )(own)


def cast_down(own, out):
    out[...] = own[0].astype(F32)


def place_down(own, chips, part, width):
    return pl.pallas_call(
        cast_down,
        grid=(2, chips),
        in_specs=[pl.BlockSpec((1, part, width), lambda k, c: (c * 2 + k, 0, 0))],
        out_specs=pl.BlockSpec((part, width), lambda k, c: (k * chips + c, 0)),
        out_shape=jax.ShapeDtypeStruct((2 * chips * part, width), F32),
    )(own)


def shards(
    inputs,
    doc_lengths,
    attn_gain,
    query_weight,
    key_projection,
    value_projection,
    query_gain,
    key_norm_gain,
    out_weight,
    ffn_gain,
    gate_weight,
    up_weight,
    down_weight,
    cotangent,
):
    tok, width = inputs.shape
    count = lax.axis_size("fsdp")
    chips = lax.axis_size("chip")
    rep = chips * 2
    mine = lax.axis_index("fsdp")
    chip = lax.axis_index("chip")
    core = lax.axis_index("core")
    seq = tok * count
    hd = HEAD_SIZE
    rows = query_weight.shape[0]
    q_cols = query_weight.shape[1] // count
    kv_cols = key_projection.shape[1] // count
    ff = gate_weight.shape[1]
    ff_own = ff // count // 2
    q_heads, kv_heads = q_cols // hd, kv_cols // hd
    groups = q_heads // kv_heads
    scale = hd ** (-0.5)

    share = rows // rep
    at = (chip * 2 + core) * share

    def proj_piece(j):
        return jnp.concatenate(
            [
                lax.dynamic_slice(w, (at, j * wide), (share, wide))
                for w, wide in (
                    (query_weight, q_cols),
                    (key_projection, kv_cols),
                    (value_projection, kv_cols),
                )
            ],
            axis=1,
        )

    x_all = jnp.concatenate(line_gather(inputs), axis=0)
    proj = lax.all_gather(exchange_line(proj_piece), PLANE, axis=0)
    proj = proj.transpose(1, 0, 2, 3).reshape(width, q_cols + 2 * kv_cols)

    gains = gather_small(jnp.concatenate([attn_gain, ffn_gain, query_gain, key_norm_gain]))
    gains = gains.astype(F32)
    gain_one = gains[:, :rows].reshape(-1)
    gain_two = gains[:, rows : 2 * rows].reshape(-1)
    small = hd // count
    gain_query = gains[:, 2 * rows : 2 * rows + small].reshape(-1)
    gain_key = gains[:, 2 * rows + small :].reshape(-1)

    part = rows // chips
    gate_up = after((gate_weight, up_weight), x_all)

    def pair_piece(j):
        return jnp.concatenate(
            [
                lax.dynamic_slice(w, (chip * part, (j * 2 + core) * ff_own), (part, ff_own))
                for w in gate_up
            ],
            axis=1,
        )

    pair = lax.all_gather(exchange_line(pair_piece), "chip", axis=0)
    pair = pair.reshape(width, 2 * ff_own)

    def to_chip_order(a):
        return a.reshape(tok, count, chips, part).transpose(0, 2, 1, 3).reshape(tok, width)

    def from_chip_order(a):
        return a.reshape(tok, chips, count, part).transpose(0, 2, 1, 3).reshape(tok, width)

    order = (mine - jnp.arange(count, dtype=jnp.int32)) % count
    positions = (order[:, None] * tok + jnp.arange(tok, dtype=jnp.int32)[None, :]).reshape(-1)
    lengths = doc_lengths[0]
    docs = lengths.shape[0]
    upto = jnp.arange(docs)[None, :] <= jnp.arange(docs)[:, None]
    ends = jnp.sum(jnp.where(upto, lengths[None, :], 0), axis=1)
    segment = jnp.sum((positions[:, None] >= ends[None, :]).astype(jnp.int32), axis=1)
    allowed = (segment[:, None] == segment[None, :]) & (positions[None, :] <= positions[:, None])
    cosine, sine = rotary_tables(positions, hd)

    unit_one, inverse_one = unit_rows(x_all.astype(F32))
    normed_one = (unit_one * gain_one).astype(BF)
    qkv = mm(normed_one, proj)
    q_unit, q_inv = unit_rows(qkv[:, :q_cols].reshape(seq, q_heads, hd))
    k_unit, k_inv = unit_rows(qkv[:, q_cols : q_cols + kv_cols].reshape(seq, kv_heads, hd))
    values = qkv[:, q_cols + kv_cols :].astype(BF).reshape(seq, kv_heads, hd)
    queries = apply_rotary(q_unit * gain_query, cosine, sine).astype(BF)
    keys = apply_rotary(k_unit * gain_key, cosine, sine).astype(BF)
    grouped = queries.reshape(seq, kv_heads, groups, hd)
    scores = jnp.einsum("tngd,snd->ngts", grouped, keys, preferred_element_type=F32) * scale
    scores = jnp.where(allowed, scores, NEG_FILL)
    expo = jnp.exp(scores - jnp.max(scores, axis=-1, keepdims=True))
    probs = expo / jnp.sum(expo, axis=-1, keepdims=True)
    probs_low = probs.astype(BF)
    attended = jnp.einsum("ngts,snd->tngd", probs_low, values, preferred_element_type=F32)
    attended = attended.astype(BF).reshape(seq, q_cols)
    out_part = mm(attended, out_weight).reshape(count, tok, width)
    inputs_wide = inputs.astype(F32)
    hidden_one = inputs_wide + line_scatter([out_part[d] for d in range(count)])

    unit_two, inverse_two = unit_rows(hidden_one)
    normed_two = jnp.concatenate(
        line_gather(to_chip_order((unit_two * gain_two).astype(BF))), axis=0
    )
    normed_two = jnp.concatenate([normed_two, swap_cores(normed_two)], axis=0)
    cot_own = jnp.concatenate(line_gather(after(cotangent, normed_two)), axis=0)
    cot_all = jnp.concatenate([cot_own, swap_cores(cot_own)], axis=0)
    down_own = lax.dynamic_slice_in_dim(down_weight, core * ff_own, ff_own)
    grad_hidden = mm_last(cot_all, down_own)
    both = mm(normed_two, pair)
    gate_pre, upward = both[:, :ff_own], both[:, ff_own:]
    sigmoid = jax.nn.sigmoid(gate_pre)
    silu = gate_pre * sigmoid
    hidden = (silu * upward).astype(BF)
    grad_both = jnp.concatenate(
        [
            (grad_hidden * upward * sigmoid * (1.0 + gate_pre * (1.0 - sigmoid))).astype(BF),
            (grad_hidden * silu).astype(BF),
        ],
        axis=1,
    )

    def sum_tokens(left, weight, product, ahead_of=()):
        other = swap_cores(product(left[seq:], weight).astype(BF))
        own = product(left[:seq], weight) + other.astype(F32)
        own = own.reshape(count, tok, width)
        return line_scatter([own[d] for d in range(count)], ahead_of)

    down_part = mm_first(hidden, cot_all).astype(BF)
    pair_part = mm_first(normed_two, grad_both).astype(BF)
    grad_normed_two = from_chip_order(
        sum_tokens(grad_both, pair, mm_last, (down_part, pair_part))
    )

    down_sum = lax.psum_scatter(down_part, "chip", scatter_dimension=0, tiled=True)
    pair_sum = lax.psum_scatter(pair_part, "chip", scatter_dimension=0, tiled=True)
    pair_sum = pair_sum.reshape(count, part, 2 * ff_own)
    pair_sum = exchange_line(
        lambda j: lax.dynamic_index_in_dim(pair_sum, j, keepdims=False)
    )
    ffn_sum = pair_sum.reshape(count * part, 2 * ff_own)

    gain_two_sum = jnp.sum(grad_normed_two * unit_two, axis=0)
    grad_hidden_one = cotangent.astype(F32) + unit_back(
        grad_normed_two * gain_two, unit_two, inverse_two
    )
    grad_attn = jnp.concatenate(line_gather(grad_hidden_one.astype(BF)), axis=0)
    output = (hidden_one + sum_tokens(after(hidden, grad_attn), down_own, mm)).astype(BF)
    grad_att = mm_last(grad_attn, out_weight).astype(BF).reshape(seq, kv_heads, groups, hd)
    grad_probs = jnp.einsum("tngd,snd->ngts", grad_att, values, preferred_element_type=F32)
    delta = jnp.sum(probs * grad_probs, axis=-1, keepdims=True)
    grad_scores = (probs * (grad_probs - delta)).astype(BF)
    grad_q = jnp.einsum("ngts,snd->tngd", grad_scores, keys, preferred_element_type=F32) * scale
    grad_k = jnp.einsum("ngts,tngd->snd", grad_scores, grouped, preferred_element_type=F32) * scale
    grad_v = jnp.einsum("ngts,tngd->snd", probs_low, grad_att, preferred_element_type=F32)
    grad_q_unit = apply_rotary(grad_q.reshape(seq, q_heads, hd), cosine, -sine)
    grad_k_unit = apply_rotary(grad_k, cosine, -sine)
    query_gain_sum = jnp.sum(grad_q_unit * q_unit, axis=(0, 1))
    key_gain_sum = jnp.sum(grad_k_unit * k_unit, axis=(0, 1))
    grad_proj = jnp.concatenate(
        [
            unit_back(grad_q_unit * gain_query, q_unit, q_inv).astype(BF).reshape(seq, q_cols),
            unit_back(grad_k_unit * gain_key, k_unit, k_inv).astype(BF).reshape(seq, kv_cols),
            grad_v.astype(BF).reshape(seq, kv_cols),
        ],
        axis=1,
    )
    one_part = mm_last(grad_proj, proj).reshape(count, tok, width)
    grad_normed_one = line_scatter([one_part[d] for d in range(count)])
    unit_own = unit_one[:tok]
    gain_one_sum = jnp.sum(grad_normed_one * unit_own, axis=0)
    input_grad = (
        grad_hidden_one + unit_back(grad_normed_one * gain_one, unit_own, inverse_one[:tok])
    ).astype(BF)

    proj_part = mm_first(normed_one, grad_proj).astype(BF)
    out_term = mm_first(attended, grad_attn).astype(BF)
    att_part = jnp.concatenate(
        [proj_part[j * rows : (j + 1) * rows] for j in range(count)] + [out_term], axis=1
    )
    att_sum = lax.psum_scatter(att_part, PLANE, scatter_dimension=0, tiled=True)
    cols = q_cols + 2 * kv_cols
    got = exchange_line(lambda j: lax.dynamic_slice(att_sum, (0, j * cols), (share, cols)))
    cuts = ((0, q_cols), (q_cols, q_cols + kv_cols), (q_cols + kv_cols, cols))
    att_sum = jnp.concatenate(
        [got[j, :, a:b] for a, b in cuts for j in range(count)] + [att_sum[:, count * cols :]],
        axis=1,
    )

    down_all = lax.all_gather(down_sum, PLANE, axis=0)
    ffn_all = lax.all_gather(ffn_sum, PLANE, axis=0)
    gate_grad, up_grad = place_pair(ffn_all, chips, count, part, ff_own)
    down_grad = place_down(down_all, chips, ff_own // chips, width)
    att_all = lax.all_gather(att_sum, PLANE, axis=0, tiled=True)
    edges = [0, q_cols * count, (q_cols + kv_cols) * count, cols * count, att_all.shape[1]]
    query_grad, key_grad, value_grad, out_grad = (
        att_all[:, a:b].astype(F32) for a, b in zip(edges[:-1], edges[1:])
    )

    sums = sum_small(
        jnp.concatenate(
            [
                v.reshape(count, -1)
                for v in (gain_one_sum, gain_two_sum, query_gain_sum, key_gain_sum)
            ],
            axis=1,
        )
    )
    return (
        output,
        input_grad,
        sums[:rows],
        query_grad,
        key_grad,
        value_grad,
        sums[2 * rows : 2 * rows + small],
        sums[2 * rows + small :],
        out_grad,
        sums[rows : 2 * rows],
        gate_grad,
        up_grad,
        down_grad,
    )


def solution(mesh):
    chips, count = mesh.shape["rep"] // 2, mesh.shape["fsdp"]
    split = Mesh(mesh.devices.reshape(chips, 2, count), ("chip", "core", "fsdp"))
    tokens, reps, fsdp = (*PLANE, "fsdp"), PLANE, "fsdp"
    in_specs = (
        P(tokens, None),
        P(reps, None),
        P(fsdp),
        P(fsdp, None),
        P(fsdp, None),
        P(fsdp, None),
        P(fsdp),
        P(fsdp),
        P(fsdp, None),
        P(fsdp),
        P(fsdp, None),
        P(fsdp, None),
        P(fsdp, None),
        P(tokens, None),
    )
    out_specs = (
        P(tokens, None),
        P(tokens, None),
        P(fsdp),
        P(fsdp, None),
        P(fsdp, None),
        P(fsdp, None),
        P(fsdp),
        P(fsdp),
        P(fsdp, None),
        P(fsdp),
        P(fsdp, None),
        P(fsdp, None),
        P(fsdp, None),
    )
    return jax.shard_map(
        shards, mesh=split, in_specs=in_specs, out_specs=out_specs, check_vma=False
    )
```

```python
import functools

import jax
import jax.numpy as jnp
from jax import lax
from jax.experimental import pallas as pl
from jax.experimental.pallas import tpu as pltpu
from jax.sharding import Mesh, PartitionSpec as P

HEAD_SIZE = 64
EPSILON = 1e-05
THETA_BASE = 1000000.0
NEG_FILL = -1e30
BF = jnp.bfloat16
F32 = jnp.float32
PLANE = ("chip", "core")


def rotary_tables(positions, head_dim):
    half_dim = head_dim // 2
    inverse = THETA_BASE ** (-(jnp.arange(half_dim, dtype=F32) * 2.0) / head_dim)
    angles = positions.astype(F32)[:, None] * inverse[None, :]
    return (jnp.cos(angles)[:, None, :], jnp.sin(angles)[:, None, :])


def apply_rotary(values, cosine_table, sine_values):
    half_dim = values.shape[-1] // 2
    first_part = values[..., :half_dim]
    second_part = values[..., half_dim:]
    return jnp.concatenate(
        [
            first_part * cosine_table - second_part * sine_values,
            second_part * cosine_table + first_part * sine_values,
        ],
        axis=-1,
    )


def unit_rows(values):
    inverse = lax.rsqrt(jnp.mean(values * values, axis=-1, keepdims=True) + EPSILON)
    return (values * inverse, inverse)


def unit_back(grad_unit, unit_vals, inverse):
    return inverse * (
        grad_unit - unit_vals * jnp.mean(grad_unit * unit_vals, axis=-1, keepdims=True)
    )


def mm(a, b):
    return jnp.dot(a, b, preferred_element_type=F32)


def mm_last(a, b):
    return lax.dot_general(a, b, (((1,), (1,)), ((), ())), preferred_element_type=F32)


def mm_first(a, b):
    return lax.dot_general(a, b, (((0,), (0,)), ((), ())), preferred_element_type=F32)


def swap_cores(a):
    return lax.ppermute(a, "core", [(0, 1), (1, 0)])


def exchanges():
    count = lax.axis_size("fsdp")
    even = [(i, i ^ 1) for i in range(count)]
    odd = [(0, 0)] + [(i, ((i - 1) ^ 1) + 1) for i in range(1, count - 1)] + [(count - 1, count - 1)]
    return even, odd


def line_step(first, second):
    even, odd = exchanges()
    return lax.ppermute(first, "fsdp", even), lax.ppermute(second, "fsdp", odd)


def line_steps(own, ahead_of={}, begun=None, turn=None):
    steps = []
    first, second = own, own
    for t in range(lax.axis_size("fsdp") - 1):
        if t in ahead_of:
            first, second = after((first, second), ahead_of[t])
        if t and turn:
            first, second = after((first, second), turn((first, second)))
        if t == 0 and begun:
            by_even, by_odd = begun
        else:
            by_even, by_odd = line_step(first, second)
        steps.append((by_even, by_odd))
        first, second = by_odd, by_even
    return steps


def line_pieces(own, steps):
    count = lax.axis_size("fsdp")
    mine = lax.axis_index("fsdp")
    is_even = mine % 2 == 0
    pieces = [own]
    for d in range(1, count):
        below, above = steps[d - 1], steps[count - d - 1]
        from_below = jnp.where(is_even, below[1], below[0])
        from_above = jnp.where(is_even, above[0], above[1])
        pieces.append(jnp.where(mine >= d, from_below, from_above))
    return pieces


def line_scatter(parts, ahead_of=None):
    count = lax.axis_size("fsdp")
    mine = lax.axis_index("fsdp")
    is_even = mine % 2 == 0
    is_end = (mine == 0) | (mine == count - 1)
    by_even = by_odd = None
    for t in range(count - 1):
        up = jnp.where(is_even, t + 1, count - 1 - t)
        first = lax.dynamic_index_in_dim(parts, up, keepdims=False)
        second = lax.dynamic_index_in_dim(parts, count - up, keepdims=False)
        if t:
            if ahead_of:
                by_even, by_odd = after((by_even, by_odd), ahead_of(t, (by_even, by_odd)))
            first, second = first + by_odd.astype(F32), second + by_even.astype(F32)
        second = jnp.where(is_end, 0.0, second)
        by_even, by_odd = line_step(first.astype(BF), second.astype(BF))
    return by_even, by_odd


def absolute(ring):
    count = len(ring)
    twice = jnp.stack(ring + ring)
    return lax.dynamic_slice_in_dim(twice, count - lax.axis_index("fsdp"), count)


def exchange_line(piece_for):
    count = lax.axis_size("fsdp")
    mine = lax.axis_index("fsdp")
    return [piece_for(mine)] + [
        lax.ppermute(
            piece_for((mine - e) % count),
            "fsdp",
            [(i, (i - e) % count) for i in range(count)],
        )
        for e in range(1, count)
    ]


def add_low(a, b):
    return (a.astype(F32) + b.astype(F32)).astype(BF)


def halve(blocks, axis, name, bit, pin=()):
    mybit = (lax.axis_index(name) >> bit) & 1
    pairs = [(i, i ^ (1 << bit)) for i in range(lax.axis_size(name))]
    got = lax.ppermute(
        lax.dynamic_index_in_dim(blocks, 1 - mybit, axis, keepdims=False), name, pairs
    )
    got = after(got, pin)
    return add_low(lax.dynamic_index_in_dim(blocks, mybit, axis, keepdims=False), got)


def chip_halves(terms):
    chips, rows, cols = terms.shape
    bits = chips.bit_length() - 1
    return [
        terms[:, g * rows // 2 : (g + 1) * rows // 2].reshape([2] * bits + [rows // 2, cols])
        for g in range(2)
    ]


def row_parts(halves):
    cut = halves[0].shape[-2] // 2
    return [h[..., :cut, :] for h in halves], [h[..., cut:, :] for h in halves]


def join_rows(one, two):
    return [jnp.concatenate(pair, axis=-2) for pair in zip(one, two)]


def chip_stage(halves, step, pin=()):
    bits = lax.axis_size("chip").bit_length() - 1
    out = []
    for g in range(2):
        done = [(g + k) % bits for k in range(step)]
        left = [b for b in range(bits - 1, -1, -1) if b not in done]
        bit = (g + step) % bits
        out.append(halve(halves[g], left.index(bit), "chip", bit, pin))
    return out


def chip_rest(halves, step, pin=()):
    for k in range(step, lax.axis_size("chip").bit_length() - 1):
        halves = chip_stage(halves, k, pin)
    return halves


def after(value, *others):
    return lax.optimization_barrier((value, *others))[0]


def gather_small(own):
    return absolute(exchange_line(lambda j: own))


def sum_small(rows):
    count = lax.axis_size("fsdp")
    chips = lax.axis_size("chip")
    mine = lax.axis_index("fsdp")
    total = lax.dynamic_index_in_dim(rows, mine, keepdims=False)
    for d in range(1, count):
        term = lax.dynamic_index_in_dim(rows, (mine + d) % count, keepdims=False)
        total = total + lax.ppermute(
            term, "fsdp", [(i, (i + d) % count) for i in range(count)]
        )
    total = total + swap_cores(total)
    bit = 1
    while bit < chips:
        total = total + lax.ppermute(total, "chip", [(i, i ^ bit) for i in range(chips)])
        bit *= 2
    return total


def lanes(width, chips, count):
    part = width // chips // count
    return [
        (slice((z * chips + c) * part, (z * chips + c + 1) * part),
         slice((c * count + z) * part, (c * count + z + 1) * part))
        for z in range(count)
        for c in range(chips)
    ]


def inverse_root(wide):
    return lax.rsqrt(jnp.mean(wide * wide, axis=-1, keepdims=True) + EPSILON)


def norm_forward(chips, count, own, part, right, left, gain, hidden, normed):
    wide = own[...].astype(F32) + part[0] + right[...].astype(F32) + left[...].astype(F32)
    hidden[...] = wide
    low = (wide * inverse_root(wide) * gain[...]).astype(BF)
    for here, there in lanes(wide.shape[1], chips, count):
        normed[:, there] = low[:, here]


def norm_backward(chips, count, part, right, left, wide, base, gain, grad, low, total, scratch):
    summed = part[0] + right[...].astype(F32) + left[...].astype(F32)
    if chips:
        for here, there in lanes(summed.shape[1], chips, count):
            scratch[:, here] = summed[:, there]
        summed = scratch[...]
    values = wide[...].astype(F32)
    inverse = inverse_root(values)
    unit = values * inverse
    sums = jnp.sum(summed * unit, axis=0, keepdims=True)

    @pl.when(pl.program_id(0) == 0)
    def _():
        total[...] = sums

    @pl.when(pl.program_id(0) > 0)
    def _():
        total[...] += sums

    scaled = summed * gain[...]
    out = base[...].astype(F32) + inverse * (
        scaled - unit * jnp.mean(scaled * unit, axis=-1, keepdims=True)
    )
    grad[...] = out
    low[...] = out.astype(BF)


def row_specs(tok, width):
    step = min(32, tok)
    block = pl.BlockSpec((step, width), lambda i: (i, 0))
    first = pl.BlockSpec((1, step, width), lambda i: (0, i, 0))
    row = pl.BlockSpec((1, width), lambda i: (0, 0))
    return tok // step, step, block, first, row


def forward_norm(own, parts, right, left, gain, chips, count):
    tok, width = own.shape
    grid, _, block, first, row = row_specs(tok, width)
    return pl.pallas_call(
        functools.partial(norm_forward, chips, count),
        grid=(grid,),
        in_specs=[block, first, block, block, row],
        out_specs=[block, block],
        out_shape=[
            jax.ShapeDtypeStruct((tok, width), F32),
            jax.ShapeDtypeStruct((tok, width), BF),
        ],
    )(own, parts, right, left, gain.reshape(1, width))


def backward_norm(parts, right, left, wide, base, gain, chips, count):
    tok, width = wide.shape
    grid, step, block, first, row = row_specs(tok, width)
    return pl.pallas_call(
        functools.partial(norm_backward, chips, count),
        grid=(grid,),
        in_specs=[first, block, block, block, block, row],
        out_specs=[block, block, row],
        out_shape=[
            jax.ShapeDtypeStruct((tok, width), F32),
            jax.ShapeDtypeStruct((tok, width), BF),
            jax.ShapeDtypeStruct((1, width), F32),
        ],
        scratch_shapes=[pltpu.VMEM((step, width), F32)],
    )(parts, right, left, wide, base, gain.reshape(1, width))


def cast_pair(own, gate, up):
    _, cores, count, _, cols = own.shape
    half = cols // 2
    for j in range(count):
        for k in range(cores):
            at = (j * cores + k) * half
            gate[:, at : at + half] = own[0, k, j, :, :half].astype(F32)
            up[:, at : at + half] = own[0, k, j, :, half:].astype(F32)


def place_pair(own, chips, count, part, half):
    step = min(32, part)
    own = own.reshape(chips, 2, count, part, 2 * half)
    block = pl.BlockSpec((step, count * 2 * half), lambda c, r: (c * (part // step) + r, 0))
    shape = jax.ShapeDtypeStruct((chips * part, count * 2 * half), F32)
    return pl.pallas_call(
        cast_pair,
        grid=(chips, part // step),
        in_specs=[pl.BlockSpec((1, 2, count, step, 2 * half), lambda c, r: (c, 0, 0, r, 0))],
        out_specs=[block, block],
        out_shape=[shape, shape],
    )(own)


def cast_down(own, out):
    out[...] = own[0].astype(F32)


def place_down(own, chips, part, width):
    return pl.pallas_call(
        cast_down,
        grid=(2, chips),
        in_specs=[pl.BlockSpec((1, part, width), lambda k, c: (c * 2 + k, 0, 0))],
        out_specs=pl.BlockSpec((part, width), lambda k, c: (k * chips + c, 0)),
        out_shape=jax.ShapeDtypeStruct((2 * chips * part, width), F32),
    )(own)


def shards(
    inputs,
    doc_lengths,
    attn_gain,
    query_weight,
    key_projection,
    value_projection,
    query_gain,
    key_norm_gain,
    out_weight,
    ffn_gain,
    gate_weight,
    up_weight,
    down_weight,
    cotangent,
):
    tok, width = inputs.shape
    count = lax.axis_size("fsdp")
    chips = lax.axis_size("chip")
    rep = chips * 2
    mine = lax.axis_index("fsdp")
    chip = lax.axis_index("chip")
    core = lax.axis_index("core")
    seq = tok * count
    hd = HEAD_SIZE
    rows = query_weight.shape[0]
    q_cols = query_weight.shape[1] // count
    kv_cols = key_projection.shape[1] // count
    ff = gate_weight.shape[1]
    ff_own = ff // count // 2
    q_heads, kv_heads = q_cols // hd, kv_cols // hd
    groups = q_heads // kv_heads
    scale = hd ** (-0.5)

    share = rows // rep
    at = (chip * 2 + core) * share

    def proj_piece(j):
        return jnp.concatenate(
            [
                lax.dynamic_slice(w, (at, j * wide), (share, wide))
                for w, wide in (
                    (query_weight, q_cols),
                    (key_projection, kv_cols),
                    (value_projection, kv_cols),
                )
            ],
            axis=1,
        )

    proj_ring = exchange_line(proj_piece)
    proj_own = absolute(proj_ring)
    x_all = jnp.concatenate(line_pieces(inputs, line_steps(inputs, {1: proj_own})), axis=0)
    proj = lax.all_gather(proj_own, PLANE, axis=0)
    proj = proj.transpose(1, 0, 2, 3).reshape(width, q_cols + 2 * kv_cols)

    gains = gather_small(jnp.concatenate([attn_gain, ffn_gain, query_gain, key_norm_gain]))
    gains = gains.astype(F32)
    gain_one = gains[:, :rows].reshape(-1)
    gain_two = gains[:, rows : 2 * rows].reshape(-1)
    small = hd // count
    gain_query = gains[:, 2 * rows : 2 * rows + small].reshape(-1)
    gain_key = gains[:, 2 * rows + small :].reshape(-1)

    part = rows // chips
    gate_up = after((gate_weight, up_weight), x_all)

    def pair_piece(j):
        return jnp.concatenate(
            [
                lax.dynamic_slice(w, (chip * part, (j * 2 + core) * ff_own), (part, ff_own))
                for w in gate_up
            ],
            axis=1,
        )

    pair_ring = exchange_line(pair_piece)

    order = (mine - jnp.arange(count, dtype=jnp.int32)) % count
    positions = (order[:, None] * tok + jnp.arange(tok, dtype=jnp.int32)[None, :]).reshape(-1)
    lengths = doc_lengths[0]
    docs = lengths.shape[0]
    upto = jnp.arange(docs)[None, :] <= jnp.arange(docs)[:, None]
    ends = jnp.sum(jnp.where(upto, lengths[None, :], 0), axis=1)
    segment = jnp.sum((positions[:, None] >= ends[None, :]).astype(jnp.int32), axis=1)
    allowed = (segment[:, None] == segment[None, :]) & (positions[None, :] <= positions[:, None])
    cosine, sine = rotary_tables(positions, hd)

    unit_one, inverse_one = unit_rows(x_all.astype(F32))
    normed_one = (unit_one * gain_one).astype(BF)
    qkv = mm(normed_one, proj)
    q_unit, q_inv = unit_rows(qkv[:, :q_cols].reshape(seq, q_heads, hd))
    k_unit, k_inv = unit_rows(qkv[:, q_cols : q_cols + kv_cols].reshape(seq, kv_heads, hd))
    values = qkv[:, q_cols + kv_cols :].astype(BF).reshape(seq, kv_heads, hd)
    queries = apply_rotary(q_unit * gain_query, cosine, sine).astype(BF)
    keys = apply_rotary(k_unit * gain_key, cosine, sine).astype(BF)
    grouped = queries.reshape(seq, kv_heads, groups, hd)
    scores = jnp.einsum("tngd,snd->ngts", grouped, keys, preferred_element_type=F32) * scale
    scores = jnp.where(allowed, scores, NEG_FILL)
    expo = jnp.exp(scores - jnp.max(scores, axis=-1, keepdims=True))
    probs = expo / jnp.sum(expo, axis=-1, keepdims=True)
    probs_low = probs.astype(BF)
    attended = jnp.einsum("ngts,snd->tngd", probs_low, values, preferred_element_type=F32)
    attended = attended.astype(BF).reshape(seq, q_cols)
    out_part = mm(attended, out_weight).reshape(count, tok, width)
    stage = {}

    def slices(t, sides):
        if t == 1:
            stage["slices"] = absolute(after(pair_ring, sides))
            return stage["slices"]
        return ()

    sides = line_scatter(out_part, slices)
    pair = lax.all_gather(stage["slices"], "chip", axis=0)
    pair = pair.reshape(width, 2 * ff_own)
    hidden_one, normed_own = forward_norm(inputs, out_part, *sides, gain_two, chips, count)

    cot_begun = line_step(*(after(cotangent, sides),) * 2)
    two_steps = line_steps(after(normed_own, cot_begun))
    normed_two = jnp.concatenate(line_pieces(normed_own, two_steps), axis=0)
    normed_two = jnp.concatenate([normed_two, swap_cores(normed_two)], axis=0)
    down_own = lax.dynamic_slice_in_dim(down_weight, core * ff_own, ff_own)
    both = mm(normed_two, pair)
    cot_steps = line_steps(cotangent, {1: two_steps[-1], count - 2: both}, cot_begun)
    cot_own = jnp.concatenate(line_pieces(cotangent, cot_steps), axis=0)
    cot_all = jnp.concatenate([cot_own, swap_cores(cot_own)], axis=0)
    grad_hidden = mm_last(cot_all, down_own)
    gate_pre, upward = both[:, :ff_own], both[:, ff_own:]
    sigmoid = jax.nn.sigmoid(gate_pre)
    silu = gate_pre * sigmoid
    hidden = (silu * upward).astype(BF)
    grad_gate = (grad_hidden * upward * sigmoid * (1.0 + gate_pre * (1.0 - sigmoid))).astype(BF)
    grad_up = (grad_hidden * silu).astype(BF)
    grad_both = jnp.concatenate([grad_gate, grad_up], axis=1)

    queue, sums_of = [], {}

    def enqueue(name, terms):
        one, two = row_parts(chip_halves(terms))

        def begin_one(pin):
            sums_of[name] = chip_stage(one, 0, pin)
            return sums_of[name]

        def begin_two(pin):
            got = chip_stage(two, 0, pin)
            sums_of[name] = join_rows(sums_of[name], got)
            return got

        def finish(pin):
            sums_of[name] = chip_rest(sums_of[name], 1, pin)
            return sums_of[name]

        return begin_one, begin_two, finish

    def turn(pin):
        return [piece(pin) for piece in queue.pop(0)] if queue else ()

    down_part = mm_first(hidden, cot_all).astype(BF)
    gate_part = mm_first(normed_two, after(grad_gate, down_part)).astype(BF)
    other = mm_last(after(grad_both[seq:], gate_part), pair).astype(BF)
    up_part = mm_first(normed_two, after(grad_up, other)).astype(BF)
    down_turns = enqueue("down", down_part.reshape(chips, -1, width))
    gate_turns = enqueue("gate", gate_part.reshape(chips, -1, ff_own))
    up_turns = enqueue("up", up_part.reshape(chips, -1, ff_own))
    queue += [[x] for x in (*down_turns[:2], *gate_turns[:2])]
    queue += [[down_turns[2], up_turns[0]], [up_turns[1]], [gate_turns[2]], [up_turns[2]]]

    own = after(grad_both[:seq], up_part, turn(other))
    two_terms = mm_last(own, pair) + swap_cores(other).astype(F32)
    two_terms = two_terms.reshape(count, tok, width)
    sides = line_scatter(after(two_terms, turn(two_terms)), lambda t, sides: turn(sides))
    grad_hidden_one, grad_low, gain_two_sum = backward_norm(
        two_terms, *sides, hidden_one, cotangent, gain_two, chips, count
    )
    attn_steps = line_steps(after(grad_low, turn(sides)), turn=turn)
    grad_attn = line_pieces(grad_low, attn_steps)
    grad_attn = after(grad_attn, turn(attn_steps[-1]))
    down_sum = jnp.concatenate(sums_of["down"], axis=0)
    pair_sum = jnp.concatenate(
        [jnp.concatenate(sums_of[name], axis=0) for name in ("gate", "up")], axis=1
    ).reshape(count, part, 2 * ff_own)
    ring = exchange_line(lambda j: lax.dynamic_index_in_dim(pair_sum, j, keepdims=False))
    down_all = lax.all_gather(down_sum, PLANE, axis=0)

    grad_attn = jnp.concatenate(grad_attn, axis=0)
    grad_att = mm_last(grad_attn, out_weight).astype(BF)
    grad_att = grad_att.reshape(seq, kv_heads, groups, hd)
    grad_probs = jnp.einsum("tngd,snd->ngts", grad_att, values, preferred_element_type=F32)
    delta = jnp.sum(probs * grad_probs, axis=-1, keepdims=True)
    grad_scores = (probs * (grad_probs - delta)).astype(BF)
    ffn_sum = absolute(after(ring, grad_scores)).reshape(count * part, 2 * ff_own)
    ffn_all = lax.all_gather(ffn_sum, PLANE, axis=0)
    grad_scores = after(grad_scores, ffn_sum)
    grad_q = jnp.einsum("ngts,snd->tngd", grad_scores, keys, preferred_element_type=F32) * scale
    grad_k = jnp.einsum("ngts,tngd->snd", grad_scores, grouped, preferred_element_type=F32) * scale
    grad_v = jnp.einsum("ngts,tngd->snd", probs_low, grad_att, preferred_element_type=F32)
    grad_q_unit = apply_rotary(grad_q.reshape(seq, q_heads, hd), cosine, -sine)
    grad_k_unit = apply_rotary(grad_k, cosine, -sine)
    query_gain_sum = jnp.sum(grad_q_unit * q_unit, axis=(0, 1))
    key_gain_sum = jnp.sum(grad_k_unit * k_unit, axis=(0, 1))
    grad_proj = jnp.concatenate(
        [
            unit_back(grad_q_unit * gain_query, q_unit, q_inv).astype(BF).reshape(seq, q_cols),
            unit_back(grad_k_unit * gain_key, k_unit, k_inv).astype(BF).reshape(seq, kv_cols),
            grad_v.astype(BF).reshape(seq, kv_cols),
        ],
        axis=1,
    )
    grad_proj = after(grad_proj, down_all)
    one_part = mm_last(grad_proj, proj).reshape(count, tok, width)
    proj_part = mm_first(normed_one, after(grad_proj, one_part)).astype(BF)
    out_term = mm_first(attended, grad_attn).astype(BF)
    att_part = jnp.concatenate(
        [proj_part[j * rows : (j + 1) * rows] for j in range(count)] + [out_term], axis=1
    ).reshape(chips, 2, share, -1)

    def cores(t, sides):
        if t == 1:
            stage["att"] = chip_halves(halve(att_part, 1, "core", 0, sides))
            return stage["att"]
        if t == 2:
            stage["att"] = chip_stage(stage["att"], 0, sides)
            return stage["att"]
        return ()

    sides = line_scatter(one_part, cores)
    att_sum = chip_rest(stage["att"], 1, sides)
    _, input_grad, gain_one_sum = backward_norm(
        one_part, *sides, inputs, grad_hidden_one, gain_one, 0, count
    )

    down_grad = place_down(down_all, chips, ff_own // chips, width)
    late = after(hidden, att_sum)
    other = mm(late[seq:], down_own).astype(BF)
    att_sum = jnp.concatenate(att_sum, axis=0)
    cols = q_cols + 2 * kv_cols
    ring = exchange_line(lambda j: lax.dynamic_slice(att_sum, (0, j * cols), (share, cols)))
    out_terms = mm(late[:seq], down_own) + swap_cores(other).astype(F32)
    out_terms = out_terms.reshape(count, tok, width)
    got = absolute(after(ring, out_terms))
    cuts = ((0, q_cols), (q_cols, q_cols + kv_cols), (q_cols + kv_cols, cols))
    att_sum = jnp.concatenate(
        [got[j, :, a:b] for a, b in cuts for j in range(count)] + [att_sum[:, count * cols :]],
        axis=1,
    )
    att_sum = after(att_sum, ffn_all)
    gate_grad, up_grad = place_pair(ffn_all, chips, count, part, ff_own)

    def casts(t, sides):
        return (down_grad,) if t == 1 else (gate_grad, up_grad)

    sides = line_scatter(after(out_terms, att_sum), casts)
    output = (
        hidden_one + out_terms[0] + sides[0].astype(F32) + sides[1].astype(F32)
    ).astype(BF)

    att_all = lax.all_gather(att_sum, PLANE, axis=0, tiled=True)
    edges = [0, q_cols * count, (q_cols + kv_cols) * count, cols * count, att_all.shape[1]]
    query_grad, key_grad, value_grad, out_grad = (
        att_all[:, a:b].astype(F32) for a, b in zip(edges[:-1], edges[1:])
    )

    sums = sum_small(
        jnp.concatenate(
            [
                v.reshape(count, -1)
                for v in (gain_one_sum, gain_two_sum, query_gain_sum, key_gain_sum)
            ],
            axis=1,
        )
    )
    return (
        output,
        input_grad,
        sums[:rows],
        query_grad,
        key_grad,
        value_grad,
        sums[2 * rows : 2 * rows + small],
        sums[2 * rows + small :],
        out_grad,
        sums[rows : 2 * rows],
        gate_grad,
        up_grad,
        down_grad,
    )


def solution(mesh):
    chips, count = mesh.shape["rep"] // 2, mesh.shape["fsdp"]
    split = Mesh(mesh.devices.reshape(chips, 2, count), ("chip", "core", "fsdp"))
    tokens, reps, fsdp = (*PLANE, "fsdp"), PLANE, "fsdp"
    in_specs = (
        P(tokens, None),
        P(reps, None),
        P(fsdp),
        P(fsdp, None),
        P(fsdp, None),
        P(fsdp, None),
        P(fsdp),
        P(fsdp),
        P(fsdp, None),
        P(fsdp),
        P(fsdp, None),
        P(fsdp, None),
        P(fsdp, None),
        P(tokens, None),
    )
    out_specs = (
        P(tokens, None),
        P(tokens, None),
        P(fsdp),
        P(fsdp, None),
        P(fsdp, None),
        P(fsdp, None),
        P(fsdp),
        P(fsdp),
        P(fsdp, None),
        P(fsdp),
        P(fsdp, None),
        P(fsdp, None),
        P(fsdp, None),
    )
    return jax.shard_map(
        shards, mesh=split, in_specs=in_specs, out_specs=out_specs, check_vma=False
    )
```

```python
import functools

import jax
import jax.numpy as jnp
from jax import lax
from jax.experimental import pallas as pl
from jax.experimental.pallas import tpu as pltpu
from jax.sharding import Mesh, PartitionSpec as P

HEAD_SIZE = 64
EPSILON = 1e-05
THETA_BASE = 1000000.0
NEG_FILL = -1e30
LOG2E = 1.4426950408889634
BF = jnp.bfloat16
F32 = jnp.float32
PLANE = ("chip", "core")


def mm(a, b):
    return jnp.dot(a, b, preferred_element_type=F32)


def mm_last(a, b):
    return lax.dot_general(a, b, (((1,), (1,)), ((), ())), preferred_element_type=F32)


def mm_first(a, b):
    return lax.dot_general(a, b, (((0,), (0,)), ((), ())), preferred_element_type=F32)


def swap_cores(a):
    return lax.ppermute(a, "core", [(0, 1), (1, 0)])


def exchanges():
    count = lax.axis_size("fsdp")
    even = [(i, i ^ 1) for i in range(count)]
    odd = [(0, 0)] + [(i, ((i - 1) ^ 1) + 1) for i in range(1, count - 1)] + [(count - 1, count - 1)]
    return even, odd


def line_step(first, second):
    even, odd = exchanges()
    return lax.ppermute(first, "fsdp", even), lax.ppermute(second, "fsdp", odd)


def line_steps(own, ahead_of={}, begun=None, turn=None):
    steps = []
    first, second = own, own
    for t in range(lax.axis_size("fsdp") - 1):
        if t in ahead_of:
            first, second = after((first, second), ahead_of[t])
        if t and turn:
            first, second = after((first, second), turn((first, second)))
        if t == 0 and begun:
            by_even, by_odd = begun
        else:
            by_even, by_odd = line_step(first, second)
        steps.append((by_even, by_odd))
        first, second = by_odd, by_even
    return steps


def line_pieces(own, steps):
    count = lax.axis_size("fsdp")
    mine = lax.axis_index("fsdp")
    is_even = mine % 2 == 0
    pieces = [own]
    for d in range(1, count):
        below, above = steps[d - 1], steps[count - d - 1]
        from_below = jnp.where(is_even, below[1], below[0])
        from_above = jnp.where(is_even, above[0], above[1])
        pieces.append(jnp.where(mine >= d, from_below, from_above))
    return jnp.concatenate(pieces, axis=0)


def line_scatter(parts, ahead_of=None):
    count = lax.axis_size("fsdp")
    mine = lax.axis_index("fsdp")
    is_even = mine % 2 == 0
    is_end = (mine == 0) | (mine == count - 1)
    by_even = by_odd = None
    for t in range(count - 1):
        up = jnp.where(is_even, t + 1, count - 1 - t)
        first = lax.dynamic_index_in_dim(parts, up, keepdims=False)
        second = lax.dynamic_index_in_dim(parts, count - up, keepdims=False)
        if t:
            if ahead_of:
                by_even, by_odd = after((by_even, by_odd), ahead_of(t, (by_even, by_odd)))
            first, second = first + by_odd.astype(F32), second + by_even.astype(F32)
        second = jnp.where(is_end, 0.0, second)
        by_even, by_odd = line_step(first.astype(BF), second.astype(BF))
    return by_even, by_odd


def absolute(ring):
    count = len(ring)
    mine = lax.axis_index("fsdp")
    out = jnp.zeros((count, *ring[0].shape), ring[0].dtype)
    for e, piece in enumerate(ring):
        out = lax.dynamic_update_index_in_dim(out, piece, (mine + e) % count, 0)
    return out


def exchange_line(piece_for):
    count = lax.axis_size("fsdp")
    mine = lax.axis_index("fsdp")
    return [piece_for(mine)] + [
        lax.ppermute(
            piece_for((mine - e) % count),
            "fsdp",
            [(i, (i - e) % count) for i in range(count)],
        )
        for e in range(1, count)
    ]


def add_low(a, b):
    return (a.astype(F32) + b.astype(F32)).astype(BF)


def halve(blocks, axis, name, bit, pin=()):
    mybit = (lax.axis_index(name) >> bit) & 1
    pairs = [(i, i ^ (1 << bit)) for i in range(lax.axis_size(name))]
    got = lax.ppermute(
        lax.dynamic_index_in_dim(blocks, 1 - mybit, axis, keepdims=False), name, pairs
    )
    got = after(got, pin)
    return add_low(lax.dynamic_index_in_dim(blocks, mybit, axis, keepdims=False), got)


def chip_halves(terms):
    chips, rows, cols = terms.shape
    bits = chips.bit_length() - 1
    return [
        terms[:, g * rows // 2 : (g + 1) * rows // 2].reshape([2] * bits + [rows // 2, cols])
        for g in range(2)
    ]


def chip_stage(halves, step, pin=(), lead=(0, 0)):
    bits = lax.axis_size("chip").bit_length() - 1
    out = []
    for g in range(2):
        done = [(g + k) % bits for k in range(step)]
        left = [b for b in range(bits - 1, -1, -1) if b not in done]
        bit = (g + step) % bits
        out.append(halve(halves[g], lead[g] + left.index(bit), "chip", bit, pin))
    return out


def chip_rest(halves, step, pin=(), lead=(0, 0)):
    for k in range(step, lax.axis_size("chip").bit_length() - 1):
        halves = chip_stage(halves, k, pin, lead)
    return halves


def after(value, *others):
    return lax.optimization_barrier((value, *others))[0]


def gather_small(own):
    return absolute(exchange_line(lambda j: own))


def small_line(rows, pin):
    count = lax.axis_size("fsdp")
    mine = lax.axis_index("fsdp")
    got = [
        lax.ppermute(
            lax.dynamic_index_in_dim(rows, (mine + d) % count, keepdims=False),
            "fsdp",
            [(i, (i + d) % count) for i in range(count)],
        )
        for d in range(1, count)
    ]
    return sum(after(got, pin), lax.dynamic_index_in_dim(rows, mine, keepdims=False))


def small_chips(total, pin):
    chips = lax.axis_size("chip")
    got = [
        lax.ppermute(total, "chip", [(i, i ^ d) for i in range(chips)]) for d in range(1, chips)
    ]
    return sum(after(got, pin), total)


def split_mean(values, block):
    high = values.astype(BF)
    low = (values - high.astype(F32)).astype(BF)
    return mm(high, block) + mm(low, block)


def swap_pairs(values):
    lane = lax.broadcasted_iota(jnp.int32, values.shape, 1)
    half = HEAD_SIZE // 2
    lanes = values.shape[1]
    return jnp.where(
        lane % HEAD_SIZE < half,
        pltpu.roll(values, lanes - half, 1),
        pltpu.roll(values, half, 1),
    )


def head_unit(pre, block):
    inverse = lax.rsqrt(split_mean(pre * pre, block) + EPSILON)
    return pre * inverse, inverse


def turn_heads(values, cosine, sine):
    return values * cosine + swap_pairs(values) * sine


def turn_back(values, cosine, sine):
    return values * cosine - swap_pairs(values) * sine


def head_grad(grad, unit, inverse, gain, block):
    scaled = grad * gain
    return inverse * (scaled - unit * split_mean(scaled * unit, block))


def spread(values, source, seq, rows):
    lanes = values.shape[1]
    a = lax.broadcasted_iota(jnp.int32, (lanes, 2 * HEAD_SIZE), 0)
    b = lax.broadcasted_iota(jnp.int32, (lanes, 2 * HEAD_SIZE), 1)
    for side in range(2):
        move = (a - source * HEAD_SIZE == b - side * HEAD_SIZE) & (b // HEAD_SIZE == side)
        rows[side * seq : (side + 1) * seq, :] = mm(values, move.astype(BF)).astype(BF)


def load_heads(keys, vals, cosine, sine, key_gain, block, kv, keys_at, vals_at):
    seq = keys.shape[0]
    unit, _ = head_unit(keys[...], block[...])
    turned = turn_heads(unit * key_gain[...], cosine[...], sine[...]).astype(BF)
    low = vals[...].astype(BF)
    for n in range(kv):
        spread(turned, n, seq, keys_at.at[n])
        spread(low, n if kv == 2 else 1, seq, vals_at.at[n])


def attend_kernel(
    kv, each, scale, pre, keys, vals, bias, cosine, sine, cos_own, sin_own, query_gain, key_gain,
    block, out, inverse, keys_at, vals_at,
):
    j, i = pl.program_id(0), pl.program_id(1)
    seq = keys.shape[0]

    @pl.when((j == 0) & (i == 0))
    def _():
        load_heads(keys, vals, cosine, sine, key_gain, block, kv, keys_at, vals_at)

    unit, _ = head_unit(pre[...], block[...])
    query = turn_heads(unit * query_gain[...], cos_own[...], sin_own[...]).astype(BF)
    head = j // each
    scores = mm_last(query, keys_at[head]) * (scale * LOG2E)
    side = lax.broadcasted_iota(jnp.int32, (2 * seq, 2 * HEAD_SIZE), 0) // seq
    lane = lax.broadcasted_iota(jnp.int32, (2 * seq, 2 * HEAD_SIZE), 1) // HEAD_SIZE
    ones = (side == lane).astype(BF)
    allowed = bias[...]
    expo = jnp.exp2(
        jnp.concatenate([scores[:, :seq] + allowed, scores[:, seq:] + allowed], axis=1)
    ).astype(BF)
    inv = 1.0 / mm(expo, ones)
    out[...] = (mm(expo, vals_at[head]) * inv).astype(BF)
    inverse[...] = inv


def attend_back_kernel(
    kv, each, scale, pre, keys, vals, bias, cosine, sine, cos_own, sin_own, query_gain, key_gain,
    block, out, inverse, grad, grad_proj, query_sum, key_sum, keys_at, vals_at, key_acc, val_acc,
):
    j, i = pl.program_id(0), pl.program_id(1)
    seq = keys.shape[0]
    rows = pre.shape[0]
    two = 2 * HEAD_SIZE

    @pl.when((j == 0) & (i == 0))
    def _():
        load_heads(keys, vals, cosine, sine, key_gain, block, kv, keys_at, vals_at)
        key_acc[...] = jnp.zeros_like(key_acc)
        val_acc[...] = jnp.zeros_like(val_acc)
        query_sum[...] = jnp.zeros_like(query_sum)

    unit, inv_unit = head_unit(pre[...], block[...])
    query = turn_heads(unit * query_gain[...], cos_own[...], sin_own[...]).astype(BF)
    head = j // each
    keys_of, vals_of = keys_at[head], vals_at[head]
    scores = mm_last(query, keys_of) * (scale * LOG2E)
    low = grad[...]
    gprobs = mm_last(low, vals_of)
    product = low.astype(F32) * out[...].astype(F32)
    delta = split_mean(product, block[...]) * HEAD_SIZE
    inv = inverse[...]
    allowed = bias[...]
    probs, gscores = [], []
    for side in range(2):
        part = slice(side * seq, (side + 1) * seq)
        at = side * HEAD_SIZE
        p = jnp.exp2(scores[:, part] + allowed) * inv[:, at : at + 1]
        probs.append(p.astype(BF))
        gscores.append((p * (gprobs[:, part] - delta[:, at : at + 1])).astype(BF))
    probs = jnp.concatenate(probs, axis=1)
    gscores = jnp.concatenate(gscores, axis=1)
    key_acc[head] += mm_first(gscores, query)
    val_acc[head] += mm_first(probs, low)
    back = turn_back(mm(gscores, keys_of) * scale, cos_own[...], sin_own[...])
    query_sum[...] += jnp.sum(back * unit, axis=0, keepdims=True)
    grad_proj[pl.ds(pl.multiple_of(i * rows, rows), rows), pl.ds(pl.multiple_of(j * two, two), two)] = (
        head_grad(back, unit, inv_unit, query_gain[...], block[...]).astype(BF)
    )

    @pl.when((j == pl.num_programs(0) - 1) & (i == pl.num_programs(1) - 1))
    def _():
        lane = lax.broadcasted_iota(jnp.int32, (seq, two), 1)

        def fold(acc, n):
            both = jnp.where(lane < HEAD_SIZE, acc[n, :seq, :], acc[n, seq:, :])
            return both + pltpu.roll(both, HEAD_SIZE, 1)

        key_tile = fold(key_acc, 0) * scale
        val_tile = fold(val_acc, 0)
        if kv == 2:
            key_tile = jnp.where(lane < HEAD_SIZE, key_tile, fold(key_acc, 1) * scale)
            val_tile = jnp.where(lane < HEAD_SIZE, val_tile, fold(val_acc, 1))
        unit_k, inv_k = head_unit(keys[...], block[...])
        back_k = turn_back(key_tile, cosine[...], sine[...])
        key_sum[...] = jnp.sum(back_k * unit_k, axis=0, keepdims=True)
        key_low = head_grad(back_k, unit_k, inv_k, key_gain[...], block[...])
        start = grad_proj.shape[1] - kv * two
        if kv == 2:
            grad_proj[:, start : start + two] = key_low.astype(BF)
            grad_proj[:, start + two :] = val_tile.astype(BF)
        else:
            grad_proj[:, start:] = jnp.where(lane < HEAD_SIZE, key_low, val_tile).astype(BF)


def attention_call(pre, bias, cosine, sine, query_gain, key_gain, kv, more=None):
    seq, cols = pre.shape
    two = 2 * HEAD_SIZE
    q_cols = cols - kv * two
    tiles = q_cols // two
    each = tiles // kv
    rows = min(256, seq)
    lane = jnp.arange(two) // HEAD_SIZE
    block = jnp.where(lane[:, None] == lane[None, :], 1.0 / HEAD_SIZE, 0.0).astype(BF)
    own = pl.BlockSpec((rows, two), lambda j, i: (i, j))
    here = pl.BlockSpec((rows, two), lambda j, i: (i, 0))
    whole = pl.BlockSpec((seq, two), lambda j, i: (0, 0))
    row = pl.BlockSpec((1, two), lambda j, i: (0, 0))
    key_tile = pl.BlockSpec((seq, two), lambda j, i: (0, tiles))
    val_tile = pl.BlockSpec((seq, two), lambda j, i: (0, tiles + kv - 1))
    in_specs = [
        own, key_tile, val_tile, pl.BlockSpec((rows, seq), lambda j, i: (i, 0)), whole, whole,
        here, here, row, row, pl.BlockSpec((two, two), lambda j, i: (0, 0)),
    ]
    twice = [jnp.concatenate([g, g]).reshape(1, two) for g in (query_gain, key_gain)]
    args = [pre, pre, pre, bias, cosine, sine, cosine, sine, *twice, block]
    heads = pltpu.VMEM((kv, 2 * seq, two), BF)
    params = pltpu.CompilerParams(vmem_limit_bytes=48 * 2**20)
    grid = (tiles, seq // rows)
    scale = HEAD_SIZE ** (-0.5)
    if more is None:
        return pl.pallas_call(
            functools.partial(attend_kernel, kv, each, scale),
            grid=grid,
            in_specs=in_specs,
            out_specs=[own, own],
            out_shape=[
                jax.ShapeDtypeStruct((seq, q_cols), BF),
                jax.ShapeDtypeStruct((seq, q_cols), F32),
            ],
            scratch_shapes=[heads, heads],
            compiler_params=params,
        )(*args)
    sums = pltpu.VMEM((kv, 2 * seq, two), F32)
    return pl.pallas_call(
        functools.partial(attend_back_kernel, kv, each, scale),
        grid=grid,
        in_specs=in_specs + [own, own, own],
        out_specs=[pl.BlockSpec((seq, cols), lambda j, i: (0, 0)), row, row],
        out_shape=[
            jax.ShapeDtypeStruct((seq, cols), BF),
            jax.ShapeDtypeStruct((1, two), F32),
            jax.ShapeDtypeStruct((1, two), F32),
        ],
        scratch_shapes=[heads, heads, sums, sums],
        compiler_params=params,
    )(*args, *more)


def pair_tables(positions):
    half = HEAD_SIZE // 2
    inverse = THETA_BASE ** (-(jnp.arange(half, dtype=F32) * 2.0) / HEAD_SIZE)
    angles = positions.astype(F32)[:, None] * inverse[None, :]
    cosine, sine = jnp.cos(angles), jnp.sin(angles)
    return jnp.tile(cosine, (1, 4)), jnp.concatenate([-sine, sine, -sine, sine], axis=1)


def lanes(width, chips, count):
    part = width // chips // count
    return [
        (slice((z * chips + c) * part, (z * chips + c + 1) * part),
         slice((c * count + z) * part, (c * count + z + 1) * part))
        for z in range(count)
        for c in range(chips)
    ]


def inverse_root(wide):
    return lax.rsqrt(jnp.mean(wide * wide, axis=-1, keepdims=True) + EPSILON)


def norm_forward(chips, count, own, part, right, left, gain, hidden, normed):
    wide = own[...].astype(F32) + part[0] + right[...].astype(F32) + left[...].astype(F32)
    hidden[...] = wide
    low = (wide * inverse_root(wide) * gain[...]).astype(BF)
    for here, there in lanes(wide.shape[1], chips, count):
        normed[:, there] = low[:, here]


def norm_backward(chips, count, part, right, left, wide, base, gain, grad, low, total, scratch):
    summed = part[0] + right[...].astype(F32) + left[...].astype(F32)
    if chips:
        for here, there in lanes(summed.shape[1], chips, count):
            scratch[:, here] = summed[:, there]
        summed = scratch[...]
    values = wide[...].astype(F32)
    inverse = inverse_root(values)
    unit = values * inverse
    sums = jnp.sum(summed * unit, axis=0, keepdims=True)

    @pl.when(pl.program_id(0) == 0)
    def _():
        total[...] = sums

    @pl.when(pl.program_id(0) > 0)
    def _():
        total[...] += sums

    scaled = summed * gain[...]
    out = base[...].astype(F32) + inverse * (
        scaled - unit * jnp.mean(scaled * unit, axis=-1, keepdims=True)
    )
    grad[...] = out
    low[...] = out.astype(BF)


def row_specs(tok, width):
    step = min(32, tok)
    block = pl.BlockSpec((step, width), lambda i: (i, 0))
    first = pl.BlockSpec((1, step, width), lambda i: (0, i, 0))
    row = pl.BlockSpec((1, width), lambda i: (0, 0))
    return tok // step, step, block, first, row


def forward_norm(own, parts, right, left, gain, chips, count):
    tok, width = own.shape
    grid, _, block, first, row = row_specs(tok, width)
    return pl.pallas_call(
        functools.partial(norm_forward, chips, count),
        grid=(grid,),
        in_specs=[block, first, block, block, row],
        out_specs=[block, block],
        out_shape=[
            jax.ShapeDtypeStruct((tok, width), F32),
            jax.ShapeDtypeStruct((tok, width), BF),
        ],
    )(own, parts, right, left, gain.reshape(1, width))


def backward_norm(parts, right, left, wide, base, gain, chips, count):
    tok, width = wide.shape
    grid, step, block, first, row = row_specs(tok, width)
    return pl.pallas_call(
        functools.partial(norm_backward, chips, count),
        grid=(grid,),
        in_specs=[first, block, block, block, block, row],
        out_specs=[block, block, row],
        out_shape=[
            jax.ShapeDtypeStruct((tok, width), F32),
            jax.ShapeDtypeStruct((tok, width), BF),
            jax.ShapeDtypeStruct((1, width), F32),
        ],
        scratch_shapes=[pltpu.VMEM((step, width), F32)],
    )(parts, right, left, wide, base, gain.reshape(1, width))


def cast_pair(own, out):
    _, cores, count, _, _ = own.shape
    half = out.shape[1] // cores // count
    for j in range(count):
        for k in range(cores):
            at = (j * cores + k) * half
            out[:, at : at + half] = own[0, k, j].astype(F32)


def place_pair(own, which, chips, count, part, half):
    step = min(64, part)
    own = own.reshape(chips, 2, count, part, 2 * half)
    cols = count * 2 * half
    return pl.pallas_call(
        cast_pair,
        grid=(chips, part // step),
        in_specs=[pl.BlockSpec((1, 2, count, step, half), lambda c, r: (c, 0, 0, r, which))],
        out_specs=pl.BlockSpec((step, cols), lambda c, r: (c * (part // step) + r, 0)),
        out_shape=jax.ShapeDtypeStruct((chips * part, cols), F32),
    )(own)


def cast_columns(_, one, two, *outs):
    half = pl.num_programs(0) // 2
    for own, mine in ((one, pl.program_id(0) < half), (two, pl.program_id(0) >= half)):

        @pl.when(mine)
        def _(own=own):
            at = 0
            for out in outs:
                out[...] = own[:, at : at + out.shape[1]].astype(F32)
                at += out.shape[1]


def place_columns(order, one, two, widths):
    blocks = order.shape[0]
    rows, cols = one.shape
    half = blocks // 2
    step = rows // half
    return pl.pallas_call(
        cast_columns,
        grid_spec=pltpu.PrefetchScalarGridSpec(
            num_scalar_prefetch=1,
            grid=(blocks,),
            in_specs=[
                pl.BlockSpec((step, cols), lambda r, order: (jnp.minimum(r, half - 1), 0)),
                pl.BlockSpec((step, cols), lambda r, order: (jnp.maximum(r - half, 0), 0)),
            ],
            out_specs=[pl.BlockSpec((step, w), lambda r, order: (order[r], 0)) for w in widths],
        ),
        out_shape=[jax.ShapeDtypeStruct((2 * rows, w), F32) for w in widths],
    )(order, one, two)


def gather_stage(halves, step, pin=()):
    chips = lax.axis_size("chip")
    bits = chips.bit_length() - 1
    out = []
    for g, half in enumerate(halves):
        bit = (g + step) % bits
        got = lax.ppermute(half, "chip", [(i, i ^ (1 << bit)) for i in range(chips)])
        out.append(jnp.concatenate([half, after(got, pin)], axis=0))
    return out


def gathered_order(g):
    chips = lax.axis_size("chip")
    bits = chips.bit_length() - 1
    chip, core = lax.axis_index("chip"), lax.axis_index("core")
    away = [0]
    for step in range(bits):
        away += [a ^ (1 << ((g + step) % bits)) for a in away]
    places = [(chip ^ a) * 2 + (core ^ k) for k in range(2) for a in away]
    return jnp.stack(places).astype(jnp.int32)


def cast_down(own, out):
    out[...] = own[0].astype(F32)


def place_down(own, chips, part, width):
    return pl.pallas_call(
        cast_down,
        grid=(2, chips),
        in_specs=[pl.BlockSpec((1, part, width), lambda k, c: (c * 2 + k, 0, 0))],
        out_specs=pl.BlockSpec((part, width), lambda k, c: (k * chips + c, 0)),
        out_shape=jax.ShapeDtypeStruct((2 * chips * part, width), F32),
    )(own)


def shards(
    inputs,
    doc_lengths,
    attn_gain,
    query_weight,
    key_projection,
    value_projection,
    query_gain,
    key_norm_gain,
    out_weight,
    ffn_gain,
    gate_weight,
    up_weight,
    down_weight,
    cotangent,
):
    tok, width = inputs.shape
    count = lax.axis_size("fsdp")
    chips = lax.axis_size("chip")
    rep = chips * 2
    mine = lax.axis_index("fsdp")
    chip = lax.axis_index("chip")
    core = lax.axis_index("core")
    seq = tok * count
    hd = HEAD_SIZE
    rows = query_weight.shape[0]
    q_cols = query_weight.shape[1] // count
    kv_cols = key_projection.shape[1] // count
    ff = gate_weight.shape[1]
    ff_own = ff // count // 2

    share = rows // rep
    at = (chip * 2 + core) * share

    def proj_piece(j):
        return jnp.concatenate(
            [
                lax.dynamic_slice(w, (at, j * wide), (share, wide))
                for w, wide in (
                    (query_weight, q_cols),
                    (key_projection, kv_cols),
                    (value_projection, kv_cols),
                )
            ],
            axis=1,
        )

    proj_ring = exchange_line(proj_piece)
    begun = line_step(inputs, inputs)
    proj_own = absolute(after(proj_ring, begun))
    x_steps = line_steps(inputs, {2: proj_own}, begun)
    x_all = line_pieces(inputs, x_steps)
    proj = lax.all_gather(proj_own, PLANE, axis=0)
    proj = proj.transpose(1, 0, 2, 3).reshape(width, q_cols + 2 * kv_cols)

    gains = jnp.concatenate([attn_gain, ffn_gain, query_gain, key_norm_gain])
    gains = gather_small(after(gains, x_steps[0]))
    gains = gains.astype(F32)
    gain_one = gains[:, :rows].reshape(-1)
    gain_two = gains[:, rows : 2 * rows].reshape(-1)
    small = hd // count
    gain_query = gains[:, 2 * rows : 2 * rows + small].reshape(-1)
    gain_key = gains[:, 2 * rows + small :].reshape(-1)

    part = rows // chips
    gate_up = after((gate_weight, up_weight), x_steps[-1])

    def pair_piece(j):
        return jnp.concatenate(
            [
                lax.dynamic_slice(w, (chip * part, (j * 2 + core) * ff_own), (part, ff_own))
                for w in gate_up
            ],
            axis=1,
        )

    pair_ring = exchange_line(pair_piece)

    order = (mine - jnp.arange(count, dtype=jnp.int32)) % count
    positions = (order[:, None] * tok + jnp.arange(tok, dtype=jnp.int32)[None, :]).reshape(-1)
    lengths = after(doc_lengths, x_steps[1])[0]
    docs = lengths.shape[0]
    upto = jnp.arange(docs)[None, :] <= jnp.arange(docs)[:, None]
    ends = jnp.sum(jnp.where(upto, lengths[None, :], 0), axis=1)
    segment = jnp.sum((positions[:, None] >= ends[None, :]).astype(jnp.int32), axis=1)
    allowed = (segment[:, None] == segment[None, :]) & (positions[None, :] <= positions[:, None])
    bias = jnp.where(allowed, 0.0, NEG_FILL).astype(F32)
    tables = pair_tables(positions)

    wide = x_all.astype(F32)
    normed_one = (wide * inverse_root(wide) * gain_one).astype(BF)
    kv_heads = kv_cols // hd
    core_args = (mm(normed_one, proj), bias, *tables, gain_query, gain_key, kv_heads)
    attended, inverse_sums = attention_call(*core_args)
    out_part = mm(attended, out_weight).reshape(count, tok, width)
    stage = {}

    def slices(t, sides):
        if t == 1:
            stage["slices"] = absolute(after(pair_ring, sides))
            return stage["slices"]
        return ()

    sides = line_scatter(out_part, slices)
    pair = lax.all_gather(stage["slices"], "chip", axis=0)
    pair = pair.reshape(width, 2 * ff_own)
    hidden_one, normed_own = forward_norm(inputs, out_part, *sides, gain_two, chips, count)

    cot_begun = line_step(*(after(cotangent, sides),) * 2)
    two_steps = line_steps(after(normed_own, cot_begun))
    normed_two = line_pieces(normed_own, two_steps)
    normed_two = jnp.concatenate([normed_two, swap_cores(normed_two)], axis=0)
    down_own = lax.dynamic_slice_in_dim(down_weight, core * ff_own, ff_own)
    both = mm(normed_two, pair)
    cot_steps = line_steps(cotangent, {1: two_steps[-1], count - 2: both}, cot_begun)
    cot_own = line_pieces(cotangent, cot_steps)
    cot_all = jnp.concatenate([cot_own, swap_cores(cot_own)], axis=0)
    grad_hidden = mm_last(cot_all, down_own)
    gate_pre, upward = both[:, :ff_own], both[:, ff_own:]
    sigmoid = jax.nn.sigmoid(gate_pre)
    silu = gate_pre * sigmoid
    hidden = (silu * upward).astype(BF)
    grad_gate = (grad_hidden * upward * sigmoid * (1.0 + gate_pre * (1.0 - sigmoid))).astype(BF)
    grad_up = (grad_hidden * silu).astype(BF)
    grad_both = jnp.concatenate([grad_gate, grad_up], axis=1)

    down_part = mm_first(hidden, cot_all).astype(BF)
    down_sum = lax.psum_scatter(down_part, "chip", scatter_dimension=0, tiled=True)
    out_other = mm(after(hidden[seq:], down_part), down_own).astype(BF)
    other = mm_last(after(grad_both[seq:], out_other), pair).astype(BF)
    out_terms = mm(after(hidden[:seq], other), down_own) + swap_cores(out_other).astype(F32)
    out_terms = out_terms.reshape(count, tok, width)
    pair_part = mm_first(normed_two, after(grad_both, out_terms)).astype(BF)
    pair_sum = lax.psum_scatter(pair_part, "chip", scatter_dimension=0, tiled=True)
    own = after(grad_both[:seq], pair_part)
    two_terms = mm_last(own, pair) + swap_cores(other).astype(F32)
    two_terms = two_terms.reshape(count, tok, width)
    sides = line_scatter(out_terms, lambda t, _: pair_part if t == 1 else two_terms)
    output = (
        hidden_one + out_terms[0] + sides[0].astype(F32) + sides[1].astype(F32)
    ).astype(BF)
    sides = line_scatter(two_terms)
    grad_hidden_one, grad_low, gain_two_sum = backward_norm(
        two_terms, *sides, hidden_one, cotangent, gain_two, chips, count
    )
    grad_attn = line_pieces(grad_low, line_steps(grad_low))

    grad_att = mm_last(grad_attn, out_weight).astype(BF)
    out_term = mm_first(attended, grad_attn).astype(BF)
    grad_att = after(grad_att, out_term)
    down_all = lax.all_gather(after(down_sum, grad_att), PLANE, axis=0)
    pair_sum = after(pair_sum, grad_att)
    rings = [
        exchange_line(
            lambda j, w=w: lax.dynamic_slice(pair_sum, (j * part, w * ff_own), (part, ff_own))
        )
        for w in range(2)
    ]
    grad_proj, query_sum, key_sum = attention_call(
        *core_args, more=(attended, inverse_sums, grad_att)
    )
    query_gain_sum = query_sum[0, :hd] + query_sum[0, hd:]
    key_gain_sum = key_sum[0, :hd] + (key_sum[0, hd:] if kv_heads == 2 else 0.0)
    proj_part = mm_first(normed_one, grad_proj).astype(BF)
    one_part = mm_last(after(grad_proj, proj_part), proj).reshape(count, tok, width)
    bits = chips.bit_length() - 1
    cols = q_cols + 2 * kv_cols
    att_terms = [proj_part.reshape(count, chips, 2, share, cols), out_term.reshape(chips, 2, share, -1)]

    def att_cores(pin):
        out = [halve(x, 2 - g, "core", 0, pin) for g, x in enumerate(att_terms)]
        return [
            out[0].reshape([count] + [2] * bits + [share, cols]),
            out[1].reshape([2] * bits + [share, width]),
        ]

    att_sum = att_cores(one_part)
    ffn_sum = jnp.concatenate([absolute(after(ring, att_sum)) for ring in rings], axis=2)
    ffn_all = lax.all_gather(ffn_sum.reshape(count * part, 2 * ff_own), PLANE, axis=0)

    def att_stages(t, sides):
        if t > 2:
            return ()
        stage["att"] = chip_stage(stage.get("att", att_sum), t - 1, sides, (1, 0))
        return (stage["att"], down_grad) if t == 2 else stage["att"]

    down_grad = place_down(down_all, chips, ff_own // chips, width)
    sides = line_scatter(after(one_part, ffn_sum), att_stages)
    _, input_grad, gain_one_sum = backward_norm(
        one_part, *sides, inputs, grad_hidden_one, gain_one, 0, count
    )

    sums = jnp.concatenate(
        [
            v.reshape(count, -1)
            for v in (gain_one_sum, gain_two_sum, query_gain_sum, key_gain_sum)
        ],
        axis=1,
    )

    att_sum = chip_rest(stage["att"], 2, sides, (1, 0))
    ring = exchange_line(lambda j: lax.dynamic_index_in_dim(att_sum[0], j, keepdims=False))
    cuts = ((0, q_cols), (q_cols, q_cols + kv_cols), (q_cols + kv_cols, cols))
    got = absolute(after(ring, input_grad))
    columns = [[got[j, :, a:b] for j in range(count)] for a, b in cuts]
    att_all = [
        jnp.concatenate(columns[0] + columns[1], axis=1),
        jnp.concatenate(columns[2] + [att_sum[1]], axis=1),
    ]
    sums = small_line(sums, att_all)
    for step in range(bits):
        att_all = gather_stage(att_all, step, sums)
        if step == 0:
            sums = sums + after(swap_cores(sums), att_all)
    sums = small_chips(sums, att_all)
    gate_grad, up_grad = (place_pair(ffn_all, w, chips, count, part, ff_own) for w in range(2))
    others = after([swap_cores(a) for a in att_all], gate_grad, up_grad)
    query_grad, key_grad = place_columns(
        gathered_order(0), att_all[0], others[0], (q_cols * count, kv_cols * count)
    )
    value_grad, out_grad = place_columns(
        gathered_order(1), att_all[1], others[1], (kv_cols * count, width)
    )
    return (
        output,
        input_grad,
        sums[:rows],
        query_grad,
        key_grad,
        value_grad,
        sums[2 * rows : 2 * rows + small],
        sums[2 * rows + small :],
        out_grad,
        sums[rows : 2 * rows],
        gate_grad,
        up_grad,
        down_grad,
    )


def solution(mesh):
    chips, count = mesh.shape["rep"] // 2, mesh.shape["fsdp"]
    split = Mesh(mesh.devices.reshape(chips, 2, count), ("chip", "core", "fsdp"))
    tokens, reps, fsdp = (*PLANE, "fsdp"), PLANE, "fsdp"
    in_specs = (
        P(tokens, None),
        P(reps, None),
        P(fsdp),
        P(fsdp, None),
        P(fsdp, None),
        P(fsdp, None),
        P(fsdp),
        P(fsdp),
        P(fsdp, None),
        P(fsdp),
        P(fsdp, None),
        P(fsdp, None),
        P(fsdp, None),
        P(tokens, None),
    )
    out_specs = (
        P(tokens, None),
        P(tokens, None),
        P(fsdp),
        P(fsdp, None),
        P(fsdp, None),
        P(fsdp, None),
        P(fsdp),
        P(fsdp),
        P(fsdp, None),
        P(fsdp),
        P(fsdp, None),
        P(fsdp, None),
        P(fsdp, None),
    )
    return jax.shard_map(
        shards, mesh=split, in_specs=in_specs, out_specs=out_specs, check_vma=False
    )
```

```python
import functools

import jax
import jax.numpy as jnp
from jax import lax
from jax.experimental import pallas as pl
from jax.experimental.pallas import tpu as pltpu
from jax.sharding import Mesh, PartitionSpec as P

HEAD_SIZE = 64
EPSILON = 1e-05
THETA_BASE = 1000000.0
NEG_FILL = -1e30
LOG2E = 1.4426950408889634
BF = jnp.bfloat16
F32 = jnp.float32
PLANE = ("chip", "core")


def mm(a, b):
    return jnp.dot(a, b, preferred_element_type=F32)


def mm_last(a, b):
    return lax.dot_general(a, b, (((1,), (1,)), ((), ())), preferred_element_type=F32)


def mm_first(a, b):
    return lax.dot_general(a, b, (((0,), (0,)), ((), ())), preferred_element_type=F32)


def swap_cores(a):
    return lax.ppermute(a, "core", [(0, 1), (1, 0)])


def exchanges():
    count = lax.axis_size("fsdp")
    even = [(i, i ^ 1) for i in range(count)]
    odd = [(0, 0)] + [(i, ((i - 1) ^ 1) + 1) for i in range(1, count - 1)] + [(count - 1, count - 1)]
    return even, odd


def line_step(first, second):
    even, odd = exchanges()
    return lax.ppermute(first, "fsdp", even), lax.ppermute(second, "fsdp", odd)


def line_steps(own, ahead_of={}, begun=None, turn=None):
    steps = []
    first, second = own, own
    for t in range(lax.axis_size("fsdp") - 1):
        if t in ahead_of:
            first, second = after((first, second), ahead_of[t])
        if t and turn:
            first, second = after((first, second), turn((first, second)))
        if t == 0 and begun:
            by_even, by_odd = begun
        else:
            by_even, by_odd = line_step(first, second)
        steps.append((by_even, by_odd))
        first, second = by_odd, by_even
    return steps


def line_pieces(own, steps):
    count = lax.axis_size("fsdp")
    mine = lax.axis_index("fsdp")
    is_even = mine % 2 == 0
    pieces = [own]
    for d in range(1, count):
        below, above = steps[d - 1], steps[count - d - 1]
        from_below = jnp.where(is_even, below[1], below[0])
        from_above = jnp.where(is_even, above[0], above[1])
        pieces.append(jnp.where(mine >= d, from_below, from_above))
    return jnp.concatenate(pieces, axis=0)


def line_scatter(parts, ahead_of=None):
    count = lax.axis_size("fsdp")
    mine = lax.axis_index("fsdp")
    is_even = mine % 2 == 0
    is_end = (mine == 0) | (mine == count - 1)
    by_even = by_odd = None
    for t in range(count - 1):
        up = jnp.where(is_even, t + 1, count - 1 - t)
        first = lax.dynamic_index_in_dim(parts, up, keepdims=False)
        second = lax.dynamic_index_in_dim(parts, count - up, keepdims=False)
        if t:
            if ahead_of:
                by_even, by_odd = after((by_even, by_odd), ahead_of(t, (by_even, by_odd)))
            first, second = first + by_odd.astype(F32), second + by_even.astype(F32)
        second = jnp.where(is_end, 0.0, second)
        by_even, by_odd = line_step(first.astype(BF), second.astype(BF))
    return by_even, by_odd


def absolute(ring):
    count = len(ring)
    mine = lax.axis_index("fsdp")
    out = jnp.zeros((count, *ring[0].shape), ring[0].dtype)
    for e, piece in enumerate(ring):
        out = lax.dynamic_update_index_in_dim(out, piece, (mine + e) % count, 0)
    return out


def exchange_line(piece_for):
    count = lax.axis_size("fsdp")
    mine = lax.axis_index("fsdp")
    return [piece_for(mine)] + [
        lax.ppermute(
            piece_for((mine - e) % count),
            "fsdp",
            [(i, (i - e) % count) for i in range(count)],
        )
        for e in range(1, count)
    ]


def add_low(a, b):
    return (a.astype(F32) + b.astype(F32)).astype(BF)


def halve(blocks, axis, name, bit, pin=()):
    mybit = (lax.axis_index(name) >> bit) & 1
    pairs = [(i, i ^ (1 << bit)) for i in range(lax.axis_size(name))]
    got = lax.ppermute(
        lax.dynamic_index_in_dim(blocks, 1 - mybit, axis, keepdims=False), name, pairs
    )
    got = after(got, pin)
    return add_low(lax.dynamic_index_in_dim(blocks, mybit, axis, keepdims=False), got)


def chip_halves(terms):
    chips, rows, cols = terms.shape
    bits = chips.bit_length() - 1
    return [
        terms[:, g * rows // 2 : (g + 1) * rows // 2].reshape([2] * bits + [rows // 2, cols])
        for g in range(2)
    ]


def chip_stage(halves, step, pin=(), lead=(0, 0)):
    bits = lax.axis_size("chip").bit_length() - 1
    out = []
    for g in range(2):
        done = [(g + k) % bits for k in range(step)]
        left = [b for b in range(bits - 1, -1, -1) if b not in done]
        bit = (g + step) % bits
        out.append(halve(halves[g], lead[g] + left.index(bit), "chip", bit, pin))
    return out


def chip_rest(halves, step, pin=(), lead=(0, 0)):
    for k in range(step, lax.axis_size("chip").bit_length() - 1):
        halves = chip_stage(halves, k, pin, lead)
    return halves


def after(value, *others):
    return lax.optimization_barrier((value, *others))[0]


def gather_small(own):
    return absolute(exchange_line(lambda j: own))


def small_line(rows, pin):
    count = lax.axis_size("fsdp")
    mine = lax.axis_index("fsdp")
    got = [
        lax.ppermute(
            lax.dynamic_index_in_dim(rows, (mine + d) % count, keepdims=False),
            "fsdp",
            [(i, (i + d) % count) for i in range(count)],
        )
        for d in range(1, count)
    ]
    return sum(after(got, pin), lax.dynamic_index_in_dim(rows, mine, keepdims=False))


def small_chips(total, pin):
    chips = lax.axis_size("chip")
    got = [
        lax.ppermute(total, "chip", [(i, i ^ d) for i in range(chips)]) for d in range(1, chips)
    ]
    return sum(after(got, pin), total)


def split_mean(values, block):
    high = values.astype(BF)
    low = (values - high.astype(F32)).astype(BF)
    return mm(high, block) + mm(low, block)


def swap_pairs(values):
    lane = lax.broadcasted_iota(jnp.int32, values.shape, 1)
    half = HEAD_SIZE // 2
    lanes = values.shape[1]
    return jnp.where(
        lane % HEAD_SIZE < half,
        pltpu.roll(values, lanes - half, 1),
        pltpu.roll(values, half, 1),
    )


def head_unit(pre, block):
    inverse = lax.rsqrt(split_mean(pre * pre, block) + EPSILON)
    return pre * inverse, inverse


def turn_heads(values, cosine, sine):
    return values * cosine + swap_pairs(values) * sine


def turn_back(values, cosine, sine):
    return values * cosine - swap_pairs(values) * sine


def head_grad(grad, unit, inverse, gain, block):
    scaled = grad * gain
    return inverse * (scaled - unit * split_mean(scaled * unit, block))


def spread(values, source, seq, rows):
    lanes = values.shape[1]
    a = lax.broadcasted_iota(jnp.int32, (lanes, 2 * HEAD_SIZE), 0)
    b = lax.broadcasted_iota(jnp.int32, (lanes, 2 * HEAD_SIZE), 1)
    for side in range(2):
        move = (a - source * HEAD_SIZE == b - side * HEAD_SIZE) & (b // HEAD_SIZE == side)
        rows[side * seq : (side + 1) * seq, :] = mm(values, move.astype(BF)).astype(BF)


def load_heads(keys, vals, cosine, sine, key_gain, block, kv, keys_at, vals_at):
    seq = keys.shape[0]
    unit, _ = head_unit(keys[...], block[...])
    turned = turn_heads(unit * key_gain[...], cosine[...], sine[...]).astype(BF)
    low = vals[...].astype(BF)
    for n in range(kv):
        spread(turned, n, seq, keys_at.at[n])
        spread(low, n if kv == 2 else 1, seq, vals_at.at[n])


def attend_kernel(
    kv, each, scale, pre, keys, vals, bias, cosine, sine, cos_own, sin_own, query_gain, key_gain,
    block, out, inverse, keys_at, vals_at,
):
    j, i = pl.program_id(0), pl.program_id(1)
    seq = keys.shape[0]

    @pl.when((j == 0) & (i == 0))
    def _():
        load_heads(keys, vals, cosine, sine, key_gain, block, kv, keys_at, vals_at)

    unit, _ = head_unit(pre[...], block[...])
    query = turn_heads(unit * query_gain[...], cos_own[...], sin_own[...]).astype(BF)
    head = j // each
    scores = mm_last(query, keys_at[head]) * (scale * LOG2E)
    side = lax.broadcasted_iota(jnp.int32, (2 * seq, 2 * HEAD_SIZE), 0) // seq
    lane = lax.broadcasted_iota(jnp.int32, (2 * seq, 2 * HEAD_SIZE), 1) // HEAD_SIZE
    ones = (side == lane).astype(BF)
    allowed = bias[...]
    expo = jnp.exp2(
        jnp.concatenate([scores[:, :seq] + allowed, scores[:, seq:] + allowed], axis=1)
    ).astype(BF)
    inv = 1.0 / mm(expo, ones)
    out[...] = (mm(expo, vals_at[head]) * inv).astype(BF)
    inverse[...] = inv


def attend_back_kernel(
    kv, each, scale, pre, keys, vals, bias, cosine, sine, cos_own, sin_own, query_gain, key_gain,
    block, out, inverse, grad, grad_proj, query_sum, key_sum, keys_at, vals_at, key_acc, val_acc,
):
    j, i = pl.program_id(0), pl.program_id(1)
    seq = keys.shape[0]
    rows = pre.shape[0]
    two = 2 * HEAD_SIZE

    @pl.when((j == 0) & (i == 0))
    def _():
        load_heads(keys, vals, cosine, sine, key_gain, block, kv, keys_at, vals_at)
        key_acc[...] = jnp.zeros_like(key_acc)
        val_acc[...] = jnp.zeros_like(val_acc)
        query_sum[...] = jnp.zeros_like(query_sum)

    unit, inv_unit = head_unit(pre[...], block[...])
    query = turn_heads(unit * query_gain[...], cos_own[...], sin_own[...]).astype(BF)
    head = j // each
    keys_of, vals_of = keys_at[head], vals_at[head]
    scores = mm_last(query, keys_of) * (scale * LOG2E)
    low = grad[...]
    gprobs = mm_last(low, vals_of)
    product = low.astype(F32) * out[...].astype(F32)
    delta = split_mean(product, block[...]) * HEAD_SIZE
    inv = inverse[...]
    allowed = bias[...]
    probs, gscores = [], []
    for side in range(2):
        part = slice(side * seq, (side + 1) * seq)
        at = side * HEAD_SIZE
        p = jnp.exp2(scores[:, part] + allowed) * inv[:, at : at + 1]
        probs.append(p.astype(BF))
        gscores.append((p * (gprobs[:, part] - delta[:, at : at + 1])).astype(BF))
    probs = jnp.concatenate(probs, axis=1)
    gscores = jnp.concatenate(gscores, axis=1)
    key_acc[head] += mm_first(gscores, query)
    val_acc[head] += mm_first(probs, low)
    back = turn_back(mm(gscores, keys_of) * scale, cos_own[...], sin_own[...])
    query_sum[...] += jnp.sum(back * unit, axis=0, keepdims=True)
    grad_proj[pl.ds(pl.multiple_of(i * rows, rows), rows), pl.ds(pl.multiple_of(j * two, two), two)] = (
        head_grad(back, unit, inv_unit, query_gain[...], block[...]).astype(BF)
    )

    @pl.when((j == pl.num_programs(0) - 1) & (i == pl.num_programs(1) - 1))
    def _():
        lane = lax.broadcasted_iota(jnp.int32, (seq, two), 1)

        def fold(acc, n):
            both = jnp.where(lane < HEAD_SIZE, acc[n, :seq, :], acc[n, seq:, :])
            return both + pltpu.roll(both, HEAD_SIZE, 1)

        key_tile = fold(key_acc, 0) * scale
        val_tile = fold(val_acc, 0)
        if kv == 2:
            key_tile = jnp.where(lane < HEAD_SIZE, key_tile, fold(key_acc, 1) * scale)
            val_tile = jnp.where(lane < HEAD_SIZE, val_tile, fold(val_acc, 1))
        unit_k, inv_k = head_unit(keys[...], block[...])
        back_k = turn_back(key_tile, cosine[...], sine[...])
        key_sum[...] = jnp.sum(back_k * unit_k, axis=0, keepdims=True)
        key_low = head_grad(back_k, unit_k, inv_k, key_gain[...], block[...])
        start = grad_proj.shape[1] - kv * two
        if kv == 2:
            grad_proj[:, start : start + two] = key_low.astype(BF)
            grad_proj[:, start + two :] = val_tile.astype(BF)
        else:
            grad_proj[:, start:] = jnp.where(lane < HEAD_SIZE, key_low, val_tile).astype(BF)


def attention_call(pre, bias, cosine, sine, query_gain, key_gain, kv, more=None):
    seq, cols = pre.shape
    two = 2 * HEAD_SIZE
    q_cols = cols - kv * two
    tiles = q_cols // two
    each = tiles // kv
    rows = min(512, seq)
    lane = jnp.arange(two) // HEAD_SIZE
    block = jnp.where(lane[:, None] == lane[None, :], 1.0 / HEAD_SIZE, 0.0).astype(BF)
    own = pl.BlockSpec((rows, two), lambda j, i: (i, j))
    here = pl.BlockSpec((rows, two), lambda j, i: (i, 0))
    whole = pl.BlockSpec((seq, two), lambda j, i: (0, 0))
    row = pl.BlockSpec((1, two), lambda j, i: (0, 0))
    key_tile = pl.BlockSpec((seq, two), lambda j, i: (0, tiles))
    val_tile = pl.BlockSpec((seq, two), lambda j, i: (0, tiles + kv - 1))
    in_specs = [
        own, key_tile, val_tile, pl.BlockSpec((rows, seq), lambda j, i: (i, 0)), whole, whole,
        here, here, row, row, pl.BlockSpec((two, two), lambda j, i: (0, 0)),
    ]
    twice = [jnp.concatenate([g, g]).reshape(1, two) for g in (query_gain, key_gain)]
    args = [pre, pre, pre, bias, cosine, sine, cosine, sine, *twice, block]
    heads = pltpu.VMEM((kv, 2 * seq, two), BF)
    params = pltpu.CompilerParams(vmem_limit_bytes=48 * 2**20)
    grid = (tiles, seq // rows)
    scale = HEAD_SIZE ** (-0.5)
    if more is None:
        return pl.pallas_call(
            functools.partial(attend_kernel, kv, each, scale),
            grid=grid,
            in_specs=in_specs,
            out_specs=[own, own],
            out_shape=[
                jax.ShapeDtypeStruct((seq, q_cols), BF),
                jax.ShapeDtypeStruct((seq, q_cols), F32),
            ],
            scratch_shapes=[heads, heads],
            compiler_params=params,
        )(*args)
    sums = pltpu.VMEM((kv, 2 * seq, two), F32)
    return pl.pallas_call(
        functools.partial(attend_back_kernel, kv, each, scale),
        grid=grid,
        in_specs=in_specs + [own, own, own],
        out_specs=[pl.BlockSpec((seq, cols), lambda j, i: (0, 0)), row, row],
        out_shape=[
            jax.ShapeDtypeStruct((seq, cols), BF),
            jax.ShapeDtypeStruct((1, two), F32),
            jax.ShapeDtypeStruct((1, two), F32),
        ],
        scratch_shapes=[heads, heads, sums, sums],
        compiler_params=params,
    )(*args, *more)


def pair_tables(positions):
    half = HEAD_SIZE // 2
    inverse = THETA_BASE ** (-(jnp.arange(half, dtype=F32) * 2.0) / HEAD_SIZE)
    angles = positions.astype(F32)[:, None] * inverse[None, :]
    cosine, sine = jnp.cos(angles), jnp.sin(angles)
    return jnp.tile(cosine, (1, 4)), jnp.concatenate([-sine, sine, -sine, sine], axis=1)


def lanes(width, chips, count):
    part = width // chips // count
    return [
        (slice((z * chips + c) * part, (z * chips + c + 1) * part),
         slice((c * count + z) * part, (c * count + z + 1) * part))
        for z in range(count)
        for c in range(chips)
    ]


def inverse_root(wide):
    return lax.rsqrt(jnp.mean(wide * wide, axis=-1, keepdims=True) + EPSILON)


def norm_forward(chips, count, own, part, right, left, gain, hidden, normed):
    wide = own[...].astype(F32) + part[0] + right[...].astype(F32) + left[...].astype(F32)
    hidden[...] = wide
    low = (wide * inverse_root(wide) * gain[...]).astype(BF)
    for here, there in lanes(wide.shape[1], chips, count):
        normed[:, there] = low[:, here]


def norm_backward(chips, count, part, right, left, wide, base, gain, grad, low, total, scratch):
    summed = part[0] + right[...].astype(F32) + left[...].astype(F32)
    if chips:
        for here, there in lanes(summed.shape[1], chips, count):
            scratch[:, here] = summed[:, there]
        summed = scratch[...]
    values = wide[...].astype(F32)
    inverse = inverse_root(values)
    unit = values * inverse
    sums = jnp.sum(summed * unit, axis=0, keepdims=True)

    @pl.when(pl.program_id(0) == 0)
    def _():
        total[...] = sums

    @pl.when(pl.program_id(0) > 0)
    def _():
        total[...] += sums

    scaled = summed * gain[...]
    out = base[...].astype(F32) + inverse * (
        scaled - unit * jnp.mean(scaled * unit, axis=-1, keepdims=True)
    )
    grad[...] = out
    low[...] = out.astype(BF)


def row_specs(tok, width):
    step = min(32, tok)
    block = pl.BlockSpec((step, width), lambda i: (i, 0))
    first = pl.BlockSpec((1, step, width), lambda i: (0, i, 0))
    row = pl.BlockSpec((1, width), lambda i: (0, 0))
    return tok // step, step, block, first, row


def forward_norm(own, parts, right, left, gain, chips, count):
    tok, width = own.shape
    grid, _, block, first, row = row_specs(tok, width)
    return pl.pallas_call(
        functools.partial(norm_forward, chips, count),
        grid=(grid,),
        in_specs=[block, first, block, block, row],
        out_specs=[block, block],
        out_shape=[
            jax.ShapeDtypeStruct((tok, width), F32),
            jax.ShapeDtypeStruct((tok, width), BF),
        ],
    )(own, parts, right, left, gain.reshape(1, width))


def backward_norm(parts, right, left, wide, base, gain, chips, count):
    tok, width = wide.shape
    grid, step, block, first, row = row_specs(tok, width)
    return pl.pallas_call(
        functools.partial(norm_backward, chips, count),
        grid=(grid,),
        in_specs=[first, block, block, block, block, row],
        out_specs=[block, block, row],
        out_shape=[
            jax.ShapeDtypeStruct((tok, width), F32),
            jax.ShapeDtypeStruct((tok, width), BF),
            jax.ShapeDtypeStruct((1, width), F32),
        ],
        scratch_shapes=[pltpu.VMEM((step, width), F32)],
    )(parts, right, left, wide, base, gain.reshape(1, width))


def cast_pair(own, out):
    _, cores, count, _, _ = own.shape
    half = out.shape[1] // cores // count
    for j in range(count):
        for k in range(cores):
            at = (j * cores + k) * half
            out[:, at : at + half] = own[0, k, j].astype(F32)


def place_pair(own, which, chips, count, part, half):
    step = min(64, part)
    own = own.reshape(chips, 2, count, part, 2 * half)
    cols = count * 2 * half
    return pl.pallas_call(
        cast_pair,
        grid=(chips, part // step),
        in_specs=[pl.BlockSpec((1, 2, count, step, half), lambda c, r: (c, 0, 0, r, which))],
        out_specs=pl.BlockSpec((step, cols), lambda c, r: (c * (part // step) + r, 0)),
        out_shape=jax.ShapeDtypeStruct((chips * part, cols), F32),
    )(own)


def cast_columns(_, one, two, *outs):
    half = pl.num_programs(0) // 2
    for own, mine in ((one, pl.program_id(0) < half), (two, pl.program_id(0) >= half)):

        @pl.when(mine)
        def _(own=own):
            at = 0
            for out in outs:
                out[...] = own[:, at : at + out.shape[1]].astype(F32)
                at += out.shape[1]


def place_columns(order, one, two, widths):
    blocks = order.shape[0]
    rows, cols = one.shape
    half = blocks // 2
    step = rows // half
    return pl.pallas_call(
        cast_columns,
        grid_spec=pltpu.PrefetchScalarGridSpec(
            num_scalar_prefetch=1,
            grid=(blocks,),
            in_specs=[
                pl.BlockSpec((step, cols), lambda r, order: (jnp.minimum(r, half - 1), 0)),
                pl.BlockSpec((step, cols), lambda r, order: (jnp.maximum(r - half, 0), 0)),
            ],
            out_specs=[pl.BlockSpec((step, w), lambda r, order: (order[r], 0)) for w in widths],
        ),
        out_shape=[jax.ShapeDtypeStruct((2 * rows, w), F32) for w in widths],
    )(order, one, two)


def gather_stage(halves, step, pin=()):
    chips = lax.axis_size("chip")
    bits = chips.bit_length() - 1
    out = []
    for g, half in enumerate(halves):
        bit = (g + step) % bits
        got = lax.ppermute(half, "chip", [(i, i ^ (1 << bit)) for i in range(chips)])
        out.append(jnp.concatenate([half, after(got, pin)], axis=0))
    return out


def gathered_order(g):
    chips = lax.axis_size("chip")
    bits = chips.bit_length() - 1
    chip, core = lax.axis_index("chip"), lax.axis_index("core")
    away = [0]
    for step in range(bits):
        away += [a ^ (1 << ((g + step) % bits)) for a in away]
    places = [(chip ^ a) * 2 + (core ^ k) for k in range(2) for a in away]
    return jnp.stack(places).astype(jnp.int32)


def cast_down(own, out):
    out[...] = own[0].astype(F32)


def place_down(own, chips, part, width):
    return pl.pallas_call(
        cast_down,
        grid=(2, chips),
        in_specs=[pl.BlockSpec((1, part, width), lambda k, c: (c * 2 + k, 0, 0))],
        out_specs=pl.BlockSpec((part, width), lambda k, c: (k * chips + c, 0)),
        out_shape=jax.ShapeDtypeStruct((2 * chips * part, width), F32),
    )(own)


def shards(
    inputs,
    doc_lengths,
    attn_gain,
    query_weight,
    key_projection,
    value_projection,
    query_gain,
    key_norm_gain,
    out_weight,
    ffn_gain,
    gate_weight,
    up_weight,
    down_weight,
    cotangent,
):
    tok, width = inputs.shape
    count = lax.axis_size("fsdp")
    chips = lax.axis_size("chip")
    rep = chips * 2
    mine = lax.axis_index("fsdp")
    chip = lax.axis_index("chip")
    core = lax.axis_index("core")
    seq = tok * count
    hd = HEAD_SIZE
    rows = query_weight.shape[0]
    q_cols = query_weight.shape[1] // count
    kv_cols = key_projection.shape[1] // count
    ff = gate_weight.shape[1]
    ff_own = ff // count // 2

    share = rows // rep
    at = (chip * 2 + core) * share

    def proj_piece(j):
        return jnp.concatenate(
            [
                lax.dynamic_slice(w, (at, j * wide), (share, wide))
                for w, wide in (
                    (query_weight, q_cols),
                    (key_projection, kv_cols),
                    (value_projection, kv_cols),
                )
            ],
            axis=1,
        )

    proj_ring = exchange_line(proj_piece)
    begun = line_step(inputs, inputs)
    proj_own = absolute(after(proj_ring, begun))
    x_steps = line_steps(inputs, {2: proj_own}, begun)
    x_all = line_pieces(inputs, x_steps)
    proj = lax.all_gather(proj_own, PLANE, axis=0)
    proj = proj.transpose(1, 0, 2, 3).reshape(width, q_cols + 2 * kv_cols)

    gains = jnp.concatenate([attn_gain, ffn_gain, query_gain, key_norm_gain])
    gains = gather_small(after(gains, x_steps[1]))
    gains = gains.astype(F32)
    gain_one = gains[:, :rows].reshape(-1)
    gain_two = gains[:, rows : 2 * rows].reshape(-1)
    small = hd // count
    gain_query = gains[:, 2 * rows : 2 * rows + small].reshape(-1)
    gain_key = gains[:, 2 * rows + small :].reshape(-1)

    part = rows // chips
    gate_up = after((gate_weight, up_weight), x_steps[-1])

    def pair_piece(j):
        return jnp.concatenate(
            [
                lax.dynamic_slice(w, (chip * part, (j * 2 + core) * ff_own), (part, ff_own))
                for w in gate_up
            ],
            axis=1,
        )

    pair_ring = exchange_line(pair_piece)

    order = (mine - jnp.arange(count, dtype=jnp.int32)) % count
    positions = (order[:, None] * tok + jnp.arange(tok, dtype=jnp.int32)[None, :]).reshape(-1)
    lengths = after(doc_lengths, x_steps[1])[0]
    docs = lengths.shape[0]
    upto = jnp.arange(docs)[None, :] <= jnp.arange(docs)[:, None]
    ends = jnp.sum(jnp.where(upto, lengths[None, :], 0), axis=1)
    segment = jnp.sum((positions[:, None] >= ends[None, :]).astype(jnp.int32), axis=1)
    allowed = (segment[:, None] == segment[None, :]) & (positions[None, :] <= positions[:, None])
    bias = jnp.where(allowed, 0.0, NEG_FILL).astype(F32)
    tables = pair_tables(positions)

    wide = x_all.astype(F32)
    normed_one = (wide * inverse_root(wide) * gain_one).astype(BF)
    kv_heads = kv_cols // hd
    core_args = (mm(normed_one, proj), bias, *tables, gain_query, gain_key, kv_heads)
    attended, inverse_sums = attention_call(*core_args)
    out_part = mm(attended, out_weight).reshape(count, tok, width)
    stage = {}

    def slices(t, sides):
        if t == 1:
            stage["slices"] = absolute(after(pair_ring, sides))
            return stage["slices"]
        return ()

    sides = line_scatter(out_part, slices)
    pair = lax.all_gather(stage["slices"], "chip", axis=0)
    pair = pair.reshape(width, 2 * ff_own)
    hidden_one, normed_own = forward_norm(inputs, out_part, *sides, gain_two, chips, count)

    cot_begun = line_step(*(after(cotangent, sides),) * 2)
    two_steps = line_steps(after(normed_own, cot_begun))
    normed_two = line_pieces(normed_own, two_steps)
    normed_two = jnp.concatenate([normed_two, swap_cores(normed_two)], axis=0)
    down_own = lax.dynamic_slice_in_dim(down_weight, core * ff_own, ff_own)
    both = mm(normed_two, pair)
    cot_steps = line_steps(cotangent, {1: two_steps[-1], count - 2: both}, cot_begun)
    cot_own = line_pieces(cotangent, cot_steps)
    cot_all = jnp.concatenate([cot_own, swap_cores(cot_own)], axis=0)
    grad_hidden = mm_last(cot_all, down_own)
    gate_pre, upward = both[:, :ff_own], both[:, ff_own:]
    sigmoid = jax.nn.sigmoid(gate_pre)
    silu = gate_pre * sigmoid
    hidden = (silu * upward).astype(BF)
    grad_gate = (grad_hidden * upward * sigmoid * (1.0 + gate_pre * (1.0 - sigmoid))).astype(BF)
    grad_up = (grad_hidden * silu).astype(BF)
    grad_both = jnp.concatenate([grad_gate, grad_up], axis=1)

    down_part = mm_first(hidden, cot_all).astype(BF)
    down_sum = lax.psum_scatter(down_part, "chip", scatter_dimension=0, tiled=True)
    out_other = mm(after(hidden[seq:], down_part), down_own).astype(BF)
    other = mm_last(after(grad_both[seq:], out_other), pair).astype(BF)
    out_terms = mm(after(hidden[:seq], other), down_own) + swap_cores(out_other).astype(F32)
    out_terms = out_terms.reshape(count, tok, width)
    pair_part = mm_first(normed_two, after(grad_both, out_terms)).astype(BF)
    pair_sum = lax.psum_scatter(pair_part, "chip", scatter_dimension=0, tiled=True)
    own = after(grad_both[:seq], pair_part)
    two_terms = mm_last(own, pair) + swap_cores(other).astype(F32)
    two_terms = two_terms.reshape(count, tok, width)
    sides = line_scatter(out_terms, lambda t, _: pair_part if t == 1 else two_terms)
    output = (
        hidden_one + out_terms[0] + sides[0].astype(F32) + sides[1].astype(F32)
    ).astype(BF)
    sides = line_scatter(two_terms)
    grad_hidden_one, grad_low, gain_two_sum = backward_norm(
        two_terms, *sides, hidden_one, cotangent, gain_two, chips, count
    )
    grad_attn = line_pieces(grad_low, line_steps(grad_low))

    grad_att = mm_last(grad_attn, out_weight).astype(BF)
    out_term = mm_first(attended, grad_attn).astype(BF)
    grad_att = after(grad_att, out_term)
    down_all = lax.all_gather(after(down_sum, grad_att), PLANE, axis=0)
    pair_sum = after(pair_sum, grad_att)
    rings = [
        exchange_line(
            lambda j, w=w: lax.dynamic_slice(pair_sum, (j * part, w * ff_own), (part, ff_own))
        )
        for w in range(2)
    ]
    grad_proj, query_sum, key_sum = attention_call(
        *core_args, more=(attended, inverse_sums, grad_att)
    )
    query_gain_sum = query_sum[0, :hd] + query_sum[0, hd:]
    key_gain_sum = key_sum[0, :hd] + (key_sum[0, hd:] if kv_heads == 2 else 0.0)
    proj_part = mm_first(normed_one, grad_proj).astype(BF)
    one_part = mm_last(after(grad_proj, proj_part), proj).reshape(count, tok, width)
    bits = chips.bit_length() - 1
    cols = q_cols + 2 * kv_cols
    att_terms = [proj_part.reshape(count, chips, 2, share, cols), out_term.reshape(chips, 2, share, -1)]

    def att_cores(pin):
        out = [halve(x, 2 - g, "core", 0, pin) for g, x in enumerate(att_terms)]
        return [
            out[0].reshape([count] + [2] * bits + [share, cols]),
            out[1].reshape([2] * bits + [share, width]),
        ]

    att_sum = att_cores(one_part)
    ffn_sum = jnp.concatenate([absolute(after(ring, att_sum)) for ring in rings], axis=2)
    ffn_all = lax.all_gather(ffn_sum.reshape(count * part, 2 * ff_own), PLANE, axis=0)

    def att_stages(t, sides):
        if t > 2:
            return ()
        stage["att"] = chip_stage(stage.get("att", att_sum), t - 1, sides, (1, 0))
        return (stage["att"], down_grad) if t == 2 else stage["att"]

    down_grad = place_down(down_all, chips, ff_own // chips, width)
    sides = line_scatter(after(one_part, ffn_sum), att_stages)
    _, input_grad, gain_one_sum = backward_norm(
        one_part, *sides, inputs, grad_hidden_one, gain_one, 0, count
    )

    sums = jnp.concatenate(
        [
            v.reshape(count, -1)
            for v in (gain_one_sum, gain_two_sum, query_gain_sum, key_gain_sum)
        ],
        axis=1,
    )

    att_sum = chip_rest(stage["att"], 2, sides, (1, 0))
    ring = exchange_line(lambda j: lax.dynamic_index_in_dim(att_sum[0], j, keepdims=False))
    cuts = ((0, q_cols), (q_cols, q_cols + kv_cols), (q_cols + kv_cols, cols))
    got = absolute(after(ring, input_grad))
    columns = [[got[j, :, a:b] for j in range(count)] for a, b in cuts]
    att_all = [
        jnp.concatenate(columns[0] + columns[1], axis=1),
        jnp.concatenate(columns[2] + [att_sum[1]], axis=1),
    ]
    sums = small_line(sums, att_all)
    gate_grad, up_grad = (place_pair(ffn_all, w, chips, count, part, ff_own) for w in range(2))
    for step in range(bits):
        last = step == bits - 1
        att_all = gather_stage(att_all, step, (gate_grad, up_grad) if last else sums)
        if step == 0:
            sums = sums + after(swap_cores(sums), att_all)
    sums = small_chips(sums, att_all)
    others = [swap_cores(a) for a in att_all]
    query_grad, key_grad = place_columns(
        gathered_order(0), att_all[0], others[0], (q_cols * count, kv_cols * count)
    )
    value_grad, out_grad = place_columns(
        gathered_order(1), att_all[1], others[1], (kv_cols * count, width)
    )
    return (
        output,
        input_grad,
        sums[:rows],
        query_grad,
        key_grad,
        value_grad,
        sums[2 * rows : 2 * rows + small],
        sums[2 * rows + small :],
        out_grad,
        sums[rows : 2 * rows],
        gate_grad,
        up_grad,
        down_grad,
    )


def solution(mesh):
    chips, count = mesh.shape["rep"] // 2, mesh.shape["fsdp"]
    split = Mesh(mesh.devices.reshape(chips, 2, count), ("chip", "core", "fsdp"))
    tokens, reps, fsdp = (*PLANE, "fsdp"), PLANE, "fsdp"
    in_specs = (
        P(tokens, None),
        P(reps, None),
        P(fsdp),
        P(fsdp, None),
        P(fsdp, None),
        P(fsdp, None),
        P(fsdp),
        P(fsdp),
        P(fsdp, None),
        P(fsdp),
        P(fsdp, None),
        P(fsdp, None),
        P(fsdp, None),
        P(tokens, None),
    )
    out_specs = (
        P(tokens, None),
        P(tokens, None),
        P(fsdp),
        P(fsdp, None),
        P(fsdp, None),
        P(fsdp, None),
        P(fsdp),
        P(fsdp),
        P(fsdp, None),
        P(fsdp),
        P(fsdp, None),
        P(fsdp, None),
        P(fsdp, None),
    )
    return jax.shard_map(
        shards, mesh=split, in_specs=in_specs, out_specs=out_specs, check_vma=False
    )
```

```python
import functools

import jax
import jax.numpy as jnp
from jax import lax
from jax.experimental import pallas as pl
from jax.experimental.pallas import tpu as pltpu
from jax.sharding import Mesh, PartitionSpec as P

HEAD_SIZE = 64
EPSILON = 1e-05
THETA_BASE = 1000000.0
NEG_FILL = -1e30
LOG2E = 1.4426950408889634
BF = jnp.bfloat16
F32 = jnp.float32
PLANE = ("chip", "core")


def mm(a, b):
    return jnp.dot(a, b, preferred_element_type=F32)


def mm_last(a, b):
    return lax.dot_general(a, b, (((1,), (1,)), ((), ())), preferred_element_type=F32)


def mm_first(a, b):
    return lax.dot_general(a, b, (((0,), (0,)), ((), ())), preferred_element_type=F32)


def swap_cores(a):
    return lax.ppermute(a, "core", [(0, 1), (1, 0)])


def exchanges():
    count = lax.axis_size("fsdp")
    even = [(i, i ^ 1) for i in range(count)]
    odd = [(0, 0)] + [(i, ((i - 1) ^ 1) + 1) for i in range(1, count - 1)] + [(count - 1, count - 1)]
    return even, odd


def line_step(first, second):
    even, odd = exchanges()
    return lax.ppermute(first, "fsdp", even), lax.ppermute(second, "fsdp", odd)


def line_steps(own, ahead_of={}, begun=None, turn=None):
    steps = []
    first, second = own, own
    for t in range(lax.axis_size("fsdp") - 1):
        if t in ahead_of:
            first, second = after((first, second), ahead_of[t])
        if t and turn:
            first, second = after((first, second), turn((first, second)))
        if t == 0 and begun:
            by_even, by_odd = begun
        else:
            by_even, by_odd = line_step(first, second)
        steps.append((by_even, by_odd))
        first, second = by_odd, by_even
    return steps


def line_pieces(own, steps):
    count = lax.axis_size("fsdp")
    mine = lax.axis_index("fsdp")
    is_even = mine % 2 == 0
    pieces = [own]
    for d in range(1, count):
        below, above = steps[d - 1], steps[count - d - 1]
        from_below = jnp.where(is_even, below[1], below[0])
        from_above = jnp.where(is_even, above[0], above[1])
        pieces.append(jnp.where(mine >= d, from_below, from_above))
    return jnp.concatenate(pieces, axis=0)


def line_scatter(parts, ahead_of=None):
    count = lax.axis_size("fsdp")
    mine = lax.axis_index("fsdp")
    is_even = mine % 2 == 0
    is_end = (mine == 0) | (mine == count - 1)
    by_even = by_odd = None
    for t in range(count - 1):
        up = jnp.where(is_even, t + 1, count - 1 - t)
        first = lax.dynamic_index_in_dim(parts, up, keepdims=False)
        second = lax.dynamic_index_in_dim(parts, count - up, keepdims=False)
        if t:
            if ahead_of:
                by_even, by_odd = after((by_even, by_odd), ahead_of(t, (by_even, by_odd)))
            first, second = first + by_odd.astype(F32), second + by_even.astype(F32)
        second = jnp.where(is_end, 0.0, second)
        by_even, by_odd = line_step(first.astype(BF), second.astype(BF))
    return by_even, by_odd


def absolute(ring):
    count = len(ring)
    mine = lax.axis_index("fsdp")
    out = jnp.zeros((count, *ring[0].shape), ring[0].dtype)
    for e, piece in enumerate(ring):
        out = lax.dynamic_update_index_in_dim(out, piece, (mine + e) % count, 0)
    return out


def exchange_line(piece_for):
    count = lax.axis_size("fsdp")
    mine = lax.axis_index("fsdp")
    return [piece_for(mine)] + [
        lax.ppermute(
            piece_for((mine - e) % count),
            "fsdp",
            [(i, (i - e) % count) for i in range(count)],
        )
        for e in range(1, count)
    ]


def add_low(a, b):
    return (a.astype(F32) + b.astype(F32)).astype(BF)


def halve(blocks, axis, name, bit, pin=()):
    mybit = (lax.axis_index(name) >> bit) & 1
    pairs = [(i, i ^ (1 << bit)) for i in range(lax.axis_size(name))]
    got = lax.ppermute(
        lax.dynamic_index_in_dim(blocks, 1 - mybit, axis, keepdims=False), name, pairs
    )
    got = after(got, pin)
    return add_low(lax.dynamic_index_in_dim(blocks, mybit, axis, keepdims=False), got)


def chip_halves(terms):
    chips, rows, cols = terms.shape
    bits = chips.bit_length() - 1
    return [
        terms[:, g * rows // 2 : (g + 1) * rows // 2].reshape([2] * bits + [rows // 2, cols])
        for g in range(2)
    ]


def chip_stage(halves, step, pin=(), lead=(0, 0)):
    bits = lax.axis_size("chip").bit_length() - 1
    out = []
    for g in range(2):
        done = [(g + k) % bits for k in range(step)]
        left = [b for b in range(bits - 1, -1, -1) if b not in done]
        bit = (g + step) % bits
        out.append(halve(halves[g], lead[g] + left.index(bit), "chip", bit, pin))
    return out


def chip_rest(halves, step, pin=(), lead=(0, 0)):
    for k in range(step, lax.axis_size("chip").bit_length() - 1):
        halves = chip_stage(halves, k, pin, lead)
    return halves


def after(value, *others):
    return lax.optimization_barrier((value, *others))[0]


def gather_small(own):
    return absolute(exchange_line(lambda j: own))


def small_line(rows, pin):
    count = lax.axis_size("fsdp")
    mine = lax.axis_index("fsdp")
    got = [
        lax.ppermute(
            lax.dynamic_index_in_dim(rows, (mine + d) % count, keepdims=False),
            "fsdp",
            [(i, (i + d) % count) for i in range(count)],
        )
        for d in range(1, count)
    ]
    return sum(after(got, pin), lax.dynamic_index_in_dim(rows, mine, keepdims=False))


def small_chips(total, pin):
    chips = lax.axis_size("chip")
    got = [
        lax.ppermute(total, "chip", [(i, i ^ d) for i in range(chips)]) for d in range(1, chips)
    ]
    return sum(after(got, pin), total)


def split_mean(values, block):
    high = values.astype(BF)
    low = (values - high.astype(F32)).astype(BF)
    return mm(high, block) + mm(low, block)


def swap_pairs(values):
    lane = lax.broadcasted_iota(jnp.int32, values.shape, 1)
    half = HEAD_SIZE // 2
    lanes = values.shape[1]
    return jnp.where(
        lane % HEAD_SIZE < half,
        pltpu.roll(values, lanes - half, 1),
        pltpu.roll(values, half, 1),
    )


def head_unit(pre, block):
    inverse = lax.rsqrt(split_mean(pre * pre, block) + EPSILON)
    return pre * inverse, inverse


def turn_heads(values, cosine, sine):
    return values * cosine + swap_pairs(values) * sine


def turn_back(values, cosine, sine):
    return values * cosine - swap_pairs(values) * sine


def head_grad(grad, unit, inverse, gain, block):
    scaled = grad * gain
    return inverse * (scaled - unit * split_mean(scaled * unit, block))


def spread(values, source, seq, rows):
    lanes = values.shape[1]
    a = lax.broadcasted_iota(jnp.int32, (lanes, 2 * HEAD_SIZE), 0)
    b = lax.broadcasted_iota(jnp.int32, (lanes, 2 * HEAD_SIZE), 1)
    for side in range(2):
        move = (a - source * HEAD_SIZE == b - side * HEAD_SIZE) & (b // HEAD_SIZE == side)
        rows[side * seq : (side + 1) * seq, :] = mm(values, move.astype(BF)).astype(BF)


def load_heads(keys, vals, cosine, sine, key_gain, block, kv, keys_at, vals_at):
    seq = keys.shape[0]
    unit, _ = head_unit(keys[...], block[...])
    turned = turn_heads(unit * key_gain[...], cosine[...], sine[...]).astype(BF)
    low = vals[...].astype(BF)
    for n in range(kv):
        spread(turned, n, seq, keys_at.at[n])
        spread(low, n if kv == 2 else 1, seq, vals_at.at[n])


def attend_kernel(
    kv, each, scale, pre, keys, vals, bias, cosine, sine, cos_own, sin_own, query_gain, key_gain,
    block, out, inverse, keys_at, vals_at,
):
    j, i = pl.program_id(0), pl.program_id(1)
    seq = keys.shape[0]

    @pl.when((j == 0) & (i == 0))
    def _():
        load_heads(keys, vals, cosine, sine, key_gain, block, kv, keys_at, vals_at)

    unit, _ = head_unit(pre[...], block[...])
    query = turn_heads(unit * query_gain[...], cos_own[...], sin_own[...]).astype(BF)
    head = j // each
    scores = mm_last(query, keys_at[head]) * (scale * LOG2E)
    side = lax.broadcasted_iota(jnp.int32, (2 * seq, 2 * HEAD_SIZE), 0) // seq
    lane = lax.broadcasted_iota(jnp.int32, (2 * seq, 2 * HEAD_SIZE), 1) // HEAD_SIZE
    ones = (side == lane).astype(BF)
    allowed = bias[...]
    expo = jnp.exp2(
        jnp.concatenate([scores[:, :seq] + allowed, scores[:, seq:] + allowed], axis=1)
    ).astype(BF)
    inv = 1.0 / mm(expo, ones)
    out[...] = (mm(expo, vals_at[head]) * inv).astype(BF)
    inverse[...] = inv


def attend_back_kernel(
    kv, each, scale, pre, keys, vals, bias, cosine, sine, cos_own, sin_own, query_gain, key_gain,
    block, out, inverse, grad, grad_proj, query_sum, key_sum, keys_at, vals_at, key_acc, val_acc,
):
    j, i = pl.program_id(0), pl.program_id(1)
    seq = keys.shape[0]
    rows = pre.shape[0]
    two = 2 * HEAD_SIZE

    @pl.when((j == 0) & (i == 0))
    def _():
        load_heads(keys, vals, cosine, sine, key_gain, block, kv, keys_at, vals_at)
        key_acc[...] = jnp.zeros_like(key_acc)
        val_acc[...] = jnp.zeros_like(val_acc)
        query_sum[...] = jnp.zeros_like(query_sum)

    unit, inv_unit = head_unit(pre[...], block[...])
    query = turn_heads(unit * query_gain[...], cos_own[...], sin_own[...]).astype(BF)
    head = j // each
    keys_of, vals_of = keys_at[head], vals_at[head]
    scores = mm_last(query, keys_of) * (scale * LOG2E)
    low = grad[...]
    gprobs = mm_last(low, vals_of)
    product = low.astype(F32) * out[...].astype(F32)
    delta = split_mean(product, block[...]) * HEAD_SIZE
    inv = inverse[...]
    allowed = bias[...]
    probs, gscores = [], []
    for side in range(2):
        part = slice(side * seq, (side + 1) * seq)
        at = side * HEAD_SIZE
        p = jnp.exp2(scores[:, part] + allowed) * inv[:, at : at + 1]
        probs.append(p.astype(BF))
        gscores.append((p * (gprobs[:, part] - delta[:, at : at + 1])).astype(BF))
    probs = jnp.concatenate(probs, axis=1)
    gscores = jnp.concatenate(gscores, axis=1)
    key_acc[head] += mm_first(gscores, query)
    val_acc[head] += mm_first(probs, low)
    back = turn_back(mm(gscores, keys_of) * scale, cos_own[...], sin_own[...])
    query_sum[...] += jnp.sum(back * unit, axis=0, keepdims=True)
    grad_proj[pl.ds(pl.multiple_of(i * rows, rows), rows), pl.ds(pl.multiple_of(j * two, two), two)] = (
        head_grad(back, unit, inv_unit, query_gain[...], block[...]).astype(BF)
    )

    @pl.when((j == pl.num_programs(0) - 1) & (i == pl.num_programs(1) - 1))
    def _():
        lane = lax.broadcasted_iota(jnp.int32, (seq, two), 1)

        def fold(acc, n):
            both = jnp.where(lane < HEAD_SIZE, acc[n, :seq, :], acc[n, seq:, :])
            return both + pltpu.roll(both, HEAD_SIZE, 1)

        key_tile = fold(key_acc, 0) * scale
        val_tile = fold(val_acc, 0)
        if kv == 2:
            key_tile = jnp.where(lane < HEAD_SIZE, key_tile, fold(key_acc, 1) * scale)
            val_tile = jnp.where(lane < HEAD_SIZE, val_tile, fold(val_acc, 1))
        unit_k, inv_k = head_unit(keys[...], block[...])
        back_k = turn_back(key_tile, cosine[...], sine[...])
        key_sum[...] = jnp.sum(back_k * unit_k, axis=0, keepdims=True)
        key_low = head_grad(back_k, unit_k, inv_k, key_gain[...], block[...])
        start = grad_proj.shape[1] - kv * two
        if kv == 2:
            grad_proj[:, start : start + two] = key_low.astype(BF)
            grad_proj[:, start + two :] = val_tile.astype(BF)
        else:
            grad_proj[:, start:] = jnp.where(lane < HEAD_SIZE, key_low, val_tile).astype(BF)


def attention_call(pre, bias, cosine, sine, query_gain, key_gain, kv, more=None):
    seq, cols = pre.shape
    two = 2 * HEAD_SIZE
    q_cols = cols - kv * two
    tiles = q_cols // two
    each = tiles // kv
    rows = min(512, seq)
    lane = jnp.arange(two) // HEAD_SIZE
    block = jnp.where(lane[:, None] == lane[None, :], 1.0 / HEAD_SIZE, 0.0).astype(BF)
    own = pl.BlockSpec((rows, two), lambda j, i: (i, j))
    here = pl.BlockSpec((rows, two), lambda j, i: (i, 0))
    whole = pl.BlockSpec((seq, two), lambda j, i: (0, 0))
    row = pl.BlockSpec((1, two), lambda j, i: (0, 0))
    key_tile = pl.BlockSpec((seq, two), lambda j, i: (0, tiles))
    val_tile = pl.BlockSpec((seq, two), lambda j, i: (0, tiles + kv - 1))
    in_specs = [
        own, key_tile, val_tile, pl.BlockSpec((rows, seq), lambda j, i: (i, 0)), whole, whole,
        here, here, row, row, pl.BlockSpec((two, two), lambda j, i: (0, 0)),
    ]
    twice = [jnp.concatenate([g, g]).reshape(1, two) for g in (query_gain, key_gain)]
    args = [pre, pre, pre, bias, cosine, sine, cosine, sine, *twice, block]
    heads = pltpu.VMEM((kv, 2 * seq, two), BF)
    params = pltpu.CompilerParams(vmem_limit_bytes=48 * 2**20)
    grid = (tiles, seq // rows)
    scale = HEAD_SIZE ** (-0.5)
    if more is None:
        return pl.pallas_call(
            functools.partial(attend_kernel, kv, each, scale),
            grid=grid,
            in_specs=in_specs,
            out_specs=[own, own],
            out_shape=[
                jax.ShapeDtypeStruct((seq, q_cols), BF),
                jax.ShapeDtypeStruct((seq, q_cols), F32),
            ],
            scratch_shapes=[heads, heads],
            compiler_params=params,
        )(*args)
    sums = pltpu.VMEM((kv, 2 * seq, two), F32)
    return pl.pallas_call(
        functools.partial(attend_back_kernel, kv, each, scale),
        grid=grid,
        in_specs=in_specs + [own, own, own],
        out_specs=[pl.BlockSpec((seq, cols), lambda j, i: (0, 0)), row, row],
        out_shape=[
            jax.ShapeDtypeStruct((seq, cols), BF),
            jax.ShapeDtypeStruct((1, two), F32),
            jax.ShapeDtypeStruct((1, two), F32),
        ],
        scratch_shapes=[heads, heads, sums, sums],
        compiler_params=params,
    )(*args, *more)


def pair_tables(positions):
    half = HEAD_SIZE // 2
    inverse = THETA_BASE ** (-(jnp.arange(half, dtype=F32) * 2.0) / HEAD_SIZE)
    angles = positions.astype(F32)[:, None] * inverse[None, :]
    cosine, sine = jnp.cos(angles), jnp.sin(angles)
    return jnp.tile(cosine, (1, 4)), jnp.concatenate([-sine, sine, -sine, sine], axis=1)


def lanes(width, chips, count):
    part = width // chips // count
    return [
        (slice((z * chips + c) * part, (z * chips + c + 1) * part),
         slice((c * count + z) * part, (c * count + z + 1) * part))
        for z in range(count)
        for c in range(chips)
    ]


def inverse_root(wide):
    return lax.rsqrt(jnp.mean(wide * wide, axis=-1, keepdims=True) + EPSILON)


def norm_forward(chips, count, own, part, right, left, gain, hidden, normed):
    wide = own[...].astype(F32) + part[0] + right[...].astype(F32) + left[...].astype(F32)
    hidden[...] = wide
    low = (wide * inverse_root(wide) * gain[...]).astype(BF)
    for here, there in lanes(wide.shape[1], chips, count):
        normed[:, there] = low[:, here]


def norm_backward(chips, count, part, right, left, wide, base, gain, grad, low, total, scratch):
    summed = part[0] + right[...].astype(F32) + left[...].astype(F32)
    if chips:
        for here, there in lanes(summed.shape[1], chips, count):
            scratch[:, here] = summed[:, there]
        summed = scratch[...]
    values = wide[...].astype(F32)
    inverse = inverse_root(values)
    unit = values * inverse
    sums = jnp.sum(summed * unit, axis=0, keepdims=True)

    @pl.when(pl.program_id(0) == 0)
    def _():
        total[...] = sums

    @pl.when(pl.program_id(0) > 0)
    def _():
        total[...] += sums

    scaled = summed * gain[...]
    out = base[...].astype(F32) + inverse * (
        scaled - unit * jnp.mean(scaled * unit, axis=-1, keepdims=True)
    )
    grad[...] = out
    low[...] = out.astype(BF)


def row_specs(tok, width):
    step = min(32, tok)
    block = pl.BlockSpec((step, width), lambda i: (i, 0))
    first = pl.BlockSpec((1, step, width), lambda i: (0, i, 0))
    row = pl.BlockSpec((1, width), lambda i: (0, 0))
    return tok // step, step, block, first, row


def forward_norm(own, parts, right, left, gain, chips, count):
    tok, width = own.shape
    grid, _, block, first, row = row_specs(tok, width)
    return pl.pallas_call(
        functools.partial(norm_forward, chips, count),
        grid=(grid,),
        in_specs=[block, first, block, block, row],
        out_specs=[block, block],
        out_shape=[
            jax.ShapeDtypeStruct((tok, width), F32),
            jax.ShapeDtypeStruct((tok, width), BF),
        ],
    )(own, parts, right, left, gain.reshape(1, width))


def backward_norm(parts, right, left, wide, base, gain, chips, count):
    tok, width = wide.shape
    grid, step, block, first, row = row_specs(tok, width)
    return pl.pallas_call(
        functools.partial(norm_backward, chips, count),
        grid=(grid,),
        in_specs=[first, block, block, block, block, row],
        out_specs=[block, block, row],
        out_shape=[
            jax.ShapeDtypeStruct((tok, width), F32),
            jax.ShapeDtypeStruct((tok, width), BF),
            jax.ShapeDtypeStruct((1, width), F32),
        ],
        scratch_shapes=[pltpu.VMEM((step, width), F32)],
    )(parts, right, left, wide, base, gain.reshape(1, width))


def cast_pair(own, out):
    _, cores, count, _, _ = own.shape
    half = out.shape[1] // cores // count
    for j in range(count):
        for k in range(cores):
            at = (j * cores + k) * half
            out[:, at : at + half] = own[0, k, j].astype(F32)


def place_pair(own, which, chips, count, part, half):
    step = min(64, part)
    own = own.reshape(chips, 2, count, part, 2 * half)
    cols = count * 2 * half
    return pl.pallas_call(
        cast_pair,
        grid=(chips, part // step),
        in_specs=[pl.BlockSpec((1, 2, count, step, half), lambda c, r: (c, 0, 0, r, which))],
        out_specs=pl.BlockSpec((step, cols), lambda c, r: (c * (part // step) + r, 0)),
        out_shape=jax.ShapeDtypeStruct((chips * part, cols), F32),
    )(own)


def cast_columns(_, *refs):
    half = pl.num_programs(0) // 2
    for g in range(2):
        outs = refs[4 + 2 * g : 6 + 2 * g]
        for own, mine in (
            (refs[2 * g], pl.program_id(0) < half),
            (refs[2 * g + 1], pl.program_id(0) >= half),
        ):

            @pl.when(mine)
            def _(own=own, outs=outs):
                at = 0
                for out in outs:
                    out[...] = own[:, at : at + out.shape[1]].astype(F32)
                    at += out.shape[1]


def place_columns(orders, pairs, widths):
    blocks = orders.shape[1]
    half = blocks // 2
    rows = pairs[0][0].shape[0]
    step = rows // half
    in_specs, out_specs, out_shape = [], [], []
    for g, (one, _) in enumerate(pairs):
        cols = one.shape[1]
        in_specs += [
            pl.BlockSpec((step, cols), lambda r, orders: (jnp.minimum(r, half - 1), 0)),
            pl.BlockSpec((step, cols), lambda r, orders: (jnp.maximum(r - half, 0), 0)),
        ]
        for w in widths[g]:
            out_specs.append(pl.BlockSpec((step, w), lambda r, orders, g=g: (orders[g, r], 0)))
            out_shape.append(jax.ShapeDtypeStruct((2 * rows, w), F32))
    return pl.pallas_call(
        cast_columns,
        grid_spec=pltpu.PrefetchScalarGridSpec(
            num_scalar_prefetch=1, grid=(blocks,), in_specs=in_specs, out_specs=out_specs
        ),
        out_shape=out_shape,
    )(orders, *pairs[0], *pairs[1])


def gather_stage(halves, step, pin=()):
    chips = lax.axis_size("chip")
    bits = chips.bit_length() - 1
    out = []
    for g, half in enumerate(halves):
        bit = (g + step) % bits
        got = lax.ppermute(half, "chip", [(i, i ^ (1 << bit)) for i in range(chips)])
        out.append(jnp.concatenate([half, after(got, pin)], axis=0))
    return out


def gathered_order(g):
    chips = lax.axis_size("chip")
    bits = chips.bit_length() - 1
    chip, core = lax.axis_index("chip"), lax.axis_index("core")
    away = [0]
    for step in range(bits):
        away += [a ^ (1 << ((g + step) % bits)) for a in away]
    places = [(chip ^ a) * 2 + (core ^ k) for k in range(2) for a in away]
    return jnp.stack(places).astype(jnp.int32)


def cast_down(own, out):
    out[...] = own[0].astype(F32)


def place_down(own, chips, part, width):
    return pl.pallas_call(
        cast_down,
        grid=(2, chips),
        in_specs=[pl.BlockSpec((1, part, width), lambda k, c: (c * 2 + k, 0, 0))],
        out_specs=pl.BlockSpec((part, width), lambda k, c: (k * chips + c, 0)),
        out_shape=jax.ShapeDtypeStruct((2 * chips * part, width), F32),
    )(own)


def shards(
    inputs,
    doc_lengths,
    attn_gain,
    query_weight,
    key_projection,
    value_projection,
    query_gain,
    key_norm_gain,
    out_weight,
    ffn_gain,
    gate_weight,
    up_weight,
    down_weight,
    cotangent,
):
    tok, width = inputs.shape
    count = lax.axis_size("fsdp")
    chips = lax.axis_size("chip")
    rep = chips * 2
    mine = lax.axis_index("fsdp")
    chip = lax.axis_index("chip")
    core = lax.axis_index("core")
    seq = tok * count
    hd = HEAD_SIZE
    rows = query_weight.shape[0]
    q_cols = query_weight.shape[1] // count
    kv_cols = key_projection.shape[1] // count
    ff = gate_weight.shape[1]
    ff_own = ff // count // 2

    share = rows // rep
    at = (chip * 2 + core) * share

    def proj_piece(j):
        return jnp.concatenate(
            [
                lax.dynamic_slice(w, (at, j * wide), (share, wide))
                for w, wide in (
                    (query_weight, q_cols),
                    (key_projection, kv_cols),
                    (value_projection, kv_cols),
                )
            ],
            axis=1,
        )

    proj_ring = exchange_line(proj_piece)
    begun = line_step(inputs, inputs)
    proj_own = absolute(after(proj_ring, begun))
    x_steps = line_steps(inputs, {2: proj_own}, begun)
    x_all = line_pieces(inputs, x_steps)
    proj = lax.all_gather(proj_own, PLANE, axis=0)
    proj = proj.transpose(1, 0, 2, 3).reshape(width, q_cols + 2 * kv_cols)

    gains = jnp.concatenate([attn_gain, ffn_gain, query_gain, key_norm_gain])
    gains = gather_small(after(gains, x_steps[1]))
    gains = gains.astype(F32)
    gain_one = gains[:, :rows].reshape(-1)
    gain_two = gains[:, rows : 2 * rows].reshape(-1)
    small = hd // count
    gain_query = gains[:, 2 * rows : 2 * rows + small].reshape(-1)
    gain_key = gains[:, 2 * rows + small :].reshape(-1)

    part = rows // chips
    gate_up = after((gate_weight, up_weight), x_steps[-1])

    def pair_piece(j):
        return jnp.concatenate(
            [
                lax.dynamic_slice(w, (chip * part, (j * 2 + core) * ff_own), (part, ff_own))
                for w in gate_up
            ],
            axis=1,
        )

    pair_ring = exchange_line(pair_piece)

    order = (mine - jnp.arange(count, dtype=jnp.int32)) % count
    positions = (order[:, None] * tok + jnp.arange(tok, dtype=jnp.int32)[None, :]).reshape(-1)
    lengths = after(doc_lengths, x_steps[1])[0]
    docs = lengths.shape[0]
    upto = jnp.arange(docs)[None, :] <= jnp.arange(docs)[:, None]
    ends = jnp.sum(jnp.where(upto, lengths[None, :], 0), axis=1)
    segment = jnp.sum((positions[:, None] >= ends[None, :]).astype(jnp.int32), axis=1)
    allowed = (segment[:, None] == segment[None, :]) & (positions[None, :] <= positions[:, None])
    bias = jnp.where(allowed, 0.0, NEG_FILL).astype(F32)
    tables = pair_tables(positions)

    wide = x_all.astype(F32)
    normed_one = (wide * inverse_root(wide) * gain_one).astype(BF)
    kv_heads = kv_cols // hd
    core_args = (mm(normed_one, proj), bias, *tables, gain_query, gain_key, kv_heads)
    attended, inverse_sums = attention_call(*core_args)
    out_part = mm(attended, out_weight).reshape(count, tok, width)
    stage = {}

    def slices(t, sides):
        if t == 1:
            stage["slices"] = absolute(after(pair_ring, sides))
            return stage["slices"]
        return ()

    sides = line_scatter(out_part, slices)
    pair = lax.all_gather(stage["slices"], "chip", axis=0)
    pair = pair.reshape(width, 2 * ff_own)
    hidden_one, normed_own = forward_norm(inputs, out_part, *sides, gain_two, chips, count)

    cot_begun = line_step(*(after(cotangent, sides),) * 2)
    two_steps = line_steps(after(normed_own, cot_begun))
    normed_two = line_pieces(normed_own, two_steps)
    normed_two = jnp.concatenate([normed_two, swap_cores(normed_two)], axis=0)
    down_own = lax.dynamic_slice_in_dim(down_weight, core * ff_own, ff_own)
    both = mm(normed_two, pair)
    cot_steps = line_steps(cotangent, {1: two_steps[-1], count - 2: both}, cot_begun)
    cot_own = line_pieces(cotangent, cot_steps)
    cot_all = jnp.concatenate([cot_own, swap_cores(cot_own)], axis=0)
    grad_hidden = mm_last(cot_all, down_own)
    gate_pre, upward = both[:, :ff_own], both[:, ff_own:]
    sigmoid = jax.nn.sigmoid(gate_pre)
    silu = gate_pre * sigmoid
    hidden = (silu * upward).astype(BF)
    grad_gate = (grad_hidden * upward * sigmoid * (1.0 + gate_pre * (1.0 - sigmoid))).astype(BF)
    grad_up = (grad_hidden * silu).astype(BF)
    grad_both = jnp.concatenate([grad_gate, grad_up], axis=1)

    down_part = mm_first(hidden, cot_all).astype(BF)
    down_sum = lax.psum_scatter(down_part, "chip", scatter_dimension=0, tiled=True)
    out_other = mm(after(hidden[seq:], down_part), down_own).astype(BF)
    other = mm_last(after(grad_both[seq:], out_other), pair).astype(BF)
    out_terms = mm(after(hidden[:seq], other), down_own) + swap_cores(out_other).astype(F32)
    out_terms = out_terms.reshape(count, tok, width)
    pair_part = mm_first(normed_two, after(grad_both, out_terms)).astype(BF)
    pair_sum = lax.psum_scatter(pair_part, "chip", scatter_dimension=0, tiled=True)
    own = after(grad_both[:seq], pair_part)
    two_terms = mm_last(own, pair) + swap_cores(other).astype(F32)
    two_terms = two_terms.reshape(count, tok, width)
    sides = line_scatter(out_terms, lambda t, _: pair_part if t == 1 else two_terms)
    output = (
        hidden_one + out_terms[0] + sides[0].astype(F32) + sides[1].astype(F32)
    ).astype(BF)
    sides = line_scatter(two_terms)
    grad_hidden_one, grad_low, gain_two_sum = backward_norm(
        two_terms, *sides, hidden_one, cotangent, gain_two, chips, count
    )
    grad_attn = line_pieces(grad_low, line_steps(grad_low))

    grad_att = mm_last(grad_attn, out_weight).astype(BF)
    out_term = mm_first(attended, grad_attn).astype(BF)
    grad_att = after(grad_att, out_term)
    down_all = lax.all_gather(after(down_sum, grad_att), PLANE, axis=0)
    pair_sum = after(pair_sum, grad_att)
    rings = [
        exchange_line(
            lambda j, w=w: lax.dynamic_slice(pair_sum, (j * part, w * ff_own), (part, ff_own))
        )
        for w in range(2)
    ]
    grad_proj, query_sum, key_sum = attention_call(
        *core_args, more=(attended, inverse_sums, grad_att)
    )
    query_gain_sum = query_sum[0, :hd] + query_sum[0, hd:]
    key_gain_sum = key_sum[0, :hd] + (key_sum[0, hd:] if kv_heads == 2 else 0.0)
    proj_part = mm_first(normed_one, grad_proj).astype(BF)
    one_part = mm_last(after(grad_proj, proj_part), proj).reshape(count, tok, width)
    bits = chips.bit_length() - 1
    cols = q_cols + 2 * kv_cols
    att_terms = [proj_part.reshape(count, chips, 2, share, cols), out_term.reshape(chips, 2, share, -1)]

    def att_cores(pin):
        out = [halve(x, 2 - g, "core", 0, pin) for g, x in enumerate(att_terms)]
        return [
            out[0].reshape([count] + [2] * bits + [share, cols]),
            out[1].reshape([2] * bits + [share, width]),
        ]

    att_sum = att_cores(one_part)
    ffn_sum = jnp.concatenate([absolute(after(ring, att_sum)) for ring in rings], axis=2)
    ffn_all = lax.all_gather(ffn_sum.reshape(count * part, 2 * ff_own), PLANE, axis=0)

    def att_stages(t, sides):
        if t > 2:
            return ()
        stage["att"] = chip_stage(stage.get("att", att_sum), t - 1, sides, (1, 0))
        return (stage["att"], down_grad) if t == 2 else stage["att"]

    down_grad = place_down(down_all, chips, ff_own // chips, width)
    sides = line_scatter(after(one_part, ffn_sum), att_stages)
    _, input_grad, gain_one_sum = backward_norm(
        one_part, *sides, inputs, grad_hidden_one, gain_one, 0, count
    )

    sums = jnp.concatenate(
        [
            v.reshape(count, -1)
            for v in (gain_one_sum, gain_two_sum, query_gain_sum, key_gain_sum)
        ],
        axis=1,
    )

    att_sum = chip_rest(stage["att"], 2, sides, (1, 0))
    ring = exchange_line(lambda j: lax.dynamic_index_in_dim(att_sum[0], j, keepdims=False))
    cuts = ((0, q_cols), (q_cols, q_cols + kv_cols), (q_cols + kv_cols, cols))
    got = absolute(after(ring, input_grad))
    columns = [[got[j, :, a:b] for j in range(count)] for a, b in cuts]
    att_all = [
        jnp.concatenate(columns[0] + columns[1], axis=1),
        jnp.concatenate(columns[2] + [att_sum[1]], axis=1),
    ]
    sums = small_line(sums, att_all)
    gate_grad, up_grad = (place_pair(ffn_all, w, chips, count, part, ff_own) for w in range(2))
    for step in range(bits):
        last = step == bits - 1
        att_all = gather_stage(att_all, step, (gate_grad, up_grad) if last else sums)
        if step == 0:
            sums = sums + after(swap_cores(sums), att_all)
    sums = small_chips(sums, att_all)
    others = [swap_cores(a) for a in att_all]
    query_grad, key_grad, value_grad, out_grad = place_columns(
        jnp.stack([gathered_order(0), gathered_order(1)]),
        list(zip(att_all, others)),
        ((q_cols * count, kv_cols * count), (kv_cols * count, width)),
    )
    return (
        output,
        input_grad,
        sums[:rows],
        query_grad,
        key_grad,
        value_grad,
        sums[2 * rows : 2 * rows + small],
        sums[2 * rows + small :],
        out_grad,
        sums[rows : 2 * rows],
        gate_grad,
        up_grad,
        down_grad,
    )


def solution(mesh):
    chips, count = mesh.shape["rep"] // 2, mesh.shape["fsdp"]
    split = Mesh(mesh.devices.reshape(chips, 2, count), ("chip", "core", "fsdp"))
    tokens, reps, fsdp = (*PLANE, "fsdp"), PLANE, "fsdp"
    in_specs = (
        P(tokens, None),
        P(reps, None),
        P(fsdp),
        P(fsdp, None),
        P(fsdp, None),
        P(fsdp, None),
        P(fsdp),
        P(fsdp),
        P(fsdp, None),
        P(fsdp),
        P(fsdp, None),
        P(fsdp, None),
        P(fsdp, None),
        P(tokens, None),
    )
    out_specs = (
        P(tokens, None),
        P(tokens, None),
        P(fsdp),
        P(fsdp, None),
        P(fsdp, None),
        P(fsdp, None),
        P(fsdp),
        P(fsdp),
        P(fsdp, None),
        P(fsdp),
        P(fsdp, None),
        P(fsdp, None),
        P(fsdp, None),
    )
    return jax.shard_map(
        shards, mesh=split, in_specs=in_specs, out_specs=out_specs, check_vma=False
    )
```

```python
import functools

import jax
import jax.numpy as jnp
from jax import lax
from jax.experimental import pallas as pl
from jax.experimental.pallas import tpu as pltpu
from jax.sharding import Mesh, PartitionSpec as P

HEAD_SIZE = 64
EPSILON = 1e-05
THETA_BASE = 1000000.0
NEG_FILL = -1e30
LOG2E = 1.4426950408889634
BF = jnp.bfloat16
F32 = jnp.float32
PLANE = ("chip", "core")


def mm(a, b):
    return jnp.dot(a, b, preferred_element_type=F32)


def mm_last(a, b):
    return lax.dot_general(a, b, (((1,), (1,)), ((), ())), preferred_element_type=F32)


def mm_first(a, b):
    return lax.dot_general(a, b, (((0,), (0,)), ((), ())), preferred_element_type=F32)


def swap_cores(a):
    return lax.ppermute(a, "core", [(0, 1), (1, 0)])


def exchanges():
    count = lax.axis_size("fsdp")
    even = [(i, i ^ 1) for i in range(count)]
    odd = [(0, 0)] + [(i, ((i - 1) ^ 1) + 1) for i in range(1, count - 1)] + [(count - 1, count - 1)]
    return even, odd


def line_step(first, second):
    even, odd = exchanges()
    return lax.ppermute(first, "fsdp", even), lax.ppermute(second, "fsdp", odd)


def line_steps(own, ahead_of={}, begun=None, turn=None):
    steps = []
    first, second = own, own
    for t in range(lax.axis_size("fsdp") - 1):
        if t in ahead_of:
            first, second = after((first, second), ahead_of[t])
        if t and turn:
            first, second = after((first, second), turn((first, second)))
        if t == 0 and begun:
            by_even, by_odd = begun
        else:
            by_even, by_odd = line_step(first, second)
        steps.append((by_even, by_odd))
        first, second = by_odd, by_even
    return steps


def line_pieces(own, steps):
    count = lax.axis_size("fsdp")
    mine = lax.axis_index("fsdp")
    is_even = mine % 2 == 0
    pieces = [own]
    for d in range(1, count):
        below, above = steps[d - 1], steps[count - d - 1]
        from_below = jnp.where(is_even, below[1], below[0])
        from_above = jnp.where(is_even, above[0], above[1])
        pieces.append(jnp.where(mine >= d, from_below, from_above))
    return jnp.concatenate(pieces, axis=0)


def line_scatter(parts, ahead_of=None):
    count = lax.axis_size("fsdp")
    mine = lax.axis_index("fsdp")
    is_even = mine % 2 == 0
    is_end = (mine == 0) | (mine == count - 1)
    by_even = by_odd = None
    for t in range(count - 1):
        up = jnp.where(is_even, t + 1, count - 1 - t)
        first = lax.dynamic_index_in_dim(parts, up, keepdims=False)
        second = lax.dynamic_index_in_dim(parts, count - up, keepdims=False)
        if t:
            if ahead_of:
                by_even, by_odd = after((by_even, by_odd), ahead_of(t, (by_even, by_odd)))
            first, second = first + by_odd.astype(F32), second + by_even.astype(F32)
        second = jnp.where(is_end, 0.0, second)
        by_even, by_odd = line_step(first.astype(BF), second.astype(BF))
    return by_even, by_odd


def absolute(ring):
    count = len(ring)
    mine = lax.axis_index("fsdp")
    out = jnp.zeros((count, *ring[0].shape), ring[0].dtype)
    for e, piece in enumerate(ring):
        out = lax.dynamic_update_index_in_dim(out, piece, (mine + e) % count, 0)
    return out


def exchange_line(piece_for):
    count = lax.axis_size("fsdp")
    mine = lax.axis_index("fsdp")
    return [piece_for(mine)] + [
        lax.ppermute(
            piece_for((mine - e) % count),
            "fsdp",
            [(i, (i - e) % count) for i in range(count)],
        )
        for e in range(1, count)
    ]


def add_low(a, b):
    return (a.astype(F32) + b.astype(F32)).astype(BF)


def halve(blocks, axis, name, bit, pin=()):
    mybit = (lax.axis_index(name) >> bit) & 1
    pairs = [(i, i ^ (1 << bit)) for i in range(lax.axis_size(name))]
    got = lax.ppermute(
        lax.dynamic_index_in_dim(blocks, 1 - mybit, axis, keepdims=False), name, pairs
    )
    got = after(got, pin)
    return add_low(lax.dynamic_index_in_dim(blocks, mybit, axis, keepdims=False), got)


def chip_halves(terms):
    chips, rows, cols = terms.shape
    bits = chips.bit_length() - 1
    return [
        terms[:, g * rows // 2 : (g + 1) * rows // 2].reshape([2] * bits + [rows // 2, cols])
        for g in range(2)
    ]


def chip_stage(halves, step, pin=(), lead=(0, 0)):
    bits = lax.axis_size("chip").bit_length() - 1
    out = []
    for g in range(2):
        done = [(g + k) % bits for k in range(step)]
        left = [b for b in range(bits - 1, -1, -1) if b not in done]
        bit = (g + step) % bits
        out.append(halve(halves[g], lead[g] + left.index(bit), "chip", bit, pin))
    return out


def chip_rest(halves, step, pin=(), lead=(0, 0)):
    for k in range(step, lax.axis_size("chip").bit_length() - 1):
        halves = chip_stage(halves, k, pin, lead)
    return halves


def after(value, *others):
    return lax.optimization_barrier((value, *others))[0]


def gather_small(own):
    return absolute(exchange_line(lambda j: own))


def small_line(rows, pin):
    count = lax.axis_size("fsdp")
    mine = lax.axis_index("fsdp")
    got = [
        lax.ppermute(
            lax.dynamic_index_in_dim(rows, (mine + d) % count, keepdims=False),
            "fsdp",
            [(i, (i + d) % count) for i in range(count)],
        )
        for d in range(1, count)
    ]
    return sum(after(got, pin), lax.dynamic_index_in_dim(rows, mine, keepdims=False))


def small_chips(total, pin):
    chips = lax.axis_size("chip")
    got = [
        lax.ppermute(total, "chip", [(i, i ^ d) for i in range(chips)]) for d in range(1, chips)
    ]
    return sum(after(got, pin), total)


def split_mean(values, block):
    high = values.astype(BF)
    low = (values - high.astype(F32)).astype(BF)
    return mm(high, block) + mm(low, block)


def swap_pairs(values):
    lane = lax.broadcasted_iota(jnp.int32, values.shape, 1)
    half = HEAD_SIZE // 2
    lanes = values.shape[1]
    return jnp.where(
        lane % HEAD_SIZE < half,
        pltpu.roll(values, lanes - half, 1),
        pltpu.roll(values, half, 1),
    )


def head_unit(pre, block):
    inverse = lax.rsqrt(split_mean(pre * pre, block) + EPSILON)
    return pre * inverse, inverse


def turn_heads(values, cosine, sine):
    return values * cosine + swap_pairs(values) * sine


def turn_back(values, cosine, sine):
    return values * cosine - swap_pairs(values) * sine


def head_grad(grad, unit, inverse, gain, block):
    scaled = grad * gain
    return inverse * (scaled - unit * split_mean(scaled * unit, block))


def spread(values, source, seq, rows):
    lanes = values.shape[1]
    a = lax.broadcasted_iota(jnp.int32, (lanes, 2 * HEAD_SIZE), 0)
    b = lax.broadcasted_iota(jnp.int32, (lanes, 2 * HEAD_SIZE), 1)
    for side in range(2):
        move = (a - source * HEAD_SIZE == b - side * HEAD_SIZE) & (b // HEAD_SIZE == side)
        rows[side * seq : (side + 1) * seq, :] = mm(values, move.astype(BF)).astype(BF)


def load_heads(keys, vals, cosine, sine, key_gain, block, kv, keys_at, vals_at):
    seq = keys.shape[0]
    unit, _ = head_unit(keys[...], block[...])
    turned = turn_heads(unit * key_gain[...], cosine[...], sine[...]).astype(BF)
    low = vals[...].astype(BF)
    for n in range(kv):
        spread(turned, n, seq, keys_at.at[n])
        spread(low, n if kv == 2 else 1, seq, vals_at.at[n])


def attend_kernel(
    kv, each, scale, pre, keys, vals, bias, cosine, sine, cos_own, sin_own, query_gain, key_gain,
    block, out, inverse, keys_at, vals_at,
):
    j, i = pl.program_id(0), pl.program_id(1)
    seq = keys.shape[0]

    @pl.when((j == 0) & (i == 0))
    def _():
        load_heads(keys, vals, cosine, sine, key_gain, block, kv, keys_at, vals_at)

    unit, _ = head_unit(pre[...], block[...])
    query = turn_heads(unit * query_gain[...], cos_own[...], sin_own[...]).astype(BF)
    head = j // each
    scores = mm_last(query, keys_at[head]) * (scale * LOG2E)
    side = lax.broadcasted_iota(jnp.int32, (2 * seq, 2 * HEAD_SIZE), 0) // seq
    lane = lax.broadcasted_iota(jnp.int32, (2 * seq, 2 * HEAD_SIZE), 1) // HEAD_SIZE
    ones = (side == lane).astype(BF)
    allowed = bias[...]
    expo = jnp.exp2(
        jnp.concatenate([scores[:, :seq] + allowed, scores[:, seq:] + allowed], axis=1)
    ).astype(BF)
    inv = 1.0 / mm(expo, ones)
    out[...] = (mm(expo, vals_at[head]) * inv).astype(BF)
    inverse[...] = inv


def attend_back_kernel(
    kv, each, scale, pre, keys, vals, bias, cosine, sine, cos_own, sin_own, query_gain, key_gain,
    block, out, inverse, grad, grad_proj, query_sum, key_sum, keys_at, vals_at, key_acc, val_acc,
):
    j, i = pl.program_id(0), pl.program_id(1)
    seq = keys.shape[0]
    rows = pre.shape[0]
    two = 2 * HEAD_SIZE

    @pl.when((j == 0) & (i == 0))
    def _():
        load_heads(keys, vals, cosine, sine, key_gain, block, kv, keys_at, vals_at)
        key_acc[...] = jnp.zeros_like(key_acc)
        val_acc[...] = jnp.zeros_like(val_acc)
        query_sum[...] = jnp.zeros_like(query_sum)

    unit, inv_unit = head_unit(pre[...], block[...])
    query = turn_heads(unit * query_gain[...], cos_own[...], sin_own[...]).astype(BF)
    head = j // each
    keys_of, vals_of = keys_at[head], vals_at[head]
    scores = mm_last(query, keys_of) * (scale * LOG2E)
    low = grad[...]
    gprobs = mm_last(low, vals_of)
    product = low.astype(F32) * out[...].astype(F32)
    delta = split_mean(product, block[...]) * HEAD_SIZE
    inv = inverse[...]
    allowed = bias[...]
    probs, gscores = [], []
    for side in range(2):
        part = slice(side * seq, (side + 1) * seq)
        at = side * HEAD_SIZE
        p = jnp.exp2(scores[:, part] + allowed) * inv[:, at : at + 1]
        probs.append(p.astype(BF))
        gscores.append((p * (gprobs[:, part] - delta[:, at : at + 1])).astype(BF))
    probs = jnp.concatenate(probs, axis=1)
    gscores = jnp.concatenate(gscores, axis=1)
    key_acc[head] += mm_first(gscores, query)
    val_acc[head] += mm_first(probs, low)
    back = turn_back(mm(gscores, keys_of) * scale, cos_own[...], sin_own[...])
    query_sum[...] += jnp.sum(back * unit, axis=0, keepdims=True)
    grad_proj[pl.ds(pl.multiple_of(i * rows, rows), rows), pl.ds(pl.multiple_of(j * two, two), two)] = (
        head_grad(back, unit, inv_unit, query_gain[...], block[...]).astype(BF)
    )

    @pl.when((j == pl.num_programs(0) - 1) & (i == pl.num_programs(1) - 1))
    def _():
        lane = lax.broadcasted_iota(jnp.int32, (seq, two), 1)

        def fold(acc, n):
            both = jnp.where(lane < HEAD_SIZE, acc[n, :seq, :], acc[n, seq:, :])
            return both + pltpu.roll(both, HEAD_SIZE, 1)

        key_tile = fold(key_acc, 0) * scale
        val_tile = fold(val_acc, 0)
        if kv == 2:
            key_tile = jnp.where(lane < HEAD_SIZE, key_tile, fold(key_acc, 1) * scale)
            val_tile = jnp.where(lane < HEAD_SIZE, val_tile, fold(val_acc, 1))
        unit_k, inv_k = head_unit(keys[...], block[...])
        back_k = turn_back(key_tile, cosine[...], sine[...])
        key_sum[...] = jnp.sum(back_k * unit_k, axis=0, keepdims=True)
        key_low = head_grad(back_k, unit_k, inv_k, key_gain[...], block[...])
        start = grad_proj.shape[1] - kv * two
        if kv == 2:
            grad_proj[:, start : start + two] = key_low.astype(BF)
            grad_proj[:, start + two :] = val_tile.astype(BF)
        else:
            grad_proj[:, start:] = jnp.where(lane < HEAD_SIZE, key_low, val_tile).astype(BF)


def attention_call(pre, bias, cosine, sine, query_gain, key_gain, kv, more=None):
    seq, cols = pre.shape
    two = 2 * HEAD_SIZE
    q_cols = cols - kv * two
    tiles = q_cols // two
    each = tiles // kv
    rows = min(512, seq)
    lane = jnp.arange(two) // HEAD_SIZE
    block = jnp.where(lane[:, None] == lane[None, :], 1.0 / HEAD_SIZE, 0.0).astype(BF)
    own = pl.BlockSpec((rows, two), lambda j, i: (i, j))
    here = pl.BlockSpec((rows, two), lambda j, i: (i, 0))
    whole = pl.BlockSpec((seq, two), lambda j, i: (0, 0))
    row = pl.BlockSpec((1, two), lambda j, i: (0, 0))
    key_tile = pl.BlockSpec((seq, two), lambda j, i: (0, tiles))
    val_tile = pl.BlockSpec((seq, two), lambda j, i: (0, tiles + kv - 1))
    in_specs = [
        own, key_tile, val_tile, pl.BlockSpec((rows, seq), lambda j, i: (i, 0)), whole, whole,
        here, here, row, row, pl.BlockSpec((two, two), lambda j, i: (0, 0)),
    ]
    twice = [jnp.concatenate([g, g]).reshape(1, two) for g in (query_gain, key_gain)]
    args = [pre, pre, pre, bias, cosine, sine, cosine, sine, *twice, block]
    heads = pltpu.VMEM((kv, 2 * seq, two), BF)
    params = pltpu.CompilerParams(vmem_limit_bytes=48 * 2**20)
    grid = (tiles, seq // rows)
    scale = HEAD_SIZE ** (-0.5)
    if more is None:
        return pl.pallas_call(
            functools.partial(attend_kernel, kv, each, scale),
            grid=grid,
            in_specs=in_specs,
            out_specs=[own, own],
            out_shape=[
                jax.ShapeDtypeStruct((seq, q_cols), BF),
                jax.ShapeDtypeStruct((seq, q_cols), F32),
            ],
            scratch_shapes=[heads, heads],
            compiler_params=params,
        )(*args)
    sums = pltpu.VMEM((kv, 2 * seq, two), F32)
    return pl.pallas_call(
        functools.partial(attend_back_kernel, kv, each, scale),
        grid=grid,
        in_specs=in_specs + [own, own, own],
        out_specs=[pl.BlockSpec((seq, cols), lambda j, i: (0, 0)), row, row],
        out_shape=[
            jax.ShapeDtypeStruct((seq, cols), BF),
            jax.ShapeDtypeStruct((1, two), F32),
            jax.ShapeDtypeStruct((1, two), F32),
        ],
        scratch_shapes=[heads, heads, sums, sums],
        compiler_params=params,
    )(*args, *more)


def pair_tables(positions):
    half = HEAD_SIZE // 2
    inverse = THETA_BASE ** (-(jnp.arange(half, dtype=F32) * 2.0) / HEAD_SIZE)
    angles = positions.astype(F32)[:, None] * inverse[None, :]
    cosine, sine = jnp.cos(angles), jnp.sin(angles)
    return jnp.tile(cosine, (1, 4)), jnp.concatenate([-sine, sine, -sine, sine], axis=1)


def lanes(width, chips, count):
    part = width // chips // count
    return [
        (slice((z * chips + c) * part, (z * chips + c + 1) * part),
         slice((c * count + z) * part, (c * count + z + 1) * part))
        for z in range(count)
        for c in range(chips)
    ]


def inverse_root(wide):
    return lax.rsqrt(jnp.mean(wide * wide, axis=-1, keepdims=True) + EPSILON)


def norm_forward(chips, count, own, part, right, left, gain, hidden, normed):
    wide = own[...].astype(F32) + part[0] + right[...].astype(F32) + left[...].astype(F32)
    hidden[...] = wide
    low = (wide * inverse_root(wide) * gain[...]).astype(BF)
    for here, there in lanes(wide.shape[1], chips, count):
        normed[:, there] = low[:, here]


def norm_backward(chips, count, part, right, left, wide, base, gain, grad, low, total, scratch):
    summed = part[0] + right[...].astype(F32) + left[...].astype(F32)
    if chips:
        for here, there in lanes(summed.shape[1], chips, count):
            scratch[:, here] = summed[:, there]
        summed = scratch[...]
    values = wide[...].astype(F32)
    inverse = inverse_root(values)
    unit = values * inverse
    sums = jnp.sum(summed * unit, axis=0, keepdims=True)

    @pl.when(pl.program_id(0) == 0)
    def _():
        total[...] = sums

    @pl.when(pl.program_id(0) > 0)
    def _():
        total[...] += sums

    scaled = summed * gain[...]
    out = base[...].astype(F32) + inverse * (
        scaled - unit * jnp.mean(scaled * unit, axis=-1, keepdims=True)
    )
    grad[...] = out
    low[...] = out.astype(BF)


def row_specs(tok, width):
    step = min(32, tok)
    block = pl.BlockSpec((step, width), lambda i: (i, 0))
    first = pl.BlockSpec((1, step, width), lambda i: (0, i, 0))
    row = pl.BlockSpec((1, width), lambda i: (0, 0))
    return tok // step, step, block, first, row


def forward_norm(own, parts, right, left, gain, chips, count):
    tok, width = own.shape
    grid, _, block, first, row = row_specs(tok, width)
    return pl.pallas_call(
        functools.partial(norm_forward, chips, count),
        grid=(grid,),
        in_specs=[block, first, block, block, row],
        out_specs=[block, block],
        out_shape=[
            jax.ShapeDtypeStruct((tok, width), F32),
            jax.ShapeDtypeStruct((tok, width), BF),
        ],
    )(own, parts, right, left, gain.reshape(1, width))


def backward_norm(parts, right, left, wide, base, gain, chips, count):
    tok, width = wide.shape
    grid, step, block, first, row = row_specs(tok, width)
    return pl.pallas_call(
        functools.partial(norm_backward, chips, count),
        grid=(grid,),
        in_specs=[first, block, block, block, block, row],
        out_specs=[block, block, row],
        out_shape=[
            jax.ShapeDtypeStruct((tok, width), F32),
            jax.ShapeDtypeStruct((tok, width), BF),
            jax.ShapeDtypeStruct((1, width), F32),
        ],
        scratch_shapes=[pltpu.VMEM((step, width), F32)],
    )(parts, right, left, wide, base, gain.reshape(1, width))


def cast_pair(own, out):
    _, cores, count, _, _ = own.shape
    half = out.shape[1] // cores // count
    for j in range(count):
        for k in range(cores):
            at = (j * cores + k) * half
            out[:, at : at + half] = own[0, k, j].astype(F32)


def place_pair(own, which, chips, count, part, half):
    step = min(128, part)
    own = own.reshape(chips, 2, count, part, 2 * half)
    cols = count * 2 * half
    return pl.pallas_call(
        cast_pair,
        grid=(chips, part // step),
        in_specs=[pl.BlockSpec((1, 2, count, step, half), lambda c, r: (c, 0, 0, r, which))],
        out_specs=pl.BlockSpec((step, cols), lambda c, r: (c * (part // step) + r, 0)),
        out_shape=jax.ShapeDtypeStruct((chips * part, cols), F32),
        compiler_params=pltpu.CompilerParams(vmem_limit_bytes=32 * 2**20),
    )(own)


def cast_columns(_, *refs):
    half = pl.num_programs(0) // 2
    for g in range(2):
        outs = refs[4 + 2 * g : 6 + 2 * g]
        for own, mine in (
            (refs[2 * g], pl.program_id(0) < half),
            (refs[2 * g + 1], pl.program_id(0) >= half),
        ):

            @pl.when(mine)
            def _(own=own, outs=outs):
                at = 0
                for out in outs:
                    out[...] = own[:, at : at + out.shape[1]].astype(F32)
                    at += out.shape[1]


def place_columns(orders, pairs, widths):
    blocks = orders.shape[1]
    half = blocks // 2
    rows = pairs[0][0].shape[0]
    step = rows // half
    in_specs, out_specs, out_shape = [], [], []
    for g, (one, _) in enumerate(pairs):
        cols = one.shape[1]
        in_specs += [
            pl.BlockSpec((step, cols), lambda r, orders: (jnp.minimum(r, half - 1), 0)),
            pl.BlockSpec((step, cols), lambda r, orders: (jnp.maximum(r - half, 0), 0)),
        ]
        for w in widths[g]:
            out_specs.append(pl.BlockSpec((step, w), lambda r, orders, g=g: (orders[g, r], 0)))
            out_shape.append(jax.ShapeDtypeStruct((2 * rows, w), F32))
    return pl.pallas_call(
        cast_columns,
        grid_spec=pltpu.PrefetchScalarGridSpec(
            num_scalar_prefetch=1, grid=(blocks,), in_specs=in_specs, out_specs=out_specs
        ),
        out_shape=out_shape,
    )(orders, *pairs[0], *pairs[1])


def gather_stage(halves, step, pin=()):
    chips = lax.axis_size("chip")
    bits = chips.bit_length() - 1
    out = []
    for g, half in enumerate(halves):
        bit = (g + step) % bits
        got = lax.ppermute(half, "chip", [(i, i ^ (1 << bit)) for i in range(chips)])
        out.append(jnp.concatenate([half, after(got, pin)], axis=0))
    return out


def gathered_order(g):
    chips = lax.axis_size("chip")
    bits = chips.bit_length() - 1
    chip, core = lax.axis_index("chip"), lax.axis_index("core")
    away = [0]
    for step in range(bits):
        away += [a ^ (1 << ((g + step) % bits)) for a in away]
    places = [(chip ^ a) * 2 + (core ^ k) for k in range(2) for a in away]
    return jnp.stack(places).astype(jnp.int32)


def cast_down(own, out):
    out[...] = own[0].astype(F32)


def place_down(own, chips, part, width):
    return pl.pallas_call(
        cast_down,
        grid=(2, chips),
        in_specs=[pl.BlockSpec((1, part, width), lambda k, c: (c * 2 + k, 0, 0))],
        out_specs=pl.BlockSpec((part, width), lambda k, c: (k * chips + c, 0)),
        out_shape=jax.ShapeDtypeStruct((2 * chips * part, width), F32),
    )(own)


def shards(
    inputs,
    doc_lengths,
    attn_gain,
    query_weight,
    key_projection,
    value_projection,
    query_gain,
    key_norm_gain,
    out_weight,
    ffn_gain,
    gate_weight,
    up_weight,
    down_weight,
    cotangent,
):
    tok, width = inputs.shape
    count = lax.axis_size("fsdp")
    chips = lax.axis_size("chip")
    rep = chips * 2
    mine = lax.axis_index("fsdp")
    chip = lax.axis_index("chip")
    core = lax.axis_index("core")
    seq = tok * count
    hd = HEAD_SIZE
    rows = query_weight.shape[0]
    q_cols = query_weight.shape[1] // count
    kv_cols = key_projection.shape[1] // count
    ff = gate_weight.shape[1]
    ff_own = ff // count // 2

    share = rows // rep
    at = (chip * 2 + core) * share

    def proj_piece(j):
        return jnp.concatenate(
            [
                lax.dynamic_slice(w, (at, j * wide), (share, wide))
                for w, wide in (
                    (query_weight, q_cols),
                    (key_projection, kv_cols),
                    (value_projection, kv_cols),
                )
            ],
            axis=1,
        )

    proj_ring = exchange_line(proj_piece)
    begun = line_step(inputs, inputs)
    proj_own = absolute(after(proj_ring, begun))
    x_steps = line_steps(inputs, {2: proj_own}, begun)
    x_all = line_pieces(inputs, x_steps)
    proj = lax.all_gather(proj_own, PLANE, axis=0)
    proj = proj.transpose(1, 0, 2, 3).reshape(width, q_cols + 2 * kv_cols)

    gains = jnp.concatenate([attn_gain, ffn_gain, query_gain, key_norm_gain])
    gains = gather_small(after(gains, x_steps[1]))
    gains = gains.astype(F32)
    gain_one = gains[:, :rows].reshape(-1)
    gain_two = gains[:, rows : 2 * rows].reshape(-1)
    small = hd // count
    gain_query = gains[:, 2 * rows : 2 * rows + small].reshape(-1)
    gain_key = gains[:, 2 * rows + small :].reshape(-1)

    part = rows // chips
    gate_up = after((gate_weight, up_weight), x_steps[-1])

    def pair_piece(j):
        return jnp.concatenate(
            [
                lax.dynamic_slice(w, (chip * part, (j * 2 + core) * ff_own), (part, ff_own))
                for w in gate_up
            ],
            axis=1,
        )

    pair_ring = exchange_line(pair_piece)

    order = (mine - jnp.arange(count, dtype=jnp.int32)) % count
    positions = (order[:, None] * tok + jnp.arange(tok, dtype=jnp.int32)[None, :]).reshape(-1)
    lengths = after(doc_lengths, x_steps[1])[0]
    docs = lengths.shape[0]
    upto = jnp.arange(docs)[None, :] <= jnp.arange(docs)[:, None]
    ends = jnp.sum(jnp.where(upto, lengths[None, :], 0), axis=1)
    segment = jnp.sum((positions[:, None] >= ends[None, :]).astype(jnp.int32), axis=1)
    allowed = (segment[:, None] == segment[None, :]) & (positions[None, :] <= positions[:, None])
    bias = jnp.where(allowed, 0.0, NEG_FILL).astype(F32)
    tables = pair_tables(positions)

    wide = x_all.astype(F32)
    normed_one = (wide * inverse_root(wide) * gain_one).astype(BF)
    kv_heads = kv_cols // hd
    core_args = (mm(normed_one, proj), bias, *tables, gain_query, gain_key, kv_heads)
    attended, inverse_sums = attention_call(*core_args)
    out_part = mm(attended, out_weight).reshape(count, tok, width)
    stage = {}

    def slices(t, sides):
        if t == 1:
            stage["slices"] = absolute(after(pair_ring, sides))
            return stage["slices"]
        return ()

    sides = line_scatter(out_part, slices)
    pair = lax.all_gather(stage["slices"], "chip", axis=0)
    pair = pair.reshape(width, 2 * ff_own)
    hidden_one, normed_own = forward_norm(inputs, out_part, *sides, gain_two, chips, count)

    cot_begun = line_step(*(after(cotangent, sides),) * 2)
    two_steps = line_steps(after(normed_own, cot_begun))
    normed_two = line_pieces(normed_own, two_steps)
    normed_two = jnp.concatenate([normed_two, swap_cores(normed_two)], axis=0)
    down_own = lax.dynamic_slice_in_dim(down_weight, core * ff_own, ff_own)
    both = mm(normed_two, pair)
    cot_steps = line_steps(cotangent, {1: two_steps[-1], count - 2: both}, cot_begun)
    cot_own = line_pieces(cotangent, cot_steps)
    cot_all = jnp.concatenate([cot_own, swap_cores(cot_own)], axis=0)
    grad_hidden = mm_last(cot_all, down_own)
    gate_pre, upward = both[:, :ff_own], both[:, ff_own:]
    sigmoid = jax.nn.sigmoid(gate_pre)
    silu = gate_pre * sigmoid
    hidden = (silu * upward).astype(BF)
    grad_gate = (grad_hidden * upward * sigmoid * (1.0 + gate_pre * (1.0 - sigmoid))).astype(BF)
    grad_up = (grad_hidden * silu).astype(BF)
    grad_both = jnp.concatenate([grad_gate, grad_up], axis=1)

    down_part = mm_first(hidden, cot_all).astype(BF)
    down_sum = lax.psum_scatter(down_part, "chip", scatter_dimension=0, tiled=True)
    out_other = mm(after(hidden[seq:], down_part), down_own).astype(BF)
    other = mm_last(after(grad_both[seq:], out_other), pair).astype(BF)
    out_terms = mm(after(hidden[:seq], other), down_own) + swap_cores(out_other).astype(F32)
    out_terms = out_terms.reshape(count, tok, width)
    pair_part = mm_first(normed_two, after(grad_both, out_terms)).astype(BF)
    pair_sum = lax.psum_scatter(pair_part, "chip", scatter_dimension=0, tiled=True)
    own = after(grad_both[:seq], pair_part)
    two_terms = mm_last(own, pair) + swap_cores(other).astype(F32)
    two_terms = two_terms.reshape(count, tok, width)
    sides = line_scatter(out_terms, lambda t, _: pair_part if t == 1 else two_terms)
    output = (
        hidden_one + out_terms[0] + sides[0].astype(F32) + sides[1].astype(F32)
    ).astype(BF)
    sides = line_scatter(two_terms)
    grad_hidden_one, grad_low, gain_two_sum = backward_norm(
        two_terms, *sides, hidden_one, cotangent, gain_two, chips, count
    )
    grad_attn = line_pieces(grad_low, line_steps(grad_low))

    grad_att = mm_last(grad_attn, out_weight).astype(BF)
    out_term = mm_first(attended, grad_attn).astype(BF)
    grad_att = after(grad_att, out_term)
    down_all = lax.all_gather(after(down_sum, grad_att), PLANE, axis=0)
    pair_sum = after(pair_sum, grad_att)
    rings = [
        exchange_line(
            lambda j, w=w: lax.dynamic_slice(pair_sum, (j * part, w * ff_own), (part, ff_own))
        )
        for w in range(2)
    ]
    grad_proj, query_sum, key_sum = attention_call(
        *core_args, more=(attended, inverse_sums, grad_att)
    )
    query_gain_sum = query_sum[0, :hd] + query_sum[0, hd:]
    key_gain_sum = key_sum[0, :hd] + (key_sum[0, hd:] if kv_heads == 2 else 0.0)
    proj_part = mm_first(normed_one, grad_proj).astype(BF)
    one_part = mm_last(after(grad_proj, proj_part), proj).reshape(count, tok, width)
    bits = chips.bit_length() - 1
    cols = q_cols + 2 * kv_cols
    att_terms = [proj_part.reshape(count, chips, 2, share, cols), out_term.reshape(chips, 2, share, -1)]

    def att_cores(pin):
        out = [halve(x, 2 - g, "core", 0, pin) for g, x in enumerate(att_terms)]
        return [
            out[0].reshape([count] + [2] * bits + [share, cols]),
            out[1].reshape([2] * bits + [share, width]),
        ]

    att_sum = att_cores(one_part)
    ffn_sum = jnp.concatenate([absolute(after(ring, att_sum)) for ring in rings], axis=2)
    ffn_all = lax.all_gather(ffn_sum.reshape(count * part, 2 * ff_own), PLANE, axis=0)

    def att_stages(t, sides):
        if t > 2:
            return ()
        stage["att"] = chip_stage(stage.get("att", att_sum), t - 1, sides, (1, 0))
        return (stage["att"], down_grad) if t == 2 else stage["att"]

    down_grad = place_down(down_all, chips, ff_own // chips, width)
    sides = line_scatter(after(one_part, ffn_sum), att_stages)
    _, input_grad, gain_one_sum = backward_norm(
        one_part, *sides, inputs, grad_hidden_one, gain_one, 0, count
    )

    sums = jnp.concatenate(
        [
            v.reshape(count, -1)
            for v in (gain_one_sum, gain_two_sum, query_gain_sum, key_gain_sum)
        ],
        axis=1,
    )

    att_sum = chip_rest(stage["att"], 2, sides, (1, 0))
    ring = exchange_line(lambda j: lax.dynamic_index_in_dim(att_sum[0], j, keepdims=False))
    cuts = ((0, q_cols), (q_cols, q_cols + kv_cols), (q_cols + kv_cols, cols))
    got = absolute(after(ring, input_grad))
    columns = [[got[j, :, a:b] for j in range(count)] for a, b in cuts]
    att_all = [
        jnp.concatenate(columns[0] + columns[1], axis=1),
        jnp.concatenate(columns[2] + [att_sum[1]], axis=1),
    ]
    sums = small_line(sums, att_all)
    gate_grad, up_grad = (place_pair(ffn_all, w, chips, count, part, ff_own) for w in range(2))
    for step in range(bits):
        last = step == bits - 1
        att_all = gather_stage(att_all, step, (gate_grad, up_grad) if last else sums)
        if step == 0:
            sums = sums + after(swap_cores(sums), att_all)
    sums = small_chips(sums, att_all)
    others = [swap_cores(a) for a in att_all]
    query_grad, key_grad, value_grad, out_grad = place_columns(
        jnp.stack([gathered_order(0), gathered_order(1)]),
        list(zip(att_all, others)),
        ((q_cols * count, kv_cols * count), (kv_cols * count, width)),
    )
    return (
        output,
        input_grad,
        sums[:rows],
        query_grad,
        key_grad,
        value_grad,
        sums[2 * rows : 2 * rows + small],
        sums[2 * rows + small :],
        out_grad,
        sums[rows : 2 * rows],
        gate_grad,
        up_grad,
        down_grad,
    )


def solution(mesh):
    chips, count = mesh.shape["rep"] // 2, mesh.shape["fsdp"]
    split = Mesh(mesh.devices.reshape(chips, 2, count), ("chip", "core", "fsdp"))
    tokens, reps, fsdp = (*PLANE, "fsdp"), PLANE, "fsdp"
    in_specs = (
        P(tokens, None),
        P(reps, None),
        P(fsdp),
        P(fsdp, None),
        P(fsdp, None),
        P(fsdp, None),
        P(fsdp),
        P(fsdp),
        P(fsdp, None),
        P(fsdp),
        P(fsdp, None),
        P(fsdp, None),
        P(fsdp, None),
        P(tokens, None),
    )
    out_specs = (
        P(tokens, None),
        P(tokens, None),
        P(fsdp),
        P(fsdp, None),
        P(fsdp, None),
        P(fsdp, None),
        P(fsdp),
        P(fsdp),
        P(fsdp, None),
        P(fsdp),
        P(fsdp, None),
        P(fsdp, None),
        P(fsdp, None),
    )
    return jax.shard_map(
        shards, mesh=split, in_specs=in_specs, out_specs=out_specs, check_vma=False
    )
```
